32 devices in a mesh: region: 2 (over x), var: 8 (over z, y), samp: 2 (over core).
Axes of the slice: x: 2, y: 2, z: 4, core: 2. Of those that a mesh axis runs over, the one named last changes fastest.
Arguments:
- dosage: bfloat16 [2048, 16384], P('samp', ('region', 'var')), parts along dimension 1, may hold values from 0 to 2
- observed: int32 [2048, 16384], P('samp', ('region', 'var')), parts along dimension 1, may hold values from 0 to 1, as said below
- counts: int32 [16], P(('region', 'var')), parts along dimension 0, may hold values from 1 to 4, as said below
Outputs:
- correlations: bfloat16 [16, 4, 1024, 1024], P(('region', 'var'), None, 'samp'), parts along dimension 0
The draws below stay inside these ranges and needn't reach their ends.
There are 2 independent parts, one for each index of `region`. The reference program is written for one: setup_inputs(seed, part) draws one part's arguments, and reference() takes and returns one part's arrays. A program takes and returns all parts, laid end to end along the dimension named above; each array names one. Nothing has to cross between parts.
Inputs may be any that keep to these rules, and one draw needn't show every extreme that they name: Block b's partners are blocks b to b + counts[b] - 1; counts[b] is at most 8 - b, and counts[0] = 4. `observed`: some variants are missing in every sample.
All inputs are finite; a program needn't handle non-finite values.
Results may differ from the reference program's by a relative error of at most 0.001.
The reference program's roundings to bfloat16 on the way (of `scored`) count: a program that leaves them out, or rounds other values in their place, can miss the bound.
Values may be sent and summed in bfloat16 or wider, within the bound.
No kernel may reach another device: no remote copies, remote signals or barrier semaphores. Data moves between devices by JAX's collectives and lax.ppermute only.
A program may use at most 128 MiB of HBM per device.

```python
import jax
import jax.numpy as jnp
from jax import lax

BLK = 1024
WIN = 4
NBLK = 8
V = 8192
S = 2048


def draw_dosage(key, part):
    spacings = [16, 128, 1024, 4096]
    strengths = [0.25, 0.25, 0.35, 0.45]
    column = jnp.arange(V, dtype=jnp.int32)
    smooth = jnp.zeros((S, V), jnp.float32)
    for number in range(4):
        spacing = spacings[number]
        anchors = jax.random.normal(jax.random.fold_in(key, 11 + number), (S, V // spacing + 2), jnp.float32)
        index = column // spacing
        weight = (column % spacing).astype(jnp.float32) / spacing
        smooth = smooth + strengths[number] * (anchors[:, index] * (1.0 - weight) + anchors[:, index + 1] * weight)
    base = jax.random.uniform(jax.random.fold_in(key, 21), (1, V), jnp.float32, 0.3, 1.7)
    noise = 0.25 * jax.random.normal(jax.random.fold_in(key, 22), (S, V), jnp.float32)
    return jnp.clip(base + smooth + noise, 0.0, 2.0).astype(jnp.bfloat16)


def draw_observed(key, part):
    entries = jax.random.randint(jax.random.fold_in(key, 41), (S, V), 0, 10, dtype=jnp.int32)
    present = (entries < 9).astype(jnp.int32)
    lottery = jax.random.randint(jax.random.fold_in(key, 42), (V,), 0, 64, dtype=jnp.int32)
    forced = jax.random.randint(jax.random.fold_in(key, 43), (), 0, V, dtype=jnp.int32)
    column = jnp.arange(V, dtype=jnp.int32)
    missing = jnp.logical_or(lottery == 0, column == forced)
    return jnp.where(missing[None, :], jnp.zeros_like(present), present)


def draw_counts(key, part):
    drawn = jax.random.randint(jax.random.fold_in(key, 31), (NBLK,), 1, WIN + 1, dtype=jnp.int32)
    limit = NBLK - jnp.arange(NBLK, dtype=jnp.int32)
    capped = jnp.minimum(drawn, limit)
    return capped.at[0].set(WIN)


def setup_inputs(seed: int = 0, part: int = 0) -> dict:
    key_list = jax.random.split(jax.random.key(seed), 4)
    own_keys = jax.random.split(jax.random.fold_in(key_list[3], part), 4)
    return {
        "dosage": draw_dosage(jax.random.fold_in(jax.random.fold_in(key_list[3], part), 71), part),
        "observed": draw_observed(jax.random.fold_in(jax.random.fold_in(key_list[3], part), 71), part),
        "counts": draw_counts(jax.random.fold_in(jax.random.fold_in(key_list[3], part), 71), part),
    }


def reference(dosage, observed, counts):
    values = dosage.astype(jnp.float32)
    present = observed.astype(jnp.float32)
    present_count = jnp.maximum(lax.optimization_barrier(jnp.sum(present, axis=0)), 1.0)
    center = lax.optimization_barrier(jnp.sum(present * values, axis=0)) / present_count
    offsets = present * (values - center)
    spread = lax.optimization_barrier(jnp.sum(offsets * offsets, axis=0)) / present_count
    scored = (offsets * lax.rsqrt(spread + 1e-05)).astype(jnp.bfloat16)

    def one_block(block):
        own = lax.dynamic_slice_in_dim(scored, block * BLK, BLK, 1)
        tiles = []
        for offset in range(WIN):
            target = jnp.minimum(block + offset, NBLK - 1).astype(jnp.int32)
            partner = lax.dynamic_slice_in_dim(scored, target * BLK, BLK, 1)
            product = jnp.dot(own.T, partner, preferred_element_type=jnp.float32) / S
            keep = offset < counts[block]
            tiles.append(jnp.where(keep, product, jnp.zeros_like(product)))
        return jnp.stack(tiles).astype(jnp.bfloat16)
    return lax.map(one_block, jnp.arange(NBLK, dtype=jnp.int32))
```

```python
import jax
import jax.numpy as jnp
from jax import lax
from jax.sharding import PartitionSpec as P

WIN = 4
epsilon = 1e-05


def from_behind(shard, axis, by):
    count = lax.axis_size(axis)
    pairs = [(i + by, i) for i in range(count - by)]
    return lax.ppermute(shard, axis, pairs)


def from_mate(shard):
    return lax.ppermute(shard, "samp", [(0, 1), (1, 0)])


def contract(left, right):
    return lax.dot_general(
        left, right, (((0,), (0,)), ((), ())), preferred_element_type=jnp.float32
    )


def per_device(dosage, observed, counts):
    values = dosage.astype(jnp.float32)
    present = observed.astype(jnp.float32)
    present_count, summed, squares = lax.psum(
        (
            jnp.sum(present, axis=0),
            jnp.sum(present * values, axis=0),
            jnp.sum(present * values * values, axis=0),
        ),
        "samp",
    )
    present_count = jnp.maximum(present_count, 1.0)
    center = summed / present_count
    offsets = present * (values - center)
    spread = squares / present_count - center * center
    scored = (offsets * lax.rsqrt(spread + epsilon)).astype(jnp.bfloat16)
    width = scored.shape[1]
    half = width // lax.axis_size("samp")
    total_samples = float(scored.shape[0] * lax.axis_size("samp"))
    partner_count = counts[0]
    first = lax.axis_index("samp") * half
    other = from_mate(scored)
    left = lax.dynamic_slice_in_dim(scored, first, half, 1)
    left_other = lax.dynamic_slice_in_dim(other, first, half, 1)
    tiles = []
    for offset in range(WIN):
        if offset == 0:
            partner, partner_other = scored, other
        else:
            partner = from_behind(scored, "var", offset)
            partner_other = from_mate(partner)
        tile = contract(left, partner) + contract(left_other, partner_other)
        tile = jnp.where(offset < partner_count, tile / total_samples, 0.0)
        tiles.append(tile.astype(jnp.bfloat16))
    return jnp.stack(tiles)[None]


def solution(mesh):
    in_specs = (P("samp", ("region", "var")), P("samp", ("region", "var")), P(("region", "var")))
    out_specs = P(("region", "var"), None, "samp", None)
    return jax.shard_map(
        per_device, mesh=mesh, in_specs=in_specs, out_specs=out_specs, check_vma=False
    )
```

```python
import functools

import jax
import jax.numpy as jnp
from jax import lax
from jax.experimental import pallas as pl
from jax.experimental.pallas import tpu as pltpu
from jax.sharding import PartitionSpec as P

WIN = 4
QUARTERS = 4
ROW_PARTS = 2
epsilon = 1e-05


def product_kernel(scale, every, parity_ref, rows_ref, mine_ref, other_ref, out_ref):
    depth = mine_ref.shape[0]

    def work():
        total = jnp.dot(
            rows_ref[:, :depth], mine_ref[...], preferred_element_type=jnp.float32
        )
        total += jnp.dot(
            rows_ref[:, depth:], other_ref[...], preferred_element_type=jnp.float32
        )
        out_ref[...] = (total * scale).astype(out_ref.dtype)

    if every is None:
        work()
    else:
        pl.when(parity_ref[0] == every)(work)


def product(rows, mine, other, parity, every=None):
    count, samples = rows.shape
    width = mine.shape[1]
    return pl.pallas_call(
        functools.partial(product_kernel, 1.0 / samples, every),
        out_shape=jax.ShapeDtypeStruct((count, width), jnp.bfloat16),
        in_specs=[pl.BlockSpec(memory_space=pltpu.SMEM)]
        + [pl.BlockSpec(memory_space=pltpu.VMEM)] * 3,
        out_specs=pl.BlockSpec(memory_space=pltpu.VMEM),
        compiler_params=pltpu.CompilerParams(vmem_limit_bytes=32 * 1024 * 1024),
        cost_estimate=pl.CostEstimate(
            flops=2 * count * samples * width,
            bytes_accessed=2 * (count * samples + samples * width + count * width),
            transcendentals=0,
        ),
    )(parity, rows, mine, other)


def per_device(dosage, observed, counts):
    places = lax.axis_size("var")
    place = lax.axis_index("var")
    parity = (place % 2).astype(jnp.int32)
    odd = parity == 1
    parity = parity[None]

    def send(shard, pairs):
        return lax.ppermute(shard, "var", pairs)

    up = [(i, i + 2) for i in range(places - 2)]
    down = [(i + 2, i) for i in range(places - 2)]
    down_even = [pair for pair in down if pair[0] % 2 == 0]
    down_odd = [pair for pair in down if pair[0] % 2 == 1]
    to_even = [(i + 1, i) for i in range(0, places - 1, 2)]
    swap = to_even + [(i, i + 1) for i in range(0, places - 1, 2)]

    def mate(shard):
        return lax.ppermute(shard, "samp", [(0, 1), (1, 0)])

    values = dosage.astype(jnp.float32)
    present = observed.astype(jnp.float32)
    present_count, summed, squares = lax.psum(
        (
            jnp.sum(present, axis=0),
            jnp.sum(present * values, axis=0),
            jnp.sum(present * values * values, axis=0),
        ),
        "samp",
    )
    present_count = jnp.maximum(present_count, 1.0)
    center = summed / present_count
    offsets = present * (values - center)
    spread = squares / present_count - center * center
    scored = (offsets * lax.rsqrt(spread + epsilon)).astype(jnp.bfloat16)
    width = scored.shape[1]
    half = width // lax.axis_size("samp")
    quarter = width // QUARTERS
    part = half // ROW_PARTS

    own = [scored[:, j * quarter : (j + 1) * quarter] for j in range(QUARTERS)]
    own_other = [mate(piece) for piece in own]

    beside = send(own[0], swap)
    from_above = [None] + [send(own[j], down_even) for j in range(1, QUARTERS)]

    first = lax.axis_index("samp") * half
    rows = jnp.concatenate(
        [
            lax.dynamic_slice_in_dim(scored, first, half, 1).T,
            lax.dynamic_slice_in_dim(jnp.concatenate(own_other, 1), first, half, 1).T,
        ],
        axis=1,
    )
    rows_parts = [rows[r * part : (r + 1) * part] for r in range(ROW_PARTS)]
    below = [send(piece, up) for piece in rows_parts]

    around = send(beside, down_odd)
    next_one = [jnp.where(odd, around, beside)]
    for j in range(1, QUARTERS):
        next_one.append(send(jnp.where(odd, own[j], from_above[j]), swap))
    from_above[0] = send(around, to_even)
    next_other = [mate(piece) for piece in next_one]
    above_other = [mate(piece) for piece in from_above]

    def columns(pieces, begin, end):
        return pieces[begin] if end == begin + 1 else jnp.concatenate(pieces[begin:end], 1)

    own_all, own_other_all = scored, jnp.concatenate(own_other, 1)
    tile0 = product(rows, own_all, own_other_all, parity)

    back2 = [
        send(product(below[r], own_all, own_other_all, parity, 1), down_odd)
        for r in range(ROW_PARTS)
    ]
    back3 = [[None] * QUARTERS for _ in range(ROW_PARTS)]
    tile1 = []
    for j in range(QUARTERS):
        tile1.append(product(rows, next_one[j], next_other[j], parity))
        for r in range(ROW_PARTS):
            back3[r][j] = product(below[r], next_one[j], next_other[j], parity)
    tile3 = jnp.concatenate(
        [
            jnp.concatenate(
                [
                    send(jnp.concatenate(back3[r][:2], 1), down),
                    send(jnp.concatenate(back3[r][2:], 1), down),
                ],
                1,
            )
            for r in range(ROW_PARTS)
        ],
        0,
    )
    tile2 = jnp.concatenate(
        [
            product(rows, from_above[j], above_other[j], parity, 0)
            for j in range(QUARTERS)
        ],
        1,
    )
    tile2 = jnp.where(odd, jnp.concatenate(back2, 0), tile2)
    tiles = jnp.stack([tile0, jnp.concatenate(tile1, 1), tile2, tile3])
    keep = jnp.arange(WIN, dtype=jnp.int32)[:, None, None] < counts[0]
    return jnp.where(keep, tiles, jnp.zeros_like(tiles))[None]


def solution(mesh):
    in_specs = (P("samp", ("region", "var")), P("samp", ("region", "var")), P(("region", "var")))
    out_specs = P(("region", "var"), None, "samp", None)
    return jax.shard_map(
        per_device, mesh=mesh, in_specs=in_specs, out_specs=out_specs, check_vma=False
    )
```

```python
import functools

import jax
import jax.numpy as jnp
from jax import lax
from jax.experimental import pallas as pl
from jax.experimental.pallas import tpu as pltpu
from jax.sharding import PartitionSpec as P

WIN = 4
QUARTERS = 4
PARTS = 2
epsilon = 1e-05

SMEM = pl.BlockSpec(memory_space=pltpu.SMEM)
VMEM = pl.BlockSpec(memory_space=pltpu.VMEM)
ANY = pl.BlockSpec(memory_space=pl.ANY)
PARAMS = pltpu.CompilerParams(vmem_limit_bytes=32 * 1024 * 1024)
COST = pl.CostEstimate(flops=1000, bytes_accessed=1000, transcendentals=0)


def stats_kernel(dosage_ref, observed_ref, sums_ref, masked_ref):
    @pl.when(pl.program_id(0) == 0)
    def _():
        sums_ref[...] = jnp.zeros_like(sums_ref)

    values = dosage_ref[...].astype(jnp.float32)
    present = observed_ref[...] > 0
    kept = jnp.where(present, values, 0.0)
    masked_ref[...] = jnp.where(present, values, -1.0).astype(masked_ref.dtype)
    rows, width = values.shape

    def fold(terms):
        return jnp.sum(terms.reshape(rows // 8, 8, width), axis=0)

    sums_ref[0] += fold(jnp.where(present, 1.0, 0.0))
    sums_ref[1] += fold(kept)
    sums_ref[2] += fold(kept * kept)


def stats(dosage, observed):
    samples, width = dosage.shape
    block = samples // 8
    return pl.pallas_call(
        stats_kernel,
        grid=(samples // block,),
        in_specs=[pl.BlockSpec((block, width), lambda i: (i, 0))] * 2,
        out_specs=[
            pl.BlockSpec((3, 8, width), lambda i: (0, 0, 0)),
            pl.BlockSpec((block, width), lambda i: (i, 0)),
        ],
        out_shape=[
            jax.ShapeDtypeStruct((3, 8, width), jnp.float32),
            jax.ShapeDtypeStruct((samples, width), jnp.bfloat16),
        ],
        compiler_params=PARAMS,
        cost_estimate=COST,
    )(dosage, observed)


def score_kernel(place_ref, masked_ref, sums_ref, sums_other_ref, *outs):
    pieces, rows_here, rows_away = outs[:QUARTERS], outs[QUARTERS:-PARTS], outs[-PARTS:]
    core = place_ref[1]
    quarter = pieces[0].shape[1]
    per_core = QUARTERS // 2
    for j in range(QUARTERS):
        columns = slice(j * quarter, (j + 1) * quarter)
        totals = [
            jnp.sum(sums_ref[n, :, columns] + sums_other_ref[n, :, columns], axis=0, keepdims=True)
            for n in range(3)
        ]
        count = jnp.maximum(totals[0], 1.0)
        center = totals[1] / count
        spread = totals[2] / count - center * center
        factor = lax.rsqrt(spread + epsilon)
        masked = masked_ref[:, columns].astype(jnp.float32)
        scored = jnp.where(masked >= 0.0, (masked - center) * factor, 0.0)
        scored = scored.astype(jnp.bfloat16)
        pieces[j][...] = scored
        turned = scored.T
        here = core == j // per_core

        @pl.when(here)
        def _():
            rows_here[j % per_core][...] = turned

        @pl.when(jnp.logical_not(here))
        def _():
            rows_away[j % per_core][...] = turned


def score(place, masked, sums, sums_other):
    samples, width = masked.shape
    quarter = width // QUARTERS
    part = width // 2 // PARTS
    return pl.pallas_call(
        score_kernel,
        in_specs=[SMEM, VMEM, VMEM, VMEM],
        out_specs=[VMEM] * (QUARTERS + 2 * PARTS),
        out_shape=[jax.ShapeDtypeStruct((samples, quarter), jnp.bfloat16)] * QUARTERS
        + [jax.ShapeDtypeStruct((part, samples), jnp.bfloat16)] * (2 * PARTS),
        compiler_params=PARAMS,
        cost_estimate=COST,
    )(place, masked, sums, sums_other)


def dots(rows, rights, scale):
    total = None
    for left, right in zip(rows, rights):
        term = jnp.dot(left[...], right[...], preferred_element_type=jnp.float32)
        total = term if total is None else total + term
    return total * scale


def tile_kernel(k, parts, scale, place_ref, *refs):
    rows, out_ref = refs[: 2 * parts], refs[-1]
    rights = refs[2 * parts :]
    keep = k < place_ref[2]
    part = rows[0].shape[0]
    pairs = (out_ref.shape[2] + rights[0].shape[1] - 1) // rights[0].shape[1]
    quarter = rights[0].shape[1]
    for q in range(pairs):
        for r in range(parts):
            block = dots(rows[2 * r : 2 * r + 2], rights[2 * q : 2 * q + 2], scale)
            block = jnp.where(keep, block, 0.0)
            out_ref[0, r * part : (r + 1) * part, q * quarter : (q + 1) * quarter] = block.astype(
                out_ref.dtype
            )


def tile(place, buffer, k, column, rows, rights, samples):
    quarter = rights[0].shape[1]
    part = rows[0].shape[0]
    parts = len(rows) // 2
    pieces = len(rights) // 2
    width = quarter * QUARTERS
    shape = jax.ShapeDtypeStruct((WIN, part * parts, width), jnp.bfloat16)
    operands = [place, *rows, *rights]
    specs = [SMEM] + [VMEM] * (len(operands) - 1)
    kernel = functools.partial(tile_kernel, k, parts, 1.0 / samples)
    aliases = {}
    if buffer is not None:
        aliases = {len(operands): 0}
        operands.append(buffer)
        specs.append(ANY)
        inner = kernel

        def kernel(*refs):
            inner(*refs[:-2], refs[-1])

    return pl.pallas_call(
        kernel,
        grid=(1,),
        in_specs=specs,
        out_specs=pl.BlockSpec(
            (1, part * parts, quarter * pieces), lambda i: (k, 0, column // pieces)
        ),
        out_shape=shape,
        input_output_aliases=aliases,
        compiler_params=PARAMS,
        cost_estimate=COST,
    )(*operands)


def far_kernel(only_odd, scale, parts, place_ref, *refs):
    rows, out_ref = refs[: 2 * parts], refs[-2]
    rights = refs[2 * parts : -3]
    part = rows[0].shape[0]
    quarter = rights[0].shape[1]

    def work():
        for q in range(len(rights) // 2):
            for r in range(parts):
                block = dots(rows[2 * r : 2 * r + 2], rights[2 * q : 2 * q + 2], scale)
                out_ref[r * part : (r + 1) * part, q * quarter : (q + 1) * quarter] = block.astype(
                    out_ref.dtype
                )

    if only_odd:
        pl.when(place_ref[0] == 1)(work)
    else:
        work()


def far(place, buffer, rows, rights, samples, only_odd=False):
    parts = len(rows) // 2
    shape = (rows[0].shape[0] * parts, rights[0].shape[1] * (len(rights) // 2))
    operands = [place, *rows, *rights, buffer]
    return pl.pallas_call(
        functools.partial(far_kernel, only_odd, 1.0 / samples, parts),
        in_specs=[SMEM] + [VMEM] * (len(operands) - 2) + [ANY],
        out_specs=[VMEM, ANY],
        out_shape=[
            jax.ShapeDtypeStruct(shape, jnp.bfloat16),
            jax.ShapeDtypeStruct(buffer.shape, buffer.dtype),
        ],
        input_output_aliases={len(operands) - 1: 1},
        compiler_params=PARAMS,
        cost_estimate=COST,
    )(*operands)


def choose_kernel(place_ref, odd_ref, even_ref, buffer_ref, out_ref, passed_ref):
    @pl.when(place_ref[0] == 1)
    def _():
        out_ref[...] = odd_ref[...]

    @pl.when(place_ref[0] == 0)
    def _():
        out_ref[...] = even_ref[...]


def choose(place, buffer, if_odd, if_even):
    return pl.pallas_call(
        choose_kernel,
        in_specs=[SMEM, VMEM, VMEM, ANY],
        out_specs=[VMEM, ANY],
        out_shape=[
            jax.ShapeDtypeStruct(if_odd.shape, if_odd.dtype),
            jax.ShapeDtypeStruct(buffer.shape, buffer.dtype),
        ],
        input_output_aliases={3: 1},
        compiler_params=PARAMS,
        cost_estimate=COST,
    )(place, if_odd, if_even, buffer)


def last_kernel(scale, place_ref, *refs):
    rows = refs[: 2 * PARTS]
    mine_ref, other_ref = refs[2 * PARTS : 2 * PARTS + 2]
    back2 = refs[2 * PARTS + 2 : 3 * PARTS + 2]
    back3 = refs[3 * PARTS + 2 : -4]
    out_ref, second, third, sems = refs[-4:]
    part = rows[0].shape[0]
    quarter = mine_ref.shape[1]
    keep2, keep3 = 2 < place_ref[2], 3 < place_ref[2]
    odd = place_ref[0] == 1
    row, column = 0, 0
    third[0:part, 0 : 2 * quarter] = jnp.where(keep3, back3[0][...], 0.0).astype(third.dtype)
    third[part:, 0 : 2 * quarter] = jnp.where(keep3, back3[1][...], 0.0).astype(third.dtype)
    third[:, 2 * quarter : 3 * quarter] = jnp.where(keep3, back3[2][...], 0.0).astype(third.dtype)
    third[:, 3 * quarter :] = jnp.where(keep3, back3[3][...], 0.0).astype(third.dtype)
    copy3 = pltpu.make_async_copy(third, out_ref.at[3], sems.at[0])
    copy3.start()

    @pl.when(odd)
    def _():
        for r in range(PARTS):
            second[r * part : (r + 1) * part, :] = jnp.where(keep2, back2[r][...], 0.0).astype(
                second.dtype
            )
        copy = pltpu.make_async_copy(second, out_ref.at[2], sems.at[1])
        copy.start()
        copy.wait()

    @pl.when(jnp.logical_not(odd))
    def _():
        for r in range(PARTS):
            block = dots(rows[2 * r : 2 * r + 2], (mine_ref, other_ref), scale)
            second[r * part : (r + 1) * part, 0:quarter] = jnp.where(keep2, block, 0.0).astype(
                second.dtype
            )
        copy = pltpu.make_async_copy(
            second.at[:, 0:quarter], out_ref.at[2, :, 0:quarter], sems.at[1]
        )
        copy.start()
        copy.wait()

    copy3.wait()


def last(place, buffer, rows, mine, other, back2, back3, samples):
    operands = [place, *rows, mine, other, *back2, *back3, buffer]

    def kernel(*refs):
        count = len(operands)
        last_kernel(1.0 / samples, *refs[: count - 1], *refs[count:])

    return pl.pallas_call(
        kernel,
        in_specs=[SMEM] + [VMEM] * (len(operands) - 2) + [ANY],
        out_specs=ANY,
        out_shape=jax.ShapeDtypeStruct(buffer.shape, buffer.dtype),
        scratch_shapes=[
            pltpu.VMEM(buffer.shape[1:], buffer.dtype),
            pltpu.VMEM(buffer.shape[1:], buffer.dtype),
            pltpu.SemaphoreType.DMA((2,)),
        ],
        input_output_aliases={len(operands) - 1: 0},
        compiler_params=PARAMS,
        cost_estimate=COST,
    )(*operands)


def per_device(dosage, observed, counts):
    places = lax.axis_size("var")
    samples = dosage.shape[0] * lax.axis_size("samp")
    place = jnp.stack(
        [
            (lax.axis_index("var") % 2).astype(jnp.int32),
            lax.axis_index("samp").astype(jnp.int32),
            counts[0],
        ]
    )

    def send(shard, pairs):
        return lax.ppermute(shard, "var", pairs)

    up = [(i, i + 2) for i in range(places - 2)]
    down = [(i + 2, i) for i in range(places - 2)]
    down_even = [pair for pair in down if pair[0] % 2 == 0]
    down_odd = [pair for pair in down if pair[0] % 2 == 1]
    to_even = [(i + 1, i) for i in range(0, places - 1, 2)]
    swap = to_even + [(i, i + 1) for i in range(0, places - 1, 2)]

    def mate(shard):
        return lax.ppermute(shard, "samp", [(0, 1), (1, 0)])

    sums, masked = stats(dosage, observed)
    made = score(place, masked, sums, mate(sums))
    own, here, away = made[:QUARTERS], made[QUARTERS:-PARTS], made[-PARTS:]

    beside = send(own[0], swap)
    above = [None] * QUARTERS
    above[1] = send(own[1], down_even)
    below = [send(here[0], up)]
    arrived = [mate(piece) for piece in away]
    own_other = [mate(piece) for piece in own]
    above[2] = send(own[2], down_even)
    below.append(send(arrived[0], up))
    above[3] = send(own[3], down_even)
    below.append(send(here[1], up))
    below.append(send(arrived[1], up))
    rows = [here[0], arrived[0], here[1], arrived[1]]
    own_rights = [piece for pair in zip(own, own_other) for piece in pair]

    buffer = tile(place, None, 0, 0, rows, own_rights, samples)
    around = send(beside, down_odd)
    next_one = [None] * QUARTERS
    swapped, buffer = choose(place, buffer, own[1], above[1])
    next_one[1] = send(swapped, swap)
    swapped, buffer = choose(place, buffer, own[2], above[2])
    next_one[2] = send(swapped, swap)
    next_one[0], buffer = choose(place, buffer, around, beside)
    above[0] = send(around, to_even)
    next_other = [mate(next_one[0]), mate(next_one[1]), mate(next_one[2]), None]
    swapped, buffer = choose(place, buffer, own[3], above[3])
    next_one[3] = send(swapped, swap)
    next_other[3] = mate(next_one[3])
    above_other = [mate(piece) for piece in above]

    def pair(j):
        return [next_one[j], next_other[j]]

    back2, back3 = [None] * PARTS, [None] * 4
    made, buffer = far(place, buffer, below[:2], own_rights, samples, True)
    back2[0] = send(made, down_odd)
    buffer = tile(place, buffer, 1, 0, rows, pair(0), samples)
    buffer = tile(place, buffer, 1, 1, rows, pair(1), samples)
    made, buffer = far(place, buffer, below[:2], pair(0) + pair(1), samples)
    back3[0] = send(made, down)
    buffer = tile(place, buffer, 2, 1, rows, [above[1], above_other[1]], samples)
    buffer = tile(place, buffer, 2, 2, rows, [above[2], above_other[2]], samples)
    buffer = tile(place, buffer, 1, 2, rows, pair(2), samples)
    made, buffer = far(place, buffer, below[2:], own_rights, samples, True)
    back2[1] = send(made, down_odd)
    made, buffer = far(place, buffer, below[2:], pair(0) + pair(1), samples)
    back3[1] = send(made, down)
    made, buffer = far(place, buffer, below, pair(2), samples)
    back3[2] = send(made, down)
    made, buffer = far(place, buffer, below, pair(3), samples)
    back3[3] = send(made, down)
    buffer = tile(place, buffer, 1, 3, rows, pair(3), samples)
    buffer = tile(place, buffer, 2, 3, rows, [above[3], above_other[3]], samples)
    buffer = last(place, buffer, rows, above[0], above_other[0], back2, back3, samples)
    return buffer[None]


def solution(mesh):
    in_specs = (P("samp", ("region", "var")), P("samp", ("region", "var")), P(("region", "var")))
    out_specs = P(("region", "var"), None, "samp", None)
    return jax.shard_map(
        per_device, mesh=mesh, in_specs=in_specs, out_specs=out_specs, check_vma=False
    )
```

```python
import functools

import jax
import jax.numpy as jnp
from jax import lax
from jax.experimental import pallas as pl
from jax.experimental.pallas import tpu as pltpu
from jax.sharding import PartitionSpec as P

WIN = 4
QUARTERS = 4
PARTS = 2
BLOCKS = 8
STATS_VMEM = 50
epsilon = 1e-05

SMEM = pl.BlockSpec(memory_space=pltpu.SMEM)
VMEM = pl.BlockSpec(memory_space=pltpu.VMEM)
ANY = pl.BlockSpec(memory_space=pl.ANY)
PARAMS = pltpu.CompilerParams(vmem_limit_bytes=32 * 1024 * 1024)
COST = pl.CostEstimate(flops=1000, bytes_accessed=1000, transcendentals=0)


def stats_kernel(dosage_hbm, observed_hbm, sums_ref, masked_ref, dosage_ref, observed_ref, sems):
    samples, width = dosage_ref.shape
    block = samples // BLOCKS
    copies = []
    for n in range(BLOCKS):
        at = pl.ds(n * block, block)
        pair = [
            pltpu.make_async_copy(observed_hbm.at[at], observed_ref.at[at], sems.at[0, n]),
            pltpu.make_async_copy(dosage_hbm.at[at], dosage_ref.at[at], sems.at[1, n]),
        ]
        for copy in pair:
            copy.start()
        copies.append(pair)

    def fold(terms):
        return jnp.sum(terms.reshape(block // 8, 8, width), axis=0)

    totals = [jnp.zeros((8, width), jnp.float32)] * 3
    for n in range(BLOCKS):
        for copy in copies[n]:
            copy.wait()
        at = slice(n * block, (n + 1) * block)
        values = dosage_ref[at, :].astype(jnp.float32)
        present = observed_ref[at, :] > 0
        kept = jnp.where(present, values, 0.0)
        masked_ref[at, :] = jnp.where(present, values, -1.0).astype(masked_ref.dtype)
        terms = [jnp.where(present, 1.0, 0.0), kept, kept * kept]
        totals = [total + fold(term) for total, term in zip(totals, terms)]
    for n in range(3):
        sums_ref[n : n + 1, :] = jnp.sum(totals[n], axis=0, keepdims=True)
    sums_ref[3:, :] = jnp.zeros((5, width), jnp.float32)


def stats(dosage, observed):
    samples, width = dosage.shape
    return pl.pallas_call(
        stats_kernel,
        in_specs=[pl.BlockSpec(memory_space=pltpu.HBM)] * 2,
        out_specs=[VMEM, VMEM],
        out_shape=[
            jax.ShapeDtypeStruct((8, width), jnp.float32),
            jax.ShapeDtypeStruct((samples, width), jnp.bfloat16),
        ],
        scratch_shapes=[
            pltpu.VMEM(dosage.shape, dosage.dtype),
            pltpu.VMEM(observed.shape, observed.dtype),
            pltpu.SemaphoreType.DMA((2, BLOCKS)),
        ],
        compiler_params=pltpu.CompilerParams(vmem_limit_bytes=STATS_VMEM * 1024 * 1024),
        cost_estimate=COST,
    )(dosage, observed)


def score_kernel(place_ref, masked_ref, sums_ref, sums_other_ref, *outs):
    pieces, whole_ref = outs[:QUARTERS], outs[QUARTERS]
    rows_here, rows_away = outs[QUARTERS + 1 :]
    core = place_ref[1]
    quarter = pieces[0].shape[1]
    per_core = QUARTERS // 2
    for j in range(QUARTERS):
        columns = slice(j * quarter, (j + 1) * quarter)
        totals = [
            sums_ref[n : n + 1, columns] + sums_other_ref[n : n + 1, columns]
            for n in range(3)
        ]
        count = jnp.maximum(totals[0], 1.0)
        center = totals[1] / count
        spread = totals[2] / count - center * center
        factor = lax.rsqrt(spread + epsilon)
        masked = masked_ref[:, columns].astype(jnp.float32)
        scored = jnp.where(masked >= 0.0, (masked - center) * factor, 0.0)
        scored = scored.astype(jnp.bfloat16)
        pieces[j][...] = scored
        whole_ref[:, columns] = scored
        turned = scored.T
        here = core == j // per_core
        at = slice((j % per_core) * quarter, (j % per_core + 1) * quarter)

        @pl.when(here)
        def _():
            rows_here[at, :] = turned

        @pl.when(jnp.logical_not(here))
        def _():
            rows_away[at, :] = turned


def score(place, masked, sums, sums_other):
    samples, width = masked.shape
    quarter = width // QUARTERS
    return pl.pallas_call(
        score_kernel,
        in_specs=[SMEM, VMEM, VMEM, VMEM],
        out_specs=[VMEM] * (QUARTERS + 3),
        out_shape=[jax.ShapeDtypeStruct((samples, quarter), jnp.bfloat16)] * QUARTERS
        + [jax.ShapeDtypeStruct((samples, width), jnp.bfloat16)]
        + [jax.ShapeDtypeStruct((width // 2, samples), jnp.bfloat16)] * 2,
        compiler_params=PARAMS,
        cost_estimate=COST,
    )(place, masked, sums, sums_other)


def stack_kernel(here_ref, arrived_ref, *outs):
    part = outs[0].shape[0] // 2
    for r in range(PARTS):
        outs[r][0:part, :] = here_ref[r * part : (r + 1) * part, :]
        outs[r][part:, :] = arrived_ref[r * part : (r + 1) * part, :]


def stack(here, arrived):
    count, samples = here.shape
    return pl.pallas_call(
        stack_kernel,
        in_specs=[VMEM, VMEM],
        out_specs=[VMEM] * PARTS,
        out_shape=[jax.ShapeDtypeStruct((2 * count // PARTS, samples), here.dtype)] * PARTS,
        compiler_params=PARAMS,
        cost_estimate=COST,
    )(here, arrived)


def blocks(rows, rights, scale):
    part = rows[0].shape[0] // 2
    piece = min(right.shape[1] for right in rights)
    at = 0
    for q in range(len(rights) // 2):
        mine, other = rights[2 * q], rights[2 * q + 1]
        width = mine.shape[1]
        for begin in range(0, width, 256):
            end = min(begin + 256, width)
            for r, row in enumerate(rows):
                total = jnp.dot(
                    row[0:part, :], mine[:, begin:end], preferred_element_type=jnp.float32
                )
                total += jnp.dot(
                    row[part:, :], other[:, begin:end], preferred_element_type=jnp.float32
                )
                yield (
                    slice(r * part, (r + 1) * part),
                    slice(at + begin, at + end),
                    total * scale,
                )
        at += width


def tile_kernel(k, parts, scale, place_ref, *refs):
    out_ref = refs[-1]
    keep = k < place_ref[2]
    for at, columns, block in blocks(refs[:parts], refs[parts:-1], scale):
        out_ref[0, at, columns] = jnp.where(keep, block, 0.0).astype(out_ref.dtype)


def tile(place, buffer, k, column, rows, rights, samples, width, after=()):
    count = rows[0].shape[0] // 2 * len(rows)
    wide = sum(right.shape[1] for right in rights) // 2
    operands = [place, *rows, *rights]
    specs = [SMEM] + [VMEM] * (len(operands) - 1)
    kernel = functools.partial(tile_kernel, k, len(rows), 1.0 / samples)
    aliases = {}
    if buffer is not None:
        aliases = {len(operands): 0}
        operands += [buffer, *after]
        specs += [ANY] * (1 + len(after))
        inner, count_in = kernel, len(operands) - 1 - len(after)

        def kernel(*refs):
            inner(*refs[:count_in], refs[-1])

    return pl.pallas_call(
        kernel,
        grid=(1,),
        in_specs=specs,
        out_specs=pl.BlockSpec((1, count, wide), lambda i: (k, 0, column)),
        out_shape=jax.ShapeDtypeStruct((WIN, count, width), jnp.bfloat16),
        input_output_aliases=aliases,
        compiler_params=PARAMS,
        cost_estimate=COST,
    )(*operands)


def far_kernel(only_odd, scale, parts, pieces, place_ref, *refs):
    out_ref = refs[-2]

    def work():
        for at, columns, block in blocks(refs[:parts], refs[parts : parts + pieces], scale):
            out_ref[at, columns] = block.astype(out_ref.dtype)

    if only_odd:
        pl.when(place_ref[0] == 1)(work)
    else:
        work()


def far(place, buffer, rows, rights, samples, only_odd=False, after=()):
    shape = (
        rows[0].shape[0] // 2 * len(rows),
        sum(right.shape[1] for right in rights) // 2,
    )
    operands = [place, *rows, *rights, *after, buffer]
    return pl.pallas_call(
        functools.partial(far_kernel, only_odd, 1.0 / samples, len(rows), len(rights)),
        in_specs=[SMEM] + [VMEM] * (len(rows) + len(rights)) + [ANY] * (len(after) + 1),
        out_specs=[VMEM, ANY],
        out_shape=[
            jax.ShapeDtypeStruct(shape, jnp.bfloat16),
            jax.ShapeDtypeStruct(buffer.shape, buffer.dtype),
        ],
        input_output_aliases={len(operands) - 1: 1},
        compiler_params=PARAMS,
        cost_estimate=COST,
    )(*operands)


def choose_kernel(place_ref, odd_ref, even_ref, *refs):
    out_ref = refs[-1]

    @pl.when(place_ref[0] == 1)
    def _():
        out_ref[...] = odd_ref[...]

    @pl.when(place_ref[0] == 0)
    def _():
        out_ref[...] = even_ref[...]


def choose(place, if_odd, if_even, *passed):
    operands = [if_even, *passed]
    return pl.pallas_call(
        choose_kernel,
        in_specs=[SMEM, VMEM, VMEM] + [ANY] * len(passed),
        out_specs=[VMEM] + [ANY] * len(passed) + [VMEM],
        out_shape=[jax.ShapeDtypeStruct(x.shape, x.dtype) for x in (*operands, if_odd)],
        input_output_aliases={2 + n: n for n in range(len(operands))},
        compiler_params=PARAMS,
        cost_estimate=COST,
    )(place, if_odd, *operands)


def hold(after, *passed):
    def kernel(*refs):
        pass

    return pl.pallas_call(
        kernel,
        in_specs=[ANY] * (len(after) + len(passed)),
        out_specs=[ANY] * len(passed),
        out_shape=[jax.ShapeDtypeStruct(x.shape, x.dtype) for x in passed],
        input_output_aliases={len(after) + n: n for n in range(len(passed))},
        compiler_params=PARAMS,
        cost_estimate=COST,
    )(*after, *passed)


def last_kernel(place_ref, low_a, low_b, top, bottom, third, fourth, out_ref, two, three, sems):
    keep2, keep3 = 2 < place_ref[2], 3 < place_ref[2]
    part, half = top.shape
    quarter = half // 2

    def kept(keep, ref):
        return jnp.where(keep, ref[...], 0.0).astype(out_ref.dtype)

    three[0:part, 0:half] = kept(keep3, top)
    three[part:, 0:half] = kept(keep3, bottom)
    three[:, half : half + quarter] = kept(keep3, third)
    three[:, half + quarter :] = kept(keep3, fourth)
    copy3 = pltpu.make_async_copy(three, out_ref.at[3], sems.at[0])
    copy3.start()

    @pl.when(place_ref[0] == 1)
    def _():
        two[0:part, :] = kept(keep2, low_a)
        two[part:, :] = kept(keep2, low_b)
        copy2 = pltpu.make_async_copy(two, out_ref.at[2, :, half:], sems.at[1])
        copy2.start()
        copy2.wait()

    copy3.wait()


def last(place, buffer, back2, back3):
    operands = [place, *back2, *back3, buffer]
    count, width = buffer.shape[1:]

    def kernel(*refs):
        n = len(operands)
        last_kernel(*refs[: n - 1], *refs[n:])

    return pl.pallas_call(
        kernel,
        in_specs=[SMEM] + [VMEM] * (len(operands) - 2) + [ANY],
        out_specs=ANY,
        out_shape=jax.ShapeDtypeStruct(buffer.shape, buffer.dtype),
        scratch_shapes=[
            pltpu.VMEM((count, width // 2), buffer.dtype),
            pltpu.VMEM((count, width), buffer.dtype),
            pltpu.SemaphoreType.DMA((2,)),
        ],
        input_output_aliases={len(operands) - 1: 0},
        compiler_params=PARAMS,
        cost_estimate=COST,
    )(*operands)


def per_device(dosage, observed, counts):
    places = lax.axis_size("var")
    samples = dosage.shape[0] * lax.axis_size("samp")
    width = dosage.shape[1]
    place = jnp.stack(
        [
            (lax.axis_index("var") % 2).astype(jnp.int32),
            lax.axis_index("samp").astype(jnp.int32),
            counts[0],
        ]
    )

    def send(shard, pairs):
        return lax.ppermute(shard, "var", pairs)

    up = [(i, i + 2) for i in range(places - 2)]
    down = [(i + 2, i) for i in range(places - 2)]
    down_even = [pair for pair in down if pair[0] % 2 == 0]
    down_odd = [pair for pair in down if pair[0] % 2 == 1]
    to_even = [(i + 1, i) for i in range(0, places - 1, 2)]
    swap = to_even + [(i, i + 1) for i in range(0, places - 1, 2)]

    def mate(shard):
        return lax.ppermute(shard, "samp", [(0, 1), (1, 0)])

    sums, masked = stats(dosage, observed)
    *own, whole, here, away = score(place, masked, sums, mate(sums))
    above = [None] * QUARTERS
    above[0] = send(own[0], down)
    above[1] = send(own[1], down)
    rows = stack(here, mate(away))
    below = [send(rows[0], up), None]
    whole_other = mate(whole)
    next_one, other = [None] * QUARTERS, [None] * QUARTERS
    back2, back3 = [None] * 2, [None] * 4

    buffer = tile(place, None, 0, 0, rows, [whole, whole_other], samples, width)

    above[0], own[2], buffer, swapped = choose(place, own[0], above[0], own[2], buffer)
    next_one[0] = send(swapped, swap)
    above[2] = send(own[2], down_even)

    (buffer,) = hold((next_one[0],), buffer)
    above[1], own[3], buffer, swapped = choose(place, own[1], above[1], own[3], buffer)
    next_one[1] = send(swapped, swap)
    above[3] = send(own[3], down_even)
    row, buffer = hold((below[0],), rows[1], buffer)
    rows = [rows[0], row]
    below[1] = send(rows[1], up)
    own_upper = [own[2], mate(own[2]), own[3], mate(own[3])]
    made, buffer = far(place, buffer, below[:1], own_upper, samples, True)
    back2[0] = send(made, down_odd)
    other[0] = mate(next_one[0])
    buffer = tile(
        place, buffer, 2, 0, rows, [above[0], mate(above[0]), above[1], mate(above[1])],
        samples, width,
    )

    (buffer,) = hold((next_one[1],), buffer)
    above[2], buffer, swapped = choose(place, own[2], above[2], buffer)
    next_one[2] = send(swapped, swap)
    other[1] = mate(next_one[1])
    low = [next_one[0], other[0], next_one[1], other[1]]
    made, buffer = far(place, buffer, below[:1], low, samples)
    back3[0] = send(made, down)
    buffer = tile(place, buffer, 1, 0, rows, low, samples, width, (back2[0],))

    made, buffer = far(place, buffer, below[1:], own_upper, samples, True, (back3[0],))
    back2[1] = send(made, down_odd)

    (buffer,) = hold((next_one[2],), buffer)
    above[3], buffer, swapped = choose(place, own[3], above[3], buffer)
    next_one[3] = send(swapped, swap)
    made, buffer = far(place, buffer, below[1:], low, samples)
    back3[1] = send(made, down)
    other[2] = mate(next_one[2])
    made, buffer = far(
        place, buffer, below, [next_one[2], other[2]], samples, False, (back2[1],)
    )
    back3[2] = send(made, down)

    other[3] = mate(next_one[3])
    made, buffer = far(
        place, buffer, below, [next_one[3], other[3]], samples, False, (back3[1],)
    )
    back3[3] = send(made, down)
    buffer = tile(
        place, buffer, 2, 1, rows, [above[2], mate(above[2]), above[3], mate(above[3])],
        samples, width,
    )
    buffer = tile(
        place, buffer, 1, 1, rows, [next_one[2], other[2], next_one[3], other[3]], samples, width
    )
    buffer = last(place, buffer, back2, back3)
    return buffer[None]


def solution(mesh):
    in_specs = (P("samp", ("region", "var")), P("samp", ("region", "var")), P(("region", "var")))
    out_specs = P(("region", "var"), None, "samp", None)
    return jax.shard_map(
        per_device, mesh=mesh, in_specs=in_specs, out_specs=out_specs, check_vma=False
    )
```

```python
import functools

import jax
import jax.numpy as jnp
from jax import lax
from jax.experimental import pallas as pl
from jax.experimental.pallas import tpu as pltpu
from jax.sharding import PartitionSpec as P

WIN = 4
QUARTERS = 4
PARTS = 2
BLOCKS = 8
STATS_VMEM = 50
epsilon = 1e-05

SMEM = pl.BlockSpec(memory_space=pltpu.SMEM)
VMEM = pl.BlockSpec(memory_space=pltpu.VMEM)
ANY = pl.BlockSpec(memory_space=pl.ANY)
PARAMS = pltpu.CompilerParams(vmem_limit_bytes=32 * 1024 * 1024)
COST = pl.CostEstimate(flops=1000, bytes_accessed=1000, transcendentals=0)


def stats_kernel(dosage_hbm, observed_hbm, sums_ref, masked_ref, dosage_ref, observed_ref, sems):
    samples, width = dosage_ref.shape
    block = samples // BLOCKS
    copies = []
    for n in range(BLOCKS):
        at = pl.ds(n * block, block)
        pair = [
            pltpu.make_async_copy(observed_hbm.at[at], observed_ref.at[at], sems.at[0, n]),
            pltpu.make_async_copy(dosage_hbm.at[at], dosage_ref.at[at], sems.at[1, n]),
        ]
        for copy in pair:
            copy.start()
        copies.append(pair)

    def fold(terms):
        return jnp.sum(terms.reshape(block // 8, 8, width), axis=0)

    totals = [jnp.zeros((8, width), jnp.float32)] * 3
    for n in range(BLOCKS):
        for copy in copies[n]:
            copy.wait()
        at = slice(n * block, (n + 1) * block)
        values = dosage_ref[at, :].astype(jnp.float32)
        present = observed_ref[at, :] > 0
        kept = jnp.where(present, values, 0.0)
        masked_ref[at, :] = jnp.where(present, values, -1.0).astype(masked_ref.dtype)
        terms = [jnp.where(present, 1.0, 0.0), kept, kept * kept]
        totals = [total + fold(term) for total, term in zip(totals, terms)]
    for n in range(3):
        sums_ref[n : n + 1, :] = jnp.sum(totals[n], axis=0, keepdims=True)
    sums_ref[3:, :] = jnp.zeros((5, width), jnp.float32)


def stats(dosage, observed):
    samples, width = dosage.shape
    return pl.pallas_call(
        stats_kernel,
        in_specs=[pl.BlockSpec(memory_space=pltpu.HBM)] * 2,
        out_specs=[VMEM, VMEM],
        out_shape=[
            jax.ShapeDtypeStruct((8, width), jnp.float32),
            jax.ShapeDtypeStruct((samples, width), jnp.bfloat16),
        ],
        scratch_shapes=[
            pltpu.VMEM(dosage.shape, dosage.dtype),
            pltpu.VMEM(observed.shape, observed.dtype),
            pltpu.SemaphoreType.DMA((2, BLOCKS)),
        ],
        compiler_params=pltpu.CompilerParams(vmem_limit_bytes=STATS_VMEM * 1024 * 1024),
        cost_estimate=COST,
    )(dosage, observed)


def score_kernel(place_ref, masked_ref, sums_ref, sums_other_ref, *outs):
    pieces, whole_ref = outs[:QUARTERS], outs[QUARTERS]
    rows_here, rows_away = outs[QUARTERS + 1 :]
    core = place_ref[1]
    quarter = pieces[0].shape[1]
    per_core = QUARTERS // 2
    for j in range(QUARTERS):
        columns = slice(j * quarter, (j + 1) * quarter)
        totals = [
            sums_ref[n : n + 1, columns] + sums_other_ref[n : n + 1, columns]
            for n in range(3)
        ]
        count = jnp.maximum(totals[0], 1.0)
        center = totals[1] / count
        spread = totals[2] / count - center * center
        factor = lax.rsqrt(spread + epsilon)
        masked = masked_ref[:, columns].astype(jnp.float32)
        scored = jnp.where(masked >= 0.0, (masked - center) * factor, 0.0)
        scored = scored.astype(jnp.bfloat16)
        pieces[j][...] = scored
        whole_ref[:, columns] = scored
        turned = scored.T
        here = core == j // per_core
        at = slice((j % per_core) * quarter, (j % per_core + 1) * quarter)

        @pl.when(here)
        def _():
            rows_here[at, :] = turned

        @pl.when(jnp.logical_not(here))
        def _():
            rows_away[at, :] = turned


def score(place, masked, sums, sums_other):
    samples, width = masked.shape
    quarter = width // QUARTERS
    return pl.pallas_call(
        score_kernel,
        in_specs=[SMEM, VMEM, VMEM, VMEM],
        out_specs=[VMEM] * (QUARTERS + 3),
        out_shape=[jax.ShapeDtypeStruct((samples, quarter), jnp.bfloat16)] * QUARTERS
        + [jax.ShapeDtypeStruct((samples, width), jnp.bfloat16)]
        + [jax.ShapeDtypeStruct((width // 2, samples), jnp.bfloat16)] * 2,
        compiler_params=PARAMS,
        cost_estimate=COST,
    )(place, masked, sums, sums_other)


def stack_kernel(here_ref, arrived_ref, whole_ref, *outs):
    part = outs[0].shape[0] // 2
    for r in range(PARTS):
        outs[r][0:part, :] = here_ref[r * part : (r + 1) * part, :]
        outs[r][part:, :] = arrived_ref[r * part : (r + 1) * part, :]


def stack(here, arrived, whole):
    count, samples = here.shape
    return pl.pallas_call(
        stack_kernel,
        in_specs=[VMEM, VMEM, ANY],
        out_specs=[VMEM] * PARTS + [ANY],
        out_shape=[jax.ShapeDtypeStruct((2 * count // PARTS, samples), here.dtype)] * PARTS
        + [jax.ShapeDtypeStruct(whole.shape, whole.dtype)],
        input_output_aliases={2: PARTS},
        compiler_params=PARAMS,
        cost_estimate=COST,
    )(here, arrived, whole)


def blocks(rows, rights, scale, skip=0):
    part = rows[0].shape[0] // 2
    at = 0
    for q in range(len(rights) // 2):
        mine, other = rights[2 * q], rights[2 * q + 1]
        width = mine.shape[1]
        start = skip if q == len(rights) // 2 - 1 else 0
        at -= start
        for begin in range(start, width, 256):
            end = min(begin + 256, width)
            for r, row in enumerate(rows):
                total = jnp.dot(
                    row[0:part, :], mine[:, begin:end], preferred_element_type=jnp.float32
                )
                total += jnp.dot(
                    row[part:, :], other[:, begin:end], preferred_element_type=jnp.float32
                )
                yield (
                    slice(r * part, (r + 1) * part),
                    slice(at + begin, at + end),
                    total * scale,
                )
        at += width


def tile_kernel(k, parts, scale, place_ref, *refs):
    out_ref = refs[-1]
    keep = k < place_ref[2]
    for at, columns, block in blocks(refs[:parts], refs[parts:-1], scale):
        out_ref[0, at, columns] = jnp.where(keep, block, 0.0).astype(out_ref.dtype)


def tile(place, buffer, k, column, rows, rights, samples, width, after=()):
    count = rows[0].shape[0] // 2 * len(rows)
    wide = sum(right.shape[1] for right in rights) // 2
    operands = [place, *rows, *rights]
    specs = [SMEM] + [VMEM] * (len(operands) - 1)
    kernel = functools.partial(tile_kernel, k, len(rows), 1.0 / samples)
    aliases = {}
    if buffer is not None:
        aliases = {len(operands): 0}
        operands += [buffer, *after]
        specs += [ANY] * (1 + len(after))
        inner, count_in = kernel, len(operands) - 1 - len(after)

        def kernel(*refs):
            inner(*refs[:count_in], refs[-1])

    return pl.pallas_call(
        kernel,
        grid=(1,),
        in_specs=specs,
        out_specs=pl.BlockSpec((1, count, wide), lambda i: (k, 0, column)),
        out_shape=jax.ShapeDtypeStruct((WIN, count, width), jnp.bfloat16),
        input_output_aliases=aliases,
        compiler_params=PARAMS,
        cost_estimate=COST,
    )(*operands)


def far_kernel(only_odd, scale, parts, pieces, skip, place_ref, *refs):
    out_ref = refs[-2]

    def work():
        for at, columns, block in blocks(refs[:parts], refs[parts : parts + pieces], scale, skip):
            out_ref[at, columns] = block.astype(out_ref.dtype)

    if only_odd:
        pl.when(place_ref[0] == 1)(work)
    else:
        work()


def far(place, buffer, rows, rights, samples, only_odd=False, after=(), skip=0):
    shape = (
        rows[0].shape[0] // 2 * len(rows),
        sum(right.shape[1] for right in rights) // 2 - skip,
    )
    operands = [place, *rows, *rights, *after, buffer]
    return pl.pallas_call(
        functools.partial(far_kernel, only_odd, 1.0 / samples, len(rows), len(rights), skip),
        in_specs=[SMEM] + [VMEM] * (len(rows) + len(rights)) + [ANY] * (len(after) + 1),
        out_specs=[VMEM, ANY],
        out_shape=[
            jax.ShapeDtypeStruct(shape, jnp.bfloat16),
            jax.ShapeDtypeStruct(buffer.shape, buffer.dtype),
        ],
        input_output_aliases={len(operands) - 1: 1},
        compiler_params=PARAMS,
        cost_estimate=COST,
    )(*operands)


def choose_kernel(place_ref, odd_ref, even_ref, *refs):
    out_ref = refs[-1]

    @pl.when(place_ref[0] == 1)
    def _():
        out_ref[...] = odd_ref[...]

    @pl.when(place_ref[0] == 0)
    def _():
        out_ref[...] = even_ref[...]


def choose(place, if_odd, if_even, *passed):
    operands = [if_even, *passed]
    return pl.pallas_call(
        choose_kernel,
        in_specs=[SMEM, VMEM, VMEM] + [ANY] * len(passed),
        out_specs=[VMEM] + [ANY] * len(passed) + [VMEM],
        out_shape=[jax.ShapeDtypeStruct(x.shape, x.dtype) for x in (*operands, if_odd)],
        input_output_aliases={2 + n: n for n in range(len(operands))},
        compiler_params=PARAMS,
        cost_estimate=COST,
    )(place, if_odd, *operands)


def hold(after, *passed):
    def kernel(*refs):
        pass

    return pl.pallas_call(
        kernel,
        in_specs=[ANY] * (len(after) + len(passed)),
        out_specs=[ANY] * len(passed),
        out_shape=[jax.ShapeDtypeStruct(x.shape, x.dtype) for x in passed],
        input_output_aliases={len(after) + n: n for n in range(len(passed))},
        compiler_params=PARAMS,
        cost_estimate=COST,
    )(*after, *passed)


def last_kernel(place_ref, top2, top3, bottom, side, out_ref, two, three, sems):
    keep2, keep3 = 2 < place_ref[2], 3 < place_ref[2]
    part, half = top2.shape
    wide = top3.shape[1]

    def kept(keep, block):
        return jnp.where(keep, block, 0.0).astype(out_ref.dtype)

    two[0:part, :] = kept(keep2, top2[...])
    two[part:, :] = kept(keep2, bottom[:, wide:])
    copy2 = pltpu.make_async_copy(two, out_ref.at[2, :, half:], sems.at[0])
    copy2.start()
    three[0:part, 0:wide] = kept(keep3, top3[...])
    three[part:, 0:wide] = kept(keep3, bottom[:, 0:wide])
    three[:, wide:] = kept(keep3, side[...])
    copy3 = pltpu.make_async_copy(three, out_ref.at[3], sems.at[1])
    copy3.start()
    copy2.wait()
    copy3.wait()


def last(place, buffer, *received):
    operands = [place, *received, buffer]
    count, width = buffer.shape[1:]

    def kernel(*refs):
        n = len(operands)
        last_kernel(*refs[: n - 1], *refs[n:])

    return pl.pallas_call(
        kernel,
        in_specs=[SMEM] + [VMEM] * (len(operands) - 2) + [ANY],
        out_specs=ANY,
        out_shape=jax.ShapeDtypeStruct(buffer.shape, buffer.dtype),
        scratch_shapes=[
            pltpu.VMEM((count, width // 2), buffer.dtype),
            pltpu.VMEM((count, width), buffer.dtype),
            pltpu.SemaphoreType.DMA((2,)),
        ],
        input_output_aliases={len(operands) - 1: 0},
        compiler_params=PARAMS,
        cost_estimate=COST,
    )(*operands)


def per_device(dosage, observed, counts):
    places = lax.axis_size("var")
    samples = dosage.shape[0] * lax.axis_size("samp")
    width = dosage.shape[1]
    place = jnp.stack(
        [
            (lax.axis_index("var") % 2).astype(jnp.int32),
            lax.axis_index("samp").astype(jnp.int32),
            counts[0],
        ]
    )

    def send(shard, pairs):
        return lax.ppermute(shard, "var", pairs)

    before = [(i + 1, i) for i in range(places - 1)]
    up = [(i, i + 2) for i in range(places - 2)]
    down = [(i + 2, i) for i in range(places - 2)]
    down_odd = [pair for pair in down if pair[0] % 2 == 1]
    to_even = [(i + 1, i) for i in range(0, places - 1, 2)]
    swap = to_even + [(i, i + 1) for i in range(0, places - 1, 2)]

    def mate(shard):
        return lax.ppermute(shard, "samp", [(0, 1), (1, 0)])

    sums, masked = stats(dosage, observed)
    *own, whole, here, away = score(place, masked, sums, mate(sums))
    above = [None] * QUARTERS
    next_one, other = [None] * QUARTERS, [None] * QUARTERS

    above[0] = send(own[0], down)
    across = send(own[2], swap)
    *rows, whole = stack(here, mate(away), whole)
    below = [send(rows[0], up), send(rows[1], up)]
    whole_other = mate(whole)
    buffer = tile(place, None, 0, 0, rows, [whole, whole_other], samples, width)

    above[0], own[1], buffer, swapped = choose(place, own[0], above[0], own[1], buffer)
    next_one[0] = send(swapped, swap)
    above[1] = send(own[1], down)

    across, buffer = hold((next_one[0], below[0]), across, buffer)
    above[1], own[3], buffer, swapped = choose(place, own[1], above[1], own[3], buffer)
    next_one[1] = send(swapped, swap)
    around = send(across, down_odd)
    next_one[3] = send(own[3], before)
    made, buffer = far(place, buffer, below[:1], [whole, whole_other], samples, False, (), width // 2)
    top2 = send(made, down)

    (buffer,) = hold((next_one[1], top2), buffer)
    across, buffer, next_one[2] = choose(place, around, across, buffer)
    other[:3] = [mate(piece) for piece in next_one[:3]]
    low = [next_one[0], other[0], next_one[1], other[1]]
    high = [next_one[2], other[2]]
    made, buffer = far(place, buffer, below[:1], low + high, samples)
    top3 = send(made, down)
    (buffer,) = hold((below[1],), buffer)
    made, buffer = far(
        place, buffer, below[1:], low + high + [whole, whole_other], samples, False, (), width // 2
    )
    bottom = send(made, down)
    (next_one[3],) = hold((made, top3), next_one[3])
    buffer = tile(place, buffer, 1, 0, rows, low, samples, width)
    other[3] = mate(next_one[3])
    made, buffer = far(
        place, buffer, below, [next_one[3], other[3]], samples
    )
    side = send(made, down)
    buffer = tile(
        place, buffer, 2, 0, rows, [above[0], mate(above[0]), above[1], mate(above[1])],
        samples, width,
    )
    buffer = tile(place, buffer, 1, 1, rows, high + [next_one[3], other[3]], samples, width)
    buffer = last(place, buffer, top2, top3, bottom, side)
    return buffer[None]


def solution(mesh):
    in_specs = (P("samp", ("region", "var")), P("samp", ("region", "var")), P(("region", "var")))
    out_specs = P(("region", "var"), None, "samp", None)
    return jax.shard_map(
        per_device, mesh=mesh, in_specs=in_specs, out_specs=out_specs, check_vma=False
    )
```

```python
import functools

import jax
import jax.numpy as jnp
from jax import lax
from jax.experimental import pallas as pl
from jax.experimental.pallas import tpu as pltpu
from jax.sharding import PartitionSpec as P

WIN = 4
PIECES = (2, 2, 4)
PARTS = 2
BLOCKS = 8
STATS_VMEM = 50
epsilon = 1e-05

SMEM = pl.BlockSpec(memory_space=pltpu.SMEM)
VMEM = pl.BlockSpec(memory_space=pltpu.VMEM)
ANY = pl.BlockSpec(memory_space=pl.ANY)
PARAMS = pltpu.CompilerParams(vmem_limit_bytes=32 * 1024 * 1024)
COST = pl.CostEstimate(flops=1000, bytes_accessed=1000, transcendentals=0)


def stats_kernel(dosage_hbm, observed_hbm, sums_ref, masked_ref, dosage_ref, observed_ref, sems):
    samples, width = dosage_ref.shape
    block = samples // BLOCKS
    copies = []
    for n in range(BLOCKS):
        at = pl.ds(n * block, block)
        pair = [
            pltpu.make_async_copy(observed_hbm.at[at], observed_ref.at[at], sems.at[0, n]),
            pltpu.make_async_copy(dosage_hbm.at[at], dosage_ref.at[at], sems.at[1, n]),
        ]
        for copy in pair:
            copy.start()
        copies.append(pair)

    def fold(terms):
        return jnp.sum(terms.reshape(block // 8, 8, width), axis=0)

    totals = [jnp.zeros((8, width), jnp.float32)] * 3
    for n in range(BLOCKS):
        for copy in copies[n]:
            copy.wait()
        at = slice(n * block, (n + 1) * block)
        values = dosage_ref[at, :].astype(jnp.float32)
        present = observed_ref[at, :] > 0
        kept = jnp.where(present, values, 0.0)
        masked_ref[at, :] = jnp.where(present, values, -1.0).astype(masked_ref.dtype)
        terms = [jnp.where(present, 1.0, 0.0), kept, kept * kept]
        totals = [total + fold(term) for total, term in zip(totals, terms)]
    for n in range(3):
        sums_ref[n : n + 1, :] = jnp.sum(totals[n], axis=0, keepdims=True)
    sums_ref[3:, :] = jnp.zeros((5, width), jnp.float32)


def stats(dosage, observed):
    samples, width = dosage.shape
    return pl.pallas_call(
        stats_kernel,
        in_specs=[pl.BlockSpec(memory_space=pltpu.HBM)] * 2,
        out_specs=[VMEM, VMEM],
        out_shape=[
            jax.ShapeDtypeStruct((8, width), jnp.float32),
            jax.ShapeDtypeStruct((samples, width), jnp.bfloat16),
        ],
        scratch_shapes=[
            pltpu.VMEM(dosage.shape, dosage.dtype),
            pltpu.VMEM(observed.shape, observed.dtype),
            pltpu.SemaphoreType.DMA((2, BLOCKS)),
        ],
        compiler_params=pltpu.CompilerParams(vmem_limit_bytes=STATS_VMEM * 1024 * 1024),
        cost_estimate=COST,
    )(dosage, observed)


def score_kernel(place_ref, masked_ref, sums_ref, sums_other_ref, *outs):
    pieces, whole_ref = outs[: len(PIECES)], outs[len(PIECES)]
    rows_here, rows_away = outs[len(PIECES) + 1 : -PARTS], outs[-PARTS:]
    core = place_ref[1]
    part = rows_here[0].shape[0]
    for step in range(2 * PARTS):
        columns = slice(step * part, (step + 1) * part)
        totals = [
            sums_ref[n : n + 1, columns] + sums_other_ref[n : n + 1, columns]
            for n in range(3)
        ]
        count = jnp.maximum(totals[0], 1.0)
        center = totals[1] / count
        spread = totals[2] / count - center * center
        factor = lax.rsqrt(spread + epsilon)
        masked = masked_ref[:, columns].astype(jnp.float32)
        scored = jnp.where(masked >= 0.0, (masked - center) * factor, 0.0)
        scored = scored.astype(jnp.bfloat16)
        whole_ref[:, columns] = scored
        turned = scored.T
        here = core == step // PARTS

        @pl.when(here)
        def _():
            rows_here[step % PARTS][...] = turned

        @pl.when(jnp.logical_not(here))
        def _():
            rows_away[step % PARTS][...] = turned

    begin = 0
    for piece in pieces:
        piece[...] = whole_ref[:, begin : begin + piece.shape[1]]
        begin += piece.shape[1]


def score(place, masked, sums, sums_other):
    samples, width = masked.shape
    return pl.pallas_call(
        score_kernel,
        in_specs=[SMEM, VMEM, VMEM, VMEM],
        out_specs=[VMEM] * (len(PIECES) + 1 + 2 * PARTS),
        out_shape=[
            jax.ShapeDtypeStruct((samples, width * eighths // 8), jnp.bfloat16) for eighths in PIECES
        ]
        + [jax.ShapeDtypeStruct((samples, width), jnp.bfloat16)]
        + [jax.ShapeDtypeStruct((width // 2 // PARTS, samples), jnp.bfloat16)] * (2 * PARTS),
        compiler_params=PARAMS,
        cost_estimate=COST,
    )(place, masked, sums, sums_other)


def stack_kernel(here_ref, arrived_ref, out_ref, *rest):
    part = here_ref.shape[0]
    out_ref[0:part, :] = here_ref[...]
    out_ref[part:, :] = arrived_ref[...]


def stack(here, arrived, *made):
    count, samples = here.shape
    return pl.pallas_call(
        stack_kernel,
        in_specs=[VMEM, VMEM],
        out_specs=[VMEM] + [ANY] * len(made),
        out_shape=[jax.ShapeDtypeStruct((2 * count, samples), here.dtype), *made],
        compiler_params=PARAMS,
        cost_estimate=COST,
    )(here, arrived)


def blocks(rows, rights, scale, skip=0):
    part = rows[0].shape[0] // 2
    at = 0
    for q in range(len(rights) // 2):
        mine, other = rights[2 * q], rights[2 * q + 1]
        width = mine.shape[1]
        start = skip if q == len(rights) // 2 - 1 else 0
        at -= start
        for begin in range(start, width, 256):
            end = min(begin + 256, width)
            for r, row in enumerate(rows):
                total = jnp.dot(
                    row[0:part, :], mine[:, begin:end], preferred_element_type=jnp.float32
                )
                total += jnp.dot(
                    row[part:, :], other[:, begin:end], preferred_element_type=jnp.float32
                )
                yield (
                    slice(r * part, (r + 1) * part),
                    slice(at + begin, at + end),
                    total * scale,
                )
        at += width


def tile_kernel(k, parts, pieces, scale, place_ref, *refs):
    out_ref = refs[-1]
    keep = k < place_ref[2]
    for at, columns, block in blocks(refs[:parts], refs[parts : parts + pieces], scale):
        out_ref[0, at, columns] = jnp.where(keep, block, 0.0).astype(out_ref.dtype)


def tile(place, buffer, k, column, rows, rights, samples, after=()):
    count = rows[0].shape[0] // 2 * len(rows)
    wide = sum(right.shape[1] for right in rights) // 2
    operands = [place, *rows, *rights, *after, buffer]
    return pl.pallas_call(
        functools.partial(tile_kernel, k, len(rows), len(rights), 1.0 / samples),
        grid=(1,),
        in_specs=[SMEM] + [VMEM] * (len(rows) + len(rights)) + [ANY] * (1 + len(after)),
        out_specs=pl.BlockSpec((1, count, wide), lambda i: (k, 0, column)),
        out_shape=jax.ShapeDtypeStruct(buffer.shape, buffer.dtype),
        input_output_aliases={len(operands) - 1: 0},
        compiler_params=PARAMS,
        cost_estimate=COST,
    )(*operands)


def far_kernel(scale, parts, pieces, skip, place_ref, *refs):
    out_ref = refs[-2]
    for at, columns, block in blocks(refs[:parts], refs[parts : parts + pieces], scale, skip):
        out_ref[at, columns] = block.astype(out_ref.dtype)


def far(place, buffer, rows, rights, samples, skip=0):
    shape = (
        rows[0].shape[0] // 2 * len(rows),
        sum(right.shape[1] for right in rights) // 2 - skip,
    )
    operands = [place, *rows, *rights, buffer]
    return pl.pallas_call(
        functools.partial(far_kernel, 1.0 / samples, len(rows), len(rights), skip),
        in_specs=[SMEM] + [VMEM] * (len(rows) + len(rights)) + [ANY],
        out_specs=[VMEM, ANY],
        out_shape=[
            jax.ShapeDtypeStruct(shape, jnp.bfloat16),
            jax.ShapeDtypeStruct(buffer.shape, buffer.dtype),
        ],
        input_output_aliases={len(operands) - 1: 1},
        compiler_params=PARAMS,
        cost_estimate=COST,
    )(*operands)


def choose_kernel(place_ref, odd_ref, even_ref, *refs):
    out_ref = refs[-1]

    @pl.when(place_ref[0] == 1)
    def _():
        out_ref[...] = odd_ref[...]

    @pl.when(place_ref[0] == 0)
    def _():
        out_ref[...] = even_ref[...]


def choose(place, if_odd, if_even, *passed):
    operands = [if_even, *passed]
    return pl.pallas_call(
        choose_kernel,
        in_specs=[SMEM, VMEM, VMEM] + [ANY] * len(passed),
        out_specs=[VMEM] + [ANY] * len(passed) + [VMEM],
        out_shape=[jax.ShapeDtypeStruct(x.shape, x.dtype) for x in (*operands, if_odd)],
        input_output_aliases={2 + n: n for n in range(len(operands))},
        compiler_params=PARAMS,
        cost_estimate=COST,
    )(place, if_odd, *operands)


def hold(after, *passed):
    def kernel(*refs):
        pass

    return pl.pallas_call(
        kernel,
        in_specs=[ANY] * (len(after) + len(passed)),
        out_specs=[ANY] * len(passed),
        out_shape=[jax.ShapeDtypeStruct(x.shape, x.dtype) for x in passed],
        input_output_aliases={len(after) + n: n for n in range(len(passed))},
        compiler_params=PARAMS,
        cost_estimate=COST,
    )(*after, *passed)


def last_kernel(place_ref, top2, bottom2, wide3, side3, out_ref, two, three, sems):
    keep2, keep3 = 2 < place_ref[2], 3 < place_ref[2]
    part = top2.shape[0]
    first = side3.shape[1]

    def kept(keep, ref):
        return jnp.where(keep, ref[...], 0.0).astype(out_ref.dtype)

    two[0:part, :] = kept(keep2, top2)
    two[part:, :] = kept(keep2, bottom2)
    copy2 = pltpu.make_async_copy(two, out_ref.at[2, :, first:], sems.at[0])
    copy2.start()
    three[:, first:] = kept(keep3, wide3)
    three[:, 0:first] = kept(keep3, side3)
    copy3 = pltpu.make_async_copy(three, out_ref.at[3], sems.at[1])
    copy3.start()
    copy2.wait()
    copy3.wait()


def last(place, buffer, top2, bottom2, wide3, side3):
    operands = [place, top2, bottom2, wide3, side3, buffer]
    count, width = buffer.shape[1:]

    def kernel(*refs):
        n = len(operands)
        last_kernel(*refs[: n - 1], *refs[n:])

    return pl.pallas_call(
        kernel,
        in_specs=[SMEM] + [VMEM] * (len(operands) - 2) + [ANY],
        out_specs=ANY,
        out_shape=jax.ShapeDtypeStruct(buffer.shape, buffer.dtype),
        scratch_shapes=[
            pltpu.VMEM((count, top2.shape[1]), buffer.dtype),
            pltpu.VMEM((count, width), buffer.dtype),
            pltpu.SemaphoreType.DMA((2,)),
        ],
        input_output_aliases={len(operands) - 1: 0},
        compiler_params=PARAMS,
        cost_estimate=COST,
    )(*operands)


def per_device(dosage, observed, counts):
    places = lax.axis_size("var")
    samples = dosage.shape[0] * lax.axis_size("samp")
    width = dosage.shape[1]
    place = jnp.stack(
        [
            (lax.axis_index("var") % 2).astype(jnp.int32),
            lax.axis_index("samp").astype(jnp.int32),
            counts[0],
        ]
    )

    def send(shard, pairs):
        return lax.ppermute(shard, "var", pairs)

    before = [(i + 1, i) for i in range(places - 1)]
    up = [(i, i + 2) for i in range(places - 2)]
    down = [(i + 2, i) for i in range(places - 2)]
    down_odd = [pair for pair in down if pair[0] % 2 == 1]
    to_even = [(i + 1, i) for i in range(0, places - 1, 2)]
    swap = to_even + [(i, i + 1) for i in range(0, places - 1, 2)]

    def mate(shard):
        return lax.ppermute(shard, "samp", [(0, 1), (1, 0)])

    sums, masked = stats(dosage, observed)
    made = score(place, masked, sums, mate(sums))
    (relayed, detoured, direct), whole = made[:3], made[3]
    here, away = made[4:-PARTS], made[-PARTS:]
    first = relayed.shape[1]
    unset = jax.ShapeDtypeStruct((WIN, width // 2, width), jnp.bfloat16)

    upper, buffer = stack(here[0], mate(away[0]), unset)
    below0 = send(upper, up)
    above = send(relayed, down)
    across = send(detoured, swap)
    next_direct = send(direct, before)
    (lower,) = stack(here[1], mate(away[1]))
    below1 = send(lower, up)
    rows = [upper, lower]
    own = [whole, mate(whole)]

    around = send(across, down_odd)
    buffer = tile(place, buffer, 0, 0, rows, own, samples)
    across, buffer, next_detoured = choose(place, around, across, buffer)
    (buffer,) = hold((below0,), buffer)
    made, buffer = far(place, buffer, [below0], own, samples, first)
    top2 = send(made, down)
    above, buffer, swapped = choose(place, relayed, above, buffer)
    next_relayed = send(swapped, swap)

    (buffer,) = hold((below1, top2), buffer)
    made, buffer = far(place, buffer, [below1], own, samples, first)
    bottom2 = send(made, down)
    (next_direct,) = hold((made,), next_direct)
    high = [next_detoured, mate(next_detoured), next_direct, mate(next_direct)]
    made, buffer = far(place, buffer, [below0, below1], high, samples)
    wide3 = send(made, down)
    (next_relayed,) = hold((made, bottom2), next_relayed)
    low = [next_relayed, mate(next_relayed)]
    made, buffer = far(place, buffer, [below0, below1], low, samples)
    side3 = send(made, down)
    buffer = tile(place, buffer, 1, 1, rows, high[:2], samples)
    buffer = tile(place, buffer, 1, 1, rows, high[2:], samples)
    buffer = tile(place, buffer, 1, 0, rows, low, samples)
    buffer = tile(place, buffer, 2, 0, rows, [above, mate(above)], samples)
    buffer = last(place, buffer, top2, bottom2, wide3, side3)
    return buffer[None]


def solution(mesh):
    in_specs = (P("samp", ("region", "var")), P("samp", ("region", "var")), P(("region", "var")))
    out_specs = P(("region", "var"), None, "samp", None)
    return jax.shard_map(
        per_device, mesh=mesh, in_specs=in_specs, out_specs=out_specs, check_vma=False
    )
```

```python
import functools

import jax
import jax.numpy as jnp
from jax import lax
from jax.experimental import pallas as pl
from jax.experimental.pallas import tpu as pltpu
from jax.sharding import PartitionSpec as P

WIN = 4
PIECES = (2, 2, 4)
PARTS = 2
BLOCKS = 8
STATS_VMEM = 50
epsilon = 1e-05

SMEM = pl.BlockSpec(memory_space=pltpu.SMEM)
VMEM = pl.BlockSpec(memory_space=pltpu.VMEM)
ANY = pl.BlockSpec(memory_space=pl.ANY)
PARAMS = pltpu.CompilerParams(vmem_limit_bytes=32 * 1024 * 1024)
COST = pl.CostEstimate(flops=1000, bytes_accessed=1000, transcendentals=0)


def stats_kernel(dosage_hbm, observed_hbm, sums_ref, masked_ref, dosage_ref, observed_ref, sems):
    samples, width = dosage_ref.shape
    block = samples // BLOCKS
    copies = []
    for n in range(BLOCKS):
        at = pl.ds(n * block, block)
        pair = [
            pltpu.make_async_copy(observed_hbm.at[at], observed_ref.at[at], sems.at[0, n]),
            pltpu.make_async_copy(dosage_hbm.at[at], dosage_ref.at[at], sems.at[1, n]),
        ]
        for copy in pair:
            copy.start()
        copies.append(pair)

    def fold(terms):
        return jnp.sum(terms.reshape(block // 8, 8, width), axis=0)

    totals = [jnp.zeros((8, width), jnp.float32)] * 3
    for n in range(BLOCKS):
        for copy in copies[n]:
            copy.wait()
        at = slice(n * block, (n + 1) * block)
        values = dosage_ref[at, :].astype(jnp.float32)
        present = observed_ref[at, :] > 0
        kept = jnp.where(present, values, 0.0)
        masked_ref[at, :] = jnp.where(present, values, -1.0).astype(masked_ref.dtype)
        terms = [jnp.where(present, 1.0, 0.0), kept, kept * kept]
        totals = [total + fold(term) for total, term in zip(totals, terms)]
    for n in range(3):
        sums_ref[n : n + 1, :] = jnp.sum(totals[n], axis=0, keepdims=True)
    sums_ref[3:, :] = jnp.zeros((5, width), jnp.float32)


def stats(dosage, observed):
    samples, width = dosage.shape
    return pl.pallas_call(
        stats_kernel,
        in_specs=[pl.BlockSpec(memory_space=pltpu.HBM)] * 2,
        out_specs=[VMEM, VMEM],
        out_shape=[
            jax.ShapeDtypeStruct((8, width), jnp.float32),
            jax.ShapeDtypeStruct((samples, width), jnp.bfloat16),
        ],
        scratch_shapes=[
            pltpu.VMEM(dosage.shape, dosage.dtype),
            pltpu.VMEM(observed.shape, observed.dtype),
            pltpu.SemaphoreType.DMA((2, BLOCKS)),
        ],
        compiler_params=pltpu.CompilerParams(vmem_limit_bytes=STATS_VMEM * 1024 * 1024),
        cost_estimate=COST,
    )(dosage, observed)


def score_kernel(place_ref, masked_ref, sums_ref, sums_other_ref, *outs):
    pieces, whole_ref = outs[: len(PIECES)], outs[len(PIECES)]
    rows_here, rows_away = outs[len(PIECES) + 1 : -PARTS], outs[-PARTS:]
    core = place_ref[1]
    part = rows_here[0].shape[0]
    for step in range(2 * PARTS):
        columns = slice(step * part, (step + 1) * part)
        totals = [
            sums_ref[n : n + 1, columns] + sums_other_ref[n : n + 1, columns]
            for n in range(3)
        ]
        count = jnp.maximum(totals[0], 1.0)
        center = totals[1] / count
        spread = totals[2] / count - center * center
        factor = lax.rsqrt(spread + epsilon)
        masked = masked_ref[:, columns].astype(jnp.float32)
        scored = jnp.where(masked >= 0.0, (masked - center) * factor, 0.0)
        scored = scored.astype(jnp.bfloat16)
        whole_ref[:, columns] = scored
        turned = scored.T
        here = core == step // PARTS

        @pl.when(here)
        def _():
            rows_here[step % PARTS][...] = turned

        @pl.when(jnp.logical_not(here))
        def _():
            rows_away[step % PARTS][...] = turned

    begin = 0
    for piece in pieces:
        piece[...] = whole_ref[:, begin : begin + piece.shape[1]]
        begin += piece.shape[1]


def score(place, masked, sums, sums_other):
    samples, width = masked.shape
    return pl.pallas_call(
        score_kernel,
        in_specs=[SMEM, VMEM, VMEM, VMEM],
        out_specs=[VMEM] * (len(PIECES) + 1 + 2 * PARTS),
        out_shape=[
            jax.ShapeDtypeStruct((samples, width * eighths // 8), jnp.bfloat16) for eighths in PIECES
        ]
        + [jax.ShapeDtypeStruct((samples, width), jnp.bfloat16)]
        + [jax.ShapeDtypeStruct((width // 2 // PARTS, samples), jnp.bfloat16)] * (2 * PARTS),
        compiler_params=PARAMS,
        cost_estimate=COST,
    )(place, masked, sums, sums_other)


def stack(here, arrived, passed=(), unset=()):
    count, samples = here.shape

    def kernel(here_ref, arrived_ref, *refs):
        out_ref = refs[len(passed)]
        out_ref[0:count, :] = here_ref[...]
        out_ref[count:, :] = arrived_ref[...]

    return pl.pallas_call(
        kernel,
        in_specs=[VMEM, VMEM] + [ANY] * len(passed),
        out_specs=[VMEM] + [ANY] * (len(passed) + len(unset)),
        out_shape=[jax.ShapeDtypeStruct((2 * count, samples), here.dtype)]
        + [jax.ShapeDtypeStruct(x.shape, x.dtype) for x in (*passed, *unset)],
        input_output_aliases={2 + n: 1 + n for n in range(len(passed))},
        compiler_params=PARAMS,
        cost_estimate=COST,
    )(here, arrived, *passed)


def blocks(rows, rights, scale, skip=0):
    part = rows[0].shape[0] // 2
    at = 0
    for q in range(len(rights) // 2):
        mine, other = rights[2 * q], rights[2 * q + 1]
        width = mine.shape[1]
        start = skip if q == len(rights) // 2 - 1 else 0
        at -= start
        for begin in range(start, width, 256):
            end = min(begin + 256, width)
            for r, row in enumerate(rows):
                total = jnp.dot(
                    row[0:part, :], mine[:, begin:end], preferred_element_type=jnp.float32
                )
                total += jnp.dot(
                    row[part:, :], other[:, begin:end], preferred_element_type=jnp.float32
                )
                yield (
                    slice(r * part, (r + 1) * part),
                    slice(at + begin, at + end),
                    total * scale,
                )
        at += width


def tile_kernel(k, parts, pieces, scale, place_ref, *refs):
    out_ref = refs[-1]
    keep = k < place_ref[2]
    for at, columns, block in blocks(refs[:parts], refs[parts : parts + pieces], scale):
        out_ref[0, at, columns] = jnp.where(keep, block, 0.0).astype(out_ref.dtype)


def tile(place, buffer, k, column, rows, rights, samples, after=()):
    count = rows[0].shape[0] // 2 * len(rows)
    wide = sum(right.shape[1] for right in rights) // 2
    operands = [place, *rows, *rights, *after, buffer]
    return pl.pallas_call(
        functools.partial(tile_kernel, k, len(rows), len(rights), 1.0 / samples),
        grid=(1,),
        in_specs=[SMEM] + [VMEM] * (len(rows) + len(rights)) + [ANY] * (1 + len(after)),
        out_specs=pl.BlockSpec((1, count, wide), lambda i: (k, 0, column)),
        out_shape=jax.ShapeDtypeStruct(buffer.shape, buffer.dtype),
        input_output_aliases={len(operands) - 1: 0},
        compiler_params=PARAMS,
        cost_estimate=COST,
    )(*operands)


def far_kernel(scale, parts, pieces, skip, place_ref, *refs):
    out_ref = refs[-2]
    for at, columns, block in blocks(refs[:parts], refs[parts : parts + pieces], scale, skip):
        out_ref[at, columns] = block.astype(out_ref.dtype)


def far(place, buffer, rows, rights, samples, skip=0):
    shape = (
        rows[0].shape[0] // 2 * len(rows),
        sum(right.shape[1] for right in rights) // 2 - skip,
    )
    operands = [place, *rows, *rights, buffer]
    return pl.pallas_call(
        functools.partial(far_kernel, 1.0 / samples, len(rows), len(rights), skip),
        in_specs=[SMEM] + [VMEM] * (len(rows) + len(rights)) + [ANY],
        out_specs=[VMEM, ANY],
        out_shape=[
            jax.ShapeDtypeStruct(shape, jnp.bfloat16),
            jax.ShapeDtypeStruct(buffer.shape, buffer.dtype),
        ],
        input_output_aliases={len(operands) - 1: 1},
        compiler_params=PARAMS,
        cost_estimate=COST,
    )(*operands)


def choose_kernel(place_ref, odd_ref, even_ref, *refs):
    out_ref = refs[-1]

    @pl.when(place_ref[0] == 1)
    def _():
        out_ref[...] = odd_ref[...]

    @pl.when(place_ref[0] == 0)
    def _():
        out_ref[...] = even_ref[...]


def choose(place, if_odd, if_even, *passed):
    operands = [if_even, *passed]
    return pl.pallas_call(
        choose_kernel,
        in_specs=[SMEM, VMEM, VMEM] + [ANY] * len(passed),
        out_specs=[VMEM] + [ANY] * len(passed) + [VMEM],
        out_shape=[jax.ShapeDtypeStruct(x.shape, x.dtype) for x in (*operands, if_odd)],
        input_output_aliases={2 + n: n for n in range(len(operands))},
        compiler_params=PARAMS,
        cost_estimate=COST,
    )(place, if_odd, *operands)


def hold(after, *passed):
    def kernel(*refs):
        pass

    return pl.pallas_call(
        kernel,
        in_specs=[ANY] * (len(after) + len(passed)),
        out_specs=[ANY] * len(passed),
        out_shape=[jax.ShapeDtypeStruct(x.shape, x.dtype) for x in passed],
        input_output_aliases={len(after) + n: n for n in range(len(passed))},
        compiler_params=PARAMS,
        cost_estimate=COST,
    )(*after, *passed)


def split_kernel(count, whole_ref, *refs):
    outs = refs[-count:]
    begin = 0
    for out in outs:
        out[...] = whole_ref[:, begin : begin + out.shape[1]]
        begin += out.shape[1]


def split(piece, after, count):
    samples, width = piece.shape
    return pl.pallas_call(
        functools.partial(split_kernel, count),
        in_specs=[VMEM] + [ANY] * len(after),
        out_specs=[VMEM] * count,
        out_shape=[jax.ShapeDtypeStruct((samples, width // count), piece.dtype)] * count,
        compiler_params=PARAMS,
        cost_estimate=COST,
    )(piece, *after)


def last_kernel(place_ref, top2, top3, bottom, side, out_ref, two, three, sems):
    keep2, keep3 = 2 < place_ref[2], 3 < place_ref[2]
    part, wide = top2.shape
    first = side.shape[1]

    def kept(keep, block):
        return jnp.where(keep, block, 0.0).astype(out_ref.dtype)

    two[0:part, :] = kept(keep2, top2[...])
    two[part:, :] = kept(keep2, bottom[:, wide:])
    copy2 = pltpu.make_async_copy(two, out_ref.at[2, :, first:], sems.at[0])
    copy2.start()
    three[0:part, first:] = kept(keep3, top3[...])
    three[part:, first:] = kept(keep3, bottom[:, 0:wide])
    three[:, 0:first] = kept(keep3, side[...])
    copy3 = pltpu.make_async_copy(three, out_ref.at[3], sems.at[1])
    copy3.start()
    copy2.wait()
    copy3.wait()


def last(place, buffer, top2, top3, bottom, side):
    operands = [place, top2, top3, bottom, side, buffer]
    count, width = buffer.shape[1:]

    def kernel(*refs):
        n = len(operands)
        last_kernel(*refs[: n - 1], *refs[n:])

    return pl.pallas_call(
        kernel,
        in_specs=[SMEM] + [VMEM] * (len(operands) - 2) + [ANY],
        out_specs=ANY,
        out_shape=jax.ShapeDtypeStruct(buffer.shape, buffer.dtype),
        scratch_shapes=[
            pltpu.VMEM((count, top2.shape[1]), buffer.dtype),
            pltpu.VMEM((count, width), buffer.dtype),
            pltpu.SemaphoreType.DMA((2,)),
        ],
        input_output_aliases={len(operands) - 1: 0},
        compiler_params=PARAMS,
        cost_estimate=COST,
    )(*operands)


def per_device(dosage, observed, counts):
    places = lax.axis_size("var")
    samples = dosage.shape[0] * lax.axis_size("samp")
    width = dosage.shape[1]
    place = jnp.stack(
        [
            (lax.axis_index("var") % 2).astype(jnp.int32),
            lax.axis_index("samp").astype(jnp.int32),
            counts[0],
        ]
    )

    def send(shard, pairs):
        return lax.ppermute(shard, "var", pairs)

    before = [(i + 1, i) for i in range(places - 1)]
    up = [(i, i + 2) for i in range(places - 2)]
    down = [(i + 2, i) for i in range(places - 2)]
    down_odd = [pair for pair in down if pair[0] % 2 == 1]
    to_even = [(i + 1, i) for i in range(0, places - 1, 2)]
    swap = to_even + [(i, i + 1) for i in range(0, places - 1, 2)]

    def mate(shard):
        return lax.ppermute(shard, "samp", [(0, 1), (1, 0)])

    sums, masked = stats(dosage, observed)
    made = score(place, masked, sums, mate(sums))
    (relayed, detoured, direct), whole = made[:3], made[3]
    here, away = made[4:-PARTS], made[-PARTS:]
    first = relayed.shape[1]
    unset = jax.ShapeDtypeStruct((WIN, width // 2, width), jnp.bfloat16)

    upper, whole, buffer = stack(here[0], mate(away[0]), (whole,), (unset,))
    below0 = send(upper, up)
    above = send(relayed, down)
    across = send(detoured, swap)
    next_direct = send(direct, before)
    (lower,) = stack(here[1], mate(away[1]))
    below1 = send(lower, up)
    rows = [upper, lower]
    own = [whole, mate(whole)]
    around = send(across, down_odd)

    buffer = tile(place, buffer, 0, 0, rows, own, samples)
    (buffer,) = hold((below0,), buffer)
    made, buffer = far(place, buffer, [below0], own, samples, first)
    top2 = send(made, down)
    across, buffer, next_detoured = choose(place, around, across, buffer)
    high = [next_detoured, mate(next_detoured)]
    for piece in split(next_direct, (made,), 2):
        high += [piece, mate(piece)]
    (buffer,) = hold((top2,), buffer)
    made, buffer = far(place, buffer, [below0], high, samples)
    top3 = send(made, down)

    (buffer,) = hold((below1,), buffer)
    made, buffer = far(place, buffer, [below1], high + own, samples, first)
    bottom = send(made, down)
    (buffer,) = hold((top3,), buffer)
    above, buffer, swapped = choose(place, relayed, above, buffer)
    next_relayed = send(swapped, swap)
    low = []
    for piece in split(next_relayed, (), 2):
        low += [piece, mate(piece)]
    made, buffer = far(place, buffer, [below0, below1], low, samples)
    side = send(made, down)
    buffer = tile(place, buffer, 1, 1, rows, high[:2], samples)
    buffer = tile(place, buffer, 1, 1, rows, high[2:], samples)
    buffer = tile(place, buffer, 1, 0, rows, low, samples)
    buffer = tile(place, buffer, 2, 0, rows, [above, mate(above)], samples)
    buffer = last(place, buffer, top2, top3, bottom, side)
    return buffer[None]


def solution(mesh):
    in_specs = (P("samp", ("region", "var")), P("samp", ("region", "var")), P(("region", "var")))
    out_specs = P(("region", "var"), None, "samp", None)
    return jax.shard_map(
        per_device, mesh=mesh, in_specs=in_specs, out_specs=out_specs, check_vma=False
    )
```

```python
import functools

import jax
import jax.numpy as jnp
from jax import lax
from jax.experimental import pallas as pl
from jax.experimental.pallas import tpu as pltpu
from jax.sharding import PartitionSpec as P

WIN = 4
PIECES = (2, 2, 4)
PARTS = 2
BLOCKS = 8
STATS_VMEM = 50
epsilon = 1e-05

SMEM = pl.BlockSpec(memory_space=pltpu.SMEM)
VMEM = pl.BlockSpec(memory_space=pltpu.VMEM)
ANY = pl.BlockSpec(memory_space=pl.ANY)
PARAMS = pltpu.CompilerParams(vmem_limit_bytes=32 * 1024 * 1024)
COST = pl.CostEstimate(flops=1000, bytes_accessed=1000, transcendentals=0)


def stats_kernel(dosage_hbm, observed_hbm, sums_ref, masked_ref, dosage_ref, observed_ref, sems):
    samples, width = dosage_ref.shape
    block = samples // BLOCKS
    copies = []
    for n in range(BLOCKS):
        at = pl.ds(n * block, block)
        pair = [
            pltpu.make_async_copy(observed_hbm.at[at], observed_ref.at[at], sems.at[0, n]),
            pltpu.make_async_copy(dosage_hbm.at[at], dosage_ref.at[at], sems.at[1, n]),
        ]
        for copy in pair:
            copy.start()
        copies.append(pair)

    def fold(terms):
        return jnp.sum(terms.reshape(block // 8, 8, width), axis=0)

    totals = [jnp.zeros((8, width), jnp.float32)] * 3
    for n in range(BLOCKS):
        for copy in copies[n]:
            copy.wait()
        at = slice(n * block, (n + 1) * block)
        values = dosage_ref[at, :].astype(jnp.float32)
        present = observed_ref[at, :] > 0
        kept = jnp.where(present, values, 0.0)
        masked_ref[at, :] = jnp.where(present, values, -1.0).astype(masked_ref.dtype)
        terms = [jnp.where(present, 1.0, 0.0), kept, kept * kept]
        totals = [total + fold(term) for total, term in zip(totals, terms)]
    for n in range(3):
        sums_ref[n : n + 1, :] = jnp.sum(totals[n], axis=0, keepdims=True)
    sums_ref[3:, :] = jnp.zeros((5, width), jnp.float32)


def stats(dosage, observed):
    samples, width = dosage.shape
    return pl.pallas_call(
        stats_kernel,
        in_specs=[pl.BlockSpec(memory_space=pltpu.HBM)] * 2,
        out_specs=[VMEM, VMEM],
        out_shape=[
            jax.ShapeDtypeStruct((8, width), jnp.float32),
            jax.ShapeDtypeStruct((samples, width), jnp.bfloat16),
        ],
        scratch_shapes=[
            pltpu.VMEM(dosage.shape, dosage.dtype),
            pltpu.VMEM(observed.shape, observed.dtype),
            pltpu.SemaphoreType.DMA((2, BLOCKS)),
        ],
        compiler_params=pltpu.CompilerParams(vmem_limit_bytes=STATS_VMEM * 1024 * 1024),
        cost_estimate=COST,
    )(dosage, observed)


def score_kernel(place_ref, masked_ref, sums_ref, sums_other_ref, *outs):
    pieces, whole_ref = outs[: len(PIECES)], outs[len(PIECES)]
    rows_here, rows_away = outs[len(PIECES) + 1 : -PARTS], outs[-PARTS:]
    core = place_ref[1]
    part = rows_here[0].shape[0]
    for step in range(2 * PARTS):
        columns = slice(step * part, (step + 1) * part)
        totals = [
            sums_ref[n : n + 1, columns] + sums_other_ref[n : n + 1, columns]
            for n in range(3)
        ]
        count = jnp.maximum(totals[0], 1.0)
        center = totals[1] / count
        spread = totals[2] / count - center * center
        factor = lax.rsqrt(spread + epsilon)
        masked = masked_ref[:, columns].astype(jnp.float32)
        scored = jnp.where(masked >= 0.0, (masked - center) * factor, 0.0)
        scored = scored.astype(jnp.bfloat16)
        whole_ref[:, columns] = scored
        turned = scored.T
        here = core == step // PARTS

        @pl.when(here)
        def _():
            rows_here[step % PARTS][...] = turned

        @pl.when(jnp.logical_not(here))
        def _():
            rows_away[step % PARTS][...] = turned

    begin = 0
    for piece in pieces:
        piece[...] = whole_ref[:, begin : begin + piece.shape[1]]
        begin += piece.shape[1]


def score(place, masked, sums, sums_other):
    samples, width = masked.shape
    return pl.pallas_call(
        score_kernel,
        in_specs=[SMEM, VMEM, VMEM, VMEM],
        out_specs=[VMEM] * (len(PIECES) + 1 + 2 * PARTS),
        out_shape=[
            jax.ShapeDtypeStruct((samples, width * eighths // 8), jnp.bfloat16) for eighths in PIECES
        ]
        + [jax.ShapeDtypeStruct((samples, width), jnp.bfloat16)]
        + [jax.ShapeDtypeStruct((width // 2 // PARTS, samples), jnp.bfloat16)] * (2 * PARTS),
        compiler_params=PARAMS,
        cost_estimate=COST,
    )(place, masked, sums, sums_other)


def stack(here, arrived, passed=(), unset=()):
    count, samples = here.shape

    def kernel(here_ref, arrived_ref, *refs):
        out_ref = refs[len(passed)]
        out_ref[0:count, :] = here_ref[...]
        out_ref[count:, :] = arrived_ref[...]

    return pl.pallas_call(
        kernel,
        in_specs=[VMEM, VMEM] + [ANY] * len(passed),
        out_specs=[VMEM] + [ANY] * (len(passed) + len(unset)),
        out_shape=[jax.ShapeDtypeStruct((2 * count, samples), here.dtype)]
        + [jax.ShapeDtypeStruct(x.shape, x.dtype) for x in (*passed, *unset)],
        input_output_aliases={2 + n: 1 + n for n in range(len(passed))},
        compiler_params=PARAMS,
        cost_estimate=COST,
    )(here, arrived, *passed)


def blocks(rows, rights, scale, skip=0):
    part = rows[0].shape[0] // 2
    at = 0
    for q in range(len(rights) // 2):
        mine, other = rights[2 * q], rights[2 * q + 1]
        width = mine.shape[1]
        start = skip if q == len(rights) // 2 - 1 else 0
        at -= start
        for begin in range(start, width, 256):
            end = min(begin + 256, width)
            for r, row in enumerate(rows):
                total = jnp.dot(
                    row[0:part, :], mine[:, begin:end], preferred_element_type=jnp.float32
                )
                total += jnp.dot(
                    row[part:, :], other[:, begin:end], preferred_element_type=jnp.float32
                )
                yield (
                    slice(r * part, (r + 1) * part),
                    slice(at + begin, at + end),
                    total * scale,
                )
        at += width


def tile_kernel(k, parts, pieces, scale, place_ref, *refs):
    out_ref = refs[-1]
    keep = k < place_ref[2]
    for at, columns, block in blocks(refs[:parts], refs[parts : parts + pieces], scale):
        out_ref[0, at, columns] = jnp.where(keep, block, 0.0).astype(out_ref.dtype)


def tile(place, buffer, k, column, rows, rights, samples, after=()):
    count = rows[0].shape[0] // 2 * len(rows)
    wide = sum(right.shape[1] for right in rights) // 2
    operands = [place, *rows, *rights, *after, buffer]
    return pl.pallas_call(
        functools.partial(tile_kernel, k, len(rows), len(rights), 1.0 / samples),
        grid=(1,),
        in_specs=[SMEM] + [VMEM] * (len(rows) + len(rights)) + [ANY] * (1 + len(after)),
        out_specs=pl.BlockSpec((1, count, wide), lambda i: (k, 0, column)),
        out_shape=jax.ShapeDtypeStruct(buffer.shape, buffer.dtype),
        input_output_aliases={len(operands) - 1: 0},
        compiler_params=PARAMS,
        cost_estimate=COST,
    )(*operands)


def far_kernel(scale, parts, pieces, skip, place_ref, *refs):
    out_ref = refs[-2]
    for at, columns, block in blocks(refs[:parts], refs[parts : parts + pieces], scale, skip):
        out_ref[at, columns] = block.astype(out_ref.dtype)


def far(place, buffer, rows, rights, samples, skip=0):
    shape = (
        rows[0].shape[0] // 2 * len(rows),
        sum(right.shape[1] for right in rights) // 2 - skip,
    )
    operands = [place, *rows, *rights, buffer]
    return pl.pallas_call(
        functools.partial(far_kernel, 1.0 / samples, len(rows), len(rights), skip),
        in_specs=[SMEM] + [VMEM] * (len(rows) + len(rights)) + [ANY],
        out_specs=[VMEM, ANY],
        out_shape=[
            jax.ShapeDtypeStruct(shape, jnp.bfloat16),
            jax.ShapeDtypeStruct(buffer.shape, buffer.dtype),
        ],
        input_output_aliases={len(operands) - 1: 1},
        compiler_params=PARAMS,
        cost_estimate=COST,
    )(*operands)


def choose_kernel(place_ref, odd_ref, even_ref, *refs):
    out_ref = refs[-1]

    @pl.when(place_ref[0] == 1)
    def _():
        out_ref[...] = odd_ref[...]

    @pl.when(place_ref[0] == 0)
    def _():
        out_ref[...] = even_ref[...]


def choose(place, if_odd, if_even, *passed):
    operands = [if_even, *passed]
    return pl.pallas_call(
        choose_kernel,
        in_specs=[SMEM, VMEM, VMEM] + [ANY] * len(passed),
        out_specs=[VMEM] + [ANY] * len(passed) + [VMEM],
        out_shape=[jax.ShapeDtypeStruct(x.shape, x.dtype) for x in (*operands, if_odd)],
        input_output_aliases={2 + n: n for n in range(len(operands))},
        compiler_params=PARAMS,
        cost_estimate=COST,
    )(place, if_odd, *operands)


def hold(after, *passed):
    def kernel(*refs):
        pass

    return pl.pallas_call(
        kernel,
        in_specs=[ANY] * (len(after) + len(passed)),
        out_specs=[ANY] * len(passed),
        out_shape=[jax.ShapeDtypeStruct(x.shape, x.dtype) for x in passed],
        input_output_aliases={len(after) + n: n for n in range(len(passed))},
        compiler_params=PARAMS,
        cost_estimate=COST,
    )(*after, *passed)


def split_kernel(count, whole_ref, *refs):
    outs = refs[-count:]
    begin = 0
    for out in outs:
        out[...] = whole_ref[:, begin : begin + out.shape[1]]
        begin += out.shape[1]


def split(piece, after, count):
    samples, width = piece.shape
    return pl.pallas_call(
        functools.partial(split_kernel, count),
        in_specs=[VMEM] + [ANY] * len(after),
        out_specs=[VMEM] * count,
        out_shape=[jax.ShapeDtypeStruct((samples, width // count), piece.dtype)] * count,
        compiler_params=PARAMS,
        cost_estimate=COST,
    )(piece, *after)


def last_kernel(place_ref, top2, top3, bottom, side, out_ref, two, three, sems):
    keep2, keep3 = 2 < place_ref[2], 3 < place_ref[2]
    part, wide = top2.shape
    first = side.shape[1]

    def kept(keep, block):
        return jnp.where(keep, block, 0.0).astype(out_ref.dtype)

    two[0:part, :] = kept(keep2, top2[...])
    two[part:, :] = kept(keep2, bottom[:, wide:])
    copy2 = pltpu.make_async_copy(two, out_ref.at[2, :, first:], sems.at[0])
    copy2.start()
    three[0:part, first:] = kept(keep3, top3[...])
    three[part:, first:] = kept(keep3, bottom[:, 0:wide])
    three[:, 0:first] = kept(keep3, side[...])
    copy3 = pltpu.make_async_copy(three, out_ref.at[3], sems.at[1])
    copy3.start()
    copy2.wait()
    copy3.wait()


def last(place, buffer, top2, top3, bottom, side):
    operands = [place, top2, top3, bottom, side, buffer]
    count, width = buffer.shape[1:]

    def kernel(*refs):
        n = len(operands)
        last_kernel(*refs[: n - 1], *refs[n:])

    return pl.pallas_call(
        kernel,
        in_specs=[SMEM] + [VMEM] * (len(operands) - 2) + [ANY],
        out_specs=ANY,
        out_shape=jax.ShapeDtypeStruct(buffer.shape, buffer.dtype),
        scratch_shapes=[
            pltpu.VMEM((count, top2.shape[1]), buffer.dtype),
            pltpu.VMEM((count, width), buffer.dtype),
            pltpu.SemaphoreType.DMA((2,)),
        ],
        input_output_aliases={len(operands) - 1: 0},
        compiler_params=PARAMS,
        cost_estimate=COST,
    )(*operands)


def per_device(dosage, observed, counts):
    places = lax.axis_size("var")
    samples = dosage.shape[0] * lax.axis_size("samp")
    width = dosage.shape[1]
    place = jnp.stack(
        [
            (lax.axis_index("var") % 2).astype(jnp.int32),
            lax.axis_index("samp").astype(jnp.int32),
            counts[0],
        ]
    )

    def send(shard, pairs):
        return lax.ppermute(shard, "var", pairs)

    before = [(i + 1, i) for i in range(places - 1)]
    up = [(i, i + 2) for i in range(places - 2)]
    down = [(i + 2, i) for i in range(places - 2)]
    down_odd = [pair for pair in down if pair[0] % 2 == 1]
    to_even = [(i + 1, i) for i in range(0, places - 1, 2)]
    swap = to_even + [(i, i + 1) for i in range(0, places - 1, 2)]

    def mate(shard):
        return lax.ppermute(shard, "samp", [(0, 1), (1, 0)])

    sums, masked = stats(dosage, observed)
    made = score(place, masked, sums, mate(sums))
    (relayed, detoured, direct), whole = made[:3], made[3]
    here, away = made[4:-PARTS], made[-PARTS:]
    first = relayed.shape[1]
    unset = jax.ShapeDtypeStruct((WIN, width // 2, width), jnp.bfloat16)

    upper, whole, buffer = stack(here[0], mate(away[0]), (whole,), (unset,))
    below0 = send(upper, up)
    above = send(relayed, down)
    across = send(detoured, swap)
    (direct,) = hold((across, above), direct)
    next_direct = send(direct, before)
    (lower,) = stack(here[1], mate(away[1]))
    below1 = send(lower, up)
    rows = [upper, lower]
    own = [whole, mate(whole)]
    around = send(across, down_odd)

    buffer = tile(place, buffer, 0, 0, rows, own, samples)
    (buffer,) = hold((below0,), buffer)
    made, buffer = far(place, buffer, [below0], own, samples, first)
    top2 = send(made, down)
    across, buffer, next_detoured = choose(place, around, across, buffer)
    above, buffer, swapped = choose(place, relayed, above, buffer)
    next_relayed = send(swapped, swap)
    high = [next_detoured, mate(next_detoured)]
    for piece in split(next_direct, (made,), 2):
        high += [piece, mate(piece)]
    (buffer,) = hold((top2,), buffer)
    made, buffer = far(place, buffer, [below0], high, samples)
    top3 = send(made, down)

    (buffer,) = hold((below1,), buffer)
    made, buffer = far(place, buffer, [below1], high + own, samples, first)
    bottom = send(made, down)
    low = []
    for piece in split(next_relayed, (made, top3), 2):
        low += [piece, mate(piece)]
    made, buffer = far(place, buffer, [below0, below1], low, samples)
    side = send(made, down)
    buffer = tile(place, buffer, 1, 1, rows, high[:2], samples)
    buffer = tile(place, buffer, 1, 1, rows, high[2:], samples)
    buffer = tile(place, buffer, 1, 0, rows, low, samples)
    buffer = tile(place, buffer, 2, 0, rows, [above, mate(above)], samples)
    buffer = last(place, buffer, top2, top3, bottom, side)
    return buffer[None]


def solution(mesh):
    in_specs = (P("samp", ("region", "var")), P("samp", ("region", "var")), P(("region", "var")))
    out_specs = P(("region", "var"), None, "samp", None)
    return jax.shard_map(
        per_device, mesh=mesh, in_specs=in_specs, out_specs=out_specs, check_vma=False
    )
```

```python
import functools

import jax
import jax.numpy as jnp
from jax import lax
from jax.experimental import pallas as pl
from jax.experimental.pallas import tpu as pltpu
from jax.sharding import PartitionSpec as P

WIN = 4
PIECES = (2, 2, 4)
PARTS = 2
BLOCKS = 8
STATS_VMEM = 50
epsilon = 1e-05

SMEM = pl.BlockSpec(memory_space=pltpu.SMEM)
VMEM = pl.BlockSpec(memory_space=pltpu.VMEM)
ANY = pl.BlockSpec(memory_space=pl.ANY)
PARAMS = pltpu.CompilerParams(vmem_limit_bytes=32 * 1024 * 1024)
COST = pl.CostEstimate(flops=1000, bytes_accessed=1000, transcendentals=0)


def stats_kernel(dosage_hbm, observed_hbm, sums_ref, masked_ref, dosage_ref, observed_ref, sems):
    samples, width = dosage_ref.shape
    block = samples // BLOCKS
    copies = []
    for n in range(BLOCKS):
        at = pl.ds(n * block, block)
        pair = [
            pltpu.make_async_copy(observed_hbm.at[at], observed_ref.at[at], sems.at[0, n]),
            pltpu.make_async_copy(dosage_hbm.at[at], dosage_ref.at[at], sems.at[1, n]),
        ]
        for copy in pair:
            copy.start()
        copies.append(pair)

    def fold(terms):
        return jnp.sum(terms.reshape(block // 8, 8, width), axis=0)

    totals = [jnp.zeros((8, width), jnp.float32)] * 3
    for n in range(BLOCKS):
        for copy in copies[n]:
            copy.wait()
        at = slice(n * block, (n + 1) * block)
        values = dosage_ref[at, :].astype(jnp.float32)
        present = observed_ref[at, :] > 0
        kept = jnp.where(present, values, 0.0)
        masked_ref[at, :] = jnp.where(present, values, -1.0).astype(masked_ref.dtype)
        terms = [jnp.where(present, 1.0, 0.0), kept, kept * kept]
        totals = [total + fold(term) for total, term in zip(totals, terms)]
    for n in range(3):
        sums_ref[n : n + 1, :] = jnp.sum(totals[n], axis=0, keepdims=True)
    sums_ref[3:, :] = jnp.zeros((5, width), jnp.float32)


def stats(dosage, observed):
    samples, width = dosage.shape
    return pl.pallas_call(
        stats_kernel,
        in_specs=[pl.BlockSpec(memory_space=pltpu.HBM)] * 2,
        out_specs=[VMEM, VMEM],
        out_shape=[
            jax.ShapeDtypeStruct((8, width), jnp.float32),
            jax.ShapeDtypeStruct((samples, width), jnp.bfloat16),
        ],
        scratch_shapes=[
            pltpu.VMEM(dosage.shape, dosage.dtype),
            pltpu.VMEM(observed.shape, observed.dtype),
            pltpu.SemaphoreType.DMA((2, BLOCKS)),
        ],
        compiler_params=pltpu.CompilerParams(vmem_limit_bytes=STATS_VMEM * 1024 * 1024),
        cost_estimate=COST,
    )(dosage, observed)


def score_kernel(place_ref, masked_ref, sums_ref, sums_other_ref, *outs):
    pieces, whole_ref = outs[: len(PIECES)], outs[len(PIECES)]
    rows_here, rows_away = outs[len(PIECES) + 1 : -PARTS], outs[-PARTS:]
    core = place_ref[1]
    part = rows_here[0].shape[0]
    for step in range(2 * PARTS):
        columns = slice(step * part, (step + 1) * part)
        totals = [
            sums_ref[n : n + 1, columns] + sums_other_ref[n : n + 1, columns]
            for n in range(3)
        ]
        count = jnp.maximum(totals[0], 1.0)
        center = totals[1] / count
        spread = totals[2] / count - center * center
        factor = lax.rsqrt(spread + epsilon)
        masked = masked_ref[:, columns].astype(jnp.float32)
        scored = jnp.where(masked >= 0.0, (masked - center) * factor, 0.0)
        scored = scored.astype(jnp.bfloat16)
        whole_ref[:, columns] = scored
        turned = scored.T
        here = core == step // PARTS

        @pl.when(here)
        def _():
            rows_here[step % PARTS][...] = turned

        @pl.when(jnp.logical_not(here))
        def _():
            rows_away[step % PARTS][...] = turned

    begin = 0
    for piece in pieces:
        piece[...] = whole_ref[:, begin : begin + piece.shape[1]]
        begin += piece.shape[1]


def score(place, masked, sums, sums_other):
    samples, width = masked.shape
    return pl.pallas_call(
        score_kernel,
        in_specs=[SMEM, VMEM, VMEM, VMEM],
        out_specs=[VMEM] * (len(PIECES) + 1 + 2 * PARTS),
        out_shape=[
            jax.ShapeDtypeStruct((samples, width * eighths // 8), jnp.bfloat16) for eighths in PIECES
        ]
        + [jax.ShapeDtypeStruct((samples, width), jnp.bfloat16)]
        + [jax.ShapeDtypeStruct((width // 2 // PARTS, samples), jnp.bfloat16)] * (2 * PARTS),
        compiler_params=PARAMS,
        cost_estimate=COST,
    )(place, masked, sums, sums_other)


def stack(here, arrived, passed=(), unset=()):
    count, samples = here.shape

    def kernel(here_ref, arrived_ref, *refs):
        out_ref = refs[len(passed)]
        out_ref[0:count, :] = here_ref[...]
        out_ref[count:, :] = arrived_ref[...]

    return pl.pallas_call(
        kernel,
        in_specs=[VMEM, VMEM] + [ANY] * len(passed),
        out_specs=[VMEM] + [ANY] * (len(passed) + len(unset)),
        out_shape=[jax.ShapeDtypeStruct((2 * count, samples), here.dtype)]
        + [jax.ShapeDtypeStruct(x.shape, x.dtype) for x in (*passed, *unset)],
        input_output_aliases={2 + n: 1 + n for n in range(len(passed))},
        compiler_params=PARAMS,
        cost_estimate=COST,
    )(here, arrived, *passed)


def blocks(rows, rights, scale, skip=0):
    part = rows[0].shape[0] // 2
    at = 0
    for q in range(len(rights) // 2):
        mine, other = rights[2 * q], rights[2 * q + 1]
        width = mine.shape[1]
        start = skip if q == len(rights) // 2 - 1 else 0
        at -= start
        for begin in range(start, width, 256):
            end = min(begin + 256, width)
            for r, row in enumerate(rows):
                total = jnp.dot(
                    row[0:part, :], mine[:, begin:end], preferred_element_type=jnp.float32
                )
                total += jnp.dot(
                    row[part:, :], other[:, begin:end], preferred_element_type=jnp.float32
                )
                yield (
                    slice(r * part, (r + 1) * part),
                    slice(at + begin, at + end),
                    total * scale,
                )
        at += width


def tile_kernel(k, parts, pieces, scale, place_ref, *refs):
    out_ref = refs[-1]
    keep = k < place_ref[2]
    for at, columns, block in blocks(refs[:parts], refs[parts : parts + pieces], scale):
        out_ref[0, at, columns] = jnp.where(keep, block, 0.0).astype(out_ref.dtype)


def tile(place, buffer, k, column, rows, rights, samples, after=()):
    count = rows[0].shape[0] // 2 * len(rows)
    wide = sum(right.shape[1] for right in rights) // 2
    operands = [place, *rows, *rights, *after, buffer]
    return pl.pallas_call(
        functools.partial(tile_kernel, k, len(rows), len(rights), 1.0 / samples),
        grid=(1,),
        in_specs=[SMEM] + [VMEM] * (len(rows) + len(rights)) + [ANY] * (1 + len(after)),
        out_specs=pl.BlockSpec((1, count, wide), lambda i: (k, 0, column)),
        out_shape=jax.ShapeDtypeStruct(buffer.shape, buffer.dtype),
        input_output_aliases={len(operands) - 1: 0},
        compiler_params=PARAMS,
        cost_estimate=COST,
    )(*operands)


def far_kernel(scale, parts, pieces, skip, place_ref, *refs):
    out_ref = refs[-2]
    for at, columns, block in blocks(refs[:parts], refs[parts : parts + pieces], scale, skip):
        out_ref[at, columns] = block.astype(out_ref.dtype)


def far(place, buffer, rows, rights, samples, skip=0):
    shape = (
        rows[0].shape[0] // 2 * len(rows),
        sum(right.shape[1] for right in rights) // 2 - skip,
    )
    operands = [place, *rows, *rights, buffer]
    return pl.pallas_call(
        functools.partial(far_kernel, 1.0 / samples, len(rows), len(rights), skip),
        in_specs=[SMEM] + [VMEM] * (len(rows) + len(rights)) + [ANY],
        out_specs=[VMEM, ANY],
        out_shape=[
            jax.ShapeDtypeStruct(shape, jnp.bfloat16),
            jax.ShapeDtypeStruct(buffer.shape, buffer.dtype),
        ],
        input_output_aliases={len(operands) - 1: 1},
        compiler_params=PARAMS,
        cost_estimate=COST,
    )(*operands)


def choose_kernel(place_ref, odd_ref, even_ref, *refs):
    out_ref = refs[-1]

    @pl.when(place_ref[0] == 1)
    def _():
        out_ref[...] = odd_ref[...]

    @pl.when(place_ref[0] == 0)
    def _():
        out_ref[...] = even_ref[...]


def choose(place, if_odd, if_even, *passed):
    operands = [if_even, *passed]
    return pl.pallas_call(
        choose_kernel,
        in_specs=[SMEM, VMEM, VMEM] + [ANY] * len(passed),
        out_specs=[VMEM] + [ANY] * len(passed) + [VMEM],
        out_shape=[jax.ShapeDtypeStruct(x.shape, x.dtype) for x in (*operands, if_odd)],
        input_output_aliases={2 + n: n for n in range(len(operands))},
        compiler_params=PARAMS,
        cost_estimate=COST,
    )(place, if_odd, *operands)


def hold(after, *passed):
    def kernel(*refs):
        pass

    return pl.pallas_call(
        kernel,
        in_specs=[ANY] * (len(after) + len(passed)),
        out_specs=[ANY] * len(passed),
        out_shape=[jax.ShapeDtypeStruct(x.shape, x.dtype) for x in passed],
        input_output_aliases={len(after) + n: n for n in range(len(passed))},
        compiler_params=PARAMS,
        cost_estimate=COST,
    )(*after, *passed)


def split_kernel(count, whole_ref, *refs):
    outs = refs[-count:]
    begin = 0
    for out in outs:
        out[...] = whole_ref[:, begin : begin + out.shape[1]]
        begin += out.shape[1]


def split(piece, after, count):
    samples, width = piece.shape
    return pl.pallas_call(
        functools.partial(split_kernel, count),
        in_specs=[VMEM] + [ANY] * len(after),
        out_specs=[VMEM] * count,
        out_shape=[jax.ShapeDtypeStruct((samples, width // count), piece.dtype)] * count,
        compiler_params=PARAMS,
        cost_estimate=COST,
    )(piece, *after)


def last_kernel(place_ref, top2, top3, bottom, side, out_ref, two, three, sems):
    keep2, keep3 = 2 < place_ref[2], 3 < place_ref[2]
    part, wide = top2.shape
    first = side.shape[1]

    def kept(keep, block):
        return jnp.where(keep, block, 0.0).astype(out_ref.dtype)

    two[0:part, :] = kept(keep2, top2[...])
    two[part:, :] = kept(keep2, bottom[:, wide:])
    copy2 = pltpu.make_async_copy(two, out_ref.at[2, :, first:], sems.at[0])
    copy2.start()
    three[0:part, first:] = kept(keep3, top3[...])
    three[part:, first:] = kept(keep3, bottom[:, 0:wide])
    three[:, 0:first] = kept(keep3, side[...])
    copy3 = pltpu.make_async_copy(three, out_ref.at[3], sems.at[1])
    copy3.start()
    copy2.wait()
    copy3.wait()


def last(place, buffer, top2, top3, bottom, side):
    operands = [place, top2, top3, bottom, side, buffer]
    count, width = buffer.shape[1:]

    def kernel(*refs):
        n = len(operands)
        last_kernel(*refs[: n - 1], *refs[n:])

    return pl.pallas_call(
        kernel,
        in_specs=[SMEM] + [VMEM] * (len(operands) - 2) + [ANY],
        out_specs=ANY,
        out_shape=jax.ShapeDtypeStruct(buffer.shape, buffer.dtype),
        scratch_shapes=[
            pltpu.VMEM((count, top2.shape[1]), buffer.dtype),
            pltpu.VMEM((count, width), buffer.dtype),
            pltpu.SemaphoreType.DMA((2,)),
        ],
        input_output_aliases={len(operands) - 1: 0},
        compiler_params=PARAMS,
        cost_estimate=COST,
    )(*operands)


def per_device(dosage, observed, counts):
    places = lax.axis_size("var")
    samples = dosage.shape[0] * lax.axis_size("samp")
    width = dosage.shape[1]
    place = jnp.stack(
        [
            (lax.axis_index("var") % 2).astype(jnp.int32),
            lax.axis_index("samp").astype(jnp.int32),
            counts[0],
        ]
    )

    def send(shard, pairs):
        return lax.ppermute(shard, "var", pairs)

    before = [(i + 1, i) for i in range(places - 1)]
    up = [(i, i + 2) for i in range(places - 2)]
    down = [(i + 2, i) for i in range(places - 2)]
    down_odd = [pair for pair in down if pair[0] % 2 == 1]
    to_even = [(i + 1, i) for i in range(0, places - 1, 2)]
    swap = to_even + [(i, i + 1) for i in range(0, places - 1, 2)]

    def mate(shard):
        return lax.ppermute(shard, "samp", [(0, 1), (1, 0)])

    sums, masked = stats(dosage, observed)
    made = score(place, masked, sums, mate(sums))
    (relayed, detoured, direct), whole = made[:3], made[3]
    here, away = made[4:-PARTS], made[-PARTS:]
    first = relayed.shape[1]
    unset = jax.ShapeDtypeStruct((WIN, width // 2, width), jnp.bfloat16)

    upper, whole, buffer = stack(here[0], mate(away[0]), (whole,), (unset,))
    below0 = send(upper, up)
    above = send(relayed, down)
    across = send(detoured, swap)
    (direct,) = hold((across,), direct)
    next_direct = send(direct, before)
    (lower,) = stack(here[1], mate(away[1]))
    below1 = send(lower, up)
    rows = [upper, lower]
    own = [whole, mate(whole)]
    (across,) = hold((above,), across)
    around = send(across, down_odd)

    buffer = tile(place, buffer, 0, 0, rows, own, samples)
    (buffer,) = hold((below0,), buffer)
    made, buffer = far(place, buffer, [below0], own, samples, first)
    top2 = send(made, down)
    across, buffer, next_detoured = choose(place, around, across, buffer)
    above, buffer, swapped = choose(place, relayed, above, buffer)
    next_relayed = send(swapped, swap)
    high = [next_detoured, mate(next_detoured)]
    for piece in split(next_direct, (made,), 2):
        high += [piece, mate(piece)]
    made, buffer = far(place, buffer, [below0], high, samples)
    top3 = send(made, down)

    (buffer,) = hold((below1, top2), buffer)
    made, buffer = far(place, buffer, [below1], high + own, samples, first)
    bottom = send(made, down)
    low = []
    for piece in split(next_relayed, (made, top3), 2):
        low += [piece, mate(piece)]
    made, buffer = far(place, buffer, [below0, below1], low, samples)
    side = send(made, down)
    buffer = tile(place, buffer, 1, 1, rows, high[:2], samples)
    buffer = tile(place, buffer, 1, 1, rows, high[2:], samples)
    buffer = tile(place, buffer, 1, 0, rows, low, samples)
    buffer = tile(place, buffer, 2, 0, rows, [above, mate(above)], samples)
    buffer = last(place, buffer, top2, top3, bottom, side)
    return buffer[None]


def solution(mesh):
    in_specs = (P("samp", ("region", "var")), P("samp", ("region", "var")), P(("region", "var")))
    out_specs = P(("region", "var"), None, "samp", None)
    return jax.shard_map(
        per_device, mesh=mesh, in_specs=in_specs, out_specs=out_specs, check_vma=False
    )
```

```python
import functools

import jax
import jax.numpy as jnp
from jax import lax
from jax.experimental import pallas as pl
from jax.experimental.pallas import tpu as pltpu
from jax.sharding import PartitionSpec as P

WIN = 4
PIECES = (4, 2, 2)
ROWS = (4, 4)
PARTS = 2
BLOCKS = 8
STATS_VMEM = 50
epsilon = 1e-05

SMEM = pl.BlockSpec(memory_space=pltpu.SMEM)
VMEM = pl.BlockSpec(memory_space=pltpu.VMEM)
ANY = pl.BlockSpec(memory_space=pl.ANY)
PARAMS = pltpu.CompilerParams(vmem_limit_bytes=32 * 1024 * 1024)
COST = pl.CostEstimate(flops=1000, bytes_accessed=1000, transcendentals=0)


def stats_kernel(dosage_hbm, observed_hbm, sums_ref, masked_ref, dosage_ref, observed_ref, sems):
    samples, width = dosage_ref.shape
    block = samples // BLOCKS
    copies = []
    for n in range(BLOCKS):
        at = pl.ds(n * block, block)
        pair = [
            pltpu.make_async_copy(observed_hbm.at[at], observed_ref.at[at], sems.at[0, n]),
            pltpu.make_async_copy(dosage_hbm.at[at], dosage_ref.at[at], sems.at[1, n]),
        ]
        for copy in pair:
            copy.start()
        copies.append(pair)

    def fold(terms):
        return jnp.sum(terms.reshape(block // 8, 8, width), axis=0)

    totals = [jnp.zeros((8, width), jnp.float32)] * 3
    for n in range(BLOCKS):
        for copy in copies[n]:
            copy.wait()
        at = slice(n * block, (n + 1) * block)
        values = dosage_ref[at, :].astype(jnp.float32)
        present = observed_ref[at, :] > 0
        kept = jnp.where(present, values, 0.0)
        masked_ref[at, :] = jnp.where(present, values, -1.0).astype(masked_ref.dtype)
        terms = [jnp.where(present, 1.0, 0.0), kept, kept * kept]
        totals = [total + fold(term) for total, term in zip(totals, terms)]
    for n in range(3):
        sums_ref[n : n + 1, :] = jnp.sum(totals[n], axis=0, keepdims=True)
    sums_ref[3:, :] = jnp.zeros((5, width), jnp.float32)


def stats(dosage, observed):
    samples, width = dosage.shape
    return pl.pallas_call(
        stats_kernel,
        in_specs=[pl.BlockSpec(memory_space=pltpu.HBM)] * 2,
        out_specs=[VMEM, VMEM],
        out_shape=[
            jax.ShapeDtypeStruct((8, width), jnp.float32),
            jax.ShapeDtypeStruct((samples, width), jnp.bfloat16),
        ],
        scratch_shapes=[
            pltpu.VMEM(dosage.shape, dosage.dtype),
            pltpu.VMEM(observed.shape, observed.dtype),
            pltpu.SemaphoreType.DMA((2, BLOCKS)),
        ],
        compiler_params=pltpu.CompilerParams(vmem_limit_bytes=STATS_VMEM * 1024 * 1024),
        cost_estimate=COST,
    )(dosage, observed)


def score_kernel(place_ref, masked_ref, sums_ref, sums_other_ref, *outs):
    pieces = outs[: len(PIECES)]
    rows_here, rows_away = outs[len(PIECES) : -PARTS], outs[-PARTS:]
    core = place_ref[1]
    half = masked_ref.shape[1] // 2
    size = half // 2
    for step in range(4):
        columns = slice(step * size, (step + 1) * size)
        totals = [
            sums_ref[n : n + 1, columns] + sums_other_ref[n : n + 1, columns]
            for n in range(3)
        ]
        count = jnp.maximum(totals[0], 1.0)
        center = totals[1] / count
        spread = totals[2] / count - center * center
        factor = lax.rsqrt(spread + epsilon)
        masked = masked_ref[:, columns].astype(jnp.float32)
        scored = jnp.where(masked >= 0.0, (masked - center) * factor, 0.0)
        scored = scored.astype(jnp.bfloat16)
        at = 0
        for piece in pieces:
            low, high = max(step * size, at), min(step * size + size, at + piece.shape[1])
            if low < high:
                piece[:, low - at : high - at] = scored[:, low - step * size : high - step * size]
            at += piece.shape[1]
        turned = scored.T

        def put(parts, turned=turned, begin=step % 2 * size):
            at = 0
            for part in parts:
                low, high = max(begin, at), min(begin + size, at + part.shape[0])
                if low < high:
                    part[low - at : high - at, :] = turned[low - begin : high - begin, :]
                at += part.shape[0]

        here = core == step // 2
        pl.when(here)(functools.partial(put, rows_here))
        pl.when(jnp.logical_not(here))(functools.partial(put, rows_away))


def score(place, masked, sums, sums_other):
    samples, width = masked.shape
    return pl.pallas_call(
        score_kernel,
        in_specs=[SMEM, VMEM, VMEM, VMEM],
        out_specs=[VMEM] * (len(PIECES) + 2 * PARTS),
        out_shape=[
            jax.ShapeDtypeStruct((samples, width * eighths // 8), jnp.bfloat16) for eighths in PIECES
        ]
        + [
            jax.ShapeDtypeStruct((width // 2 * eighths // 8, samples), jnp.bfloat16)
            for eighths in ROWS + ROWS
        ],
        compiler_params=PARAMS,
        cost_estimate=COST,
    )(place, masked, sums, sums_other)


def stack(here, arrived, passed=(), unset=()):
    count, samples = here.shape

    def kernel(here_ref, arrived_ref, *refs):
        out_ref = refs[len(passed)]
        out_ref[0:count, :] = here_ref[...]
        out_ref[count:, :] = arrived_ref[...]

    return pl.pallas_call(
        kernel,
        in_specs=[VMEM, VMEM] + [ANY] * len(passed),
        out_specs=[VMEM] + [ANY] * (len(passed) + len(unset)),
        out_shape=[jax.ShapeDtypeStruct((2 * count, samples), here.dtype)]
        + [jax.ShapeDtypeStruct(x.shape, x.dtype) for x in (*passed, *unset)],
        input_output_aliases={2 + n: 1 + n for n in range(len(passed))},
        compiler_params=PARAMS,
        cost_estimate=COST,
    )(here, arrived, *passed)


def blocks(rows, rights, scale, stop=None):
    left = 0
    for q in range(len(rights) // 2):
        mine, other = rights[2 * q], rights[2 * q + 1]
        width = mine.shape[1]
        if stop is not None and q == len(rights) // 2 - 1:
            width = stop
        for begin in range(0, width, 256):
            end = min(begin + 256, width)
            top = 0
            for row in rows:
                part = row.shape[0] // 2
                total = jnp.dot(
                    row[0:part, :], mine[:, begin:end], preferred_element_type=jnp.float32
                )
                total += jnp.dot(
                    row[part:, :], other[:, begin:end], preferred_element_type=jnp.float32
                )
                yield slice(top, top + part), slice(left + begin, left + end), total * scale
                top += part
        left += width


def tile_kernel(k, parts, pieces, scale, place_ref, *refs):
    out_ref = refs[-1]
    keep = k < place_ref[2]
    for at, columns, block in blocks(refs[:parts], refs[parts : parts + pieces], scale):
        out_ref[0, at, columns] = jnp.where(keep, block, 0.0).astype(out_ref.dtype)


def tile(place, buffer, k, column, rows, rights, samples, after=()):
    count = sum(row.shape[0] for row in rows) // 2
    wide = sum(right.shape[1] for right in rights) // 2
    operands = [place, *rows, *rights, *after, buffer]
    return pl.pallas_call(
        functools.partial(tile_kernel, k, len(rows), len(rights), 1.0 / samples),
        grid=(1,),
        in_specs=[SMEM] + [VMEM] * (len(rows) + len(rights)) + [ANY] * (1 + len(after)),
        out_specs=pl.BlockSpec((1, count, wide), lambda i: (k, 0, column)),
        out_shape=jax.ShapeDtypeStruct(buffer.shape, buffer.dtype),
        input_output_aliases={len(operands) - 1: 0},
        compiler_params=PARAMS,
        cost_estimate=COST,
    )(*operands)


def far_kernel(scale, parts, pieces, stop, place_ref, *refs):
    out_ref = refs[-2]
    for at, columns, block in blocks(refs[:parts], refs[parts : parts + pieces], scale, stop):
        out_ref[at, columns] = block.astype(out_ref.dtype)


def far(place, buffer, rows, rights, samples, stop=None):
    wide = sum(right.shape[1] for right in rights) // 2
    if stop is not None:
        wide += stop - rights[-1].shape[1]
    shape = (sum(row.shape[0] for row in rows) // 2, wide)
    operands = [place, *rows, *rights, buffer]
    return pl.pallas_call(
        functools.partial(far_kernel, 1.0 / samples, len(rows), len(rights), stop),
        in_specs=[SMEM] + [VMEM] * (len(rows) + len(rights)) + [ANY],
        out_specs=[VMEM, ANY],
        out_shape=[
            jax.ShapeDtypeStruct(shape, jnp.bfloat16),
            jax.ShapeDtypeStruct(buffer.shape, buffer.dtype),
        ],
        input_output_aliases={len(operands) - 1: 1},
        compiler_params=PARAMS,
        cost_estimate=COST,
    )(*operands)


def choose_kernel(place_ref, odd_ref, even_ref, *refs):
    out_ref = refs[-1]

    @pl.when(place_ref[0] == 1)
    def _():
        out_ref[...] = odd_ref[...]

    @pl.when(place_ref[0] == 0)
    def _():
        out_ref[...] = even_ref[...]


def choose(place, if_odd, if_even, passed=(), after=()):
    operands = [if_even, *passed]
    return pl.pallas_call(
        choose_kernel,
        in_specs=[SMEM, VMEM, VMEM] + [ANY] * (len(passed) + len(after)),
        out_specs=[VMEM] + [ANY] * len(passed) + [VMEM],
        out_shape=[jax.ShapeDtypeStruct(x.shape, x.dtype) for x in (*operands, if_odd)],
        input_output_aliases={2 + n: n for n in range(len(operands))},
        compiler_params=PARAMS,
        cost_estimate=COST,
    )(place, if_odd, *operands, *after)


def hold(after, *passed):
    def kernel(*refs):
        pass

    return pl.pallas_call(
        kernel,
        in_specs=[ANY] * (len(after) + len(passed)),
        out_specs=[ANY] * len(passed),
        out_shape=[jax.ShapeDtypeStruct(x.shape, x.dtype) for x in passed],
        input_output_aliases={len(after) + n: n for n in range(len(passed))},
        compiler_params=PARAMS,
        cost_estimate=COST,
    )(*after, *passed)


def split_kernel(count, whole_ref, *refs):
    outs = refs[-count:]
    begin = 0
    for out in outs:
        out[...] = whole_ref[:, begin : begin + out.shape[1]]
        begin += out.shape[1]


def split(piece, after, count):
    samples, width = piece.shape
    return pl.pallas_call(
        functools.partial(split_kernel, count),
        in_specs=[VMEM] + [ANY] * len(after),
        out_specs=[VMEM] * count,
        out_shape=[jax.ShapeDtypeStruct((samples, width // count), piece.dtype)] * count,
        compiler_params=PARAMS,
        cost_estimate=COST,
    )(piece, *after)


def last_kernel(place_ref, top2, top3, bottom, side, out_ref, two, three, sems):
    keep2, keep3 = 2 < place_ref[2], 3 < place_ref[2]
    part, wide = top2.shape
    first, after = wide - wide * PIECES[2] // (PIECES[0] + PIECES[2]), side.shape[1]

    def kept(keep, block):
        return jnp.where(keep, block, 0.0).astype(out_ref.dtype)

    two[0:part, 0:wide] = kept(keep2, top2[...])
    two[part:, 0:wide] = kept(keep2, bottom[:, wide:])
    copies = [
        pltpu.make_async_copy(two.at[:, 0:first], out_ref.at[2, :, 0:first], sems.at[0]),
        pltpu.make_async_copy(two.at[:, first:], out_ref.at[2, :, first + after :], sems.at[1]),
        pltpu.make_async_copy(three, out_ref.at[3], sems.at[2]),
    ]
    copies[0].start()
    copies[1].start()
    for at, columns in ((0, slice(0, first)), (first, slice(first + after, None))):
        received = slice(at, first if at == 0 else wide)
        three[0:part, columns] = kept(keep3, top3[:, received])
        three[part:, columns] = kept(keep3, bottom[:, received])
    three[:, first : first + after] = kept(keep3, side[...])
    copies[2].start()
    for copy in copies:
        copy.wait()


def last(place, buffer, top2, top3, bottom, side):
    operands = [place, top2, top3, bottom, side, buffer]
    count, width = buffer.shape[1:]

    def kernel(*refs):
        n = len(operands)
        last_kernel(*refs[: n - 1], *refs[n:])

    return pl.pallas_call(
        kernel,
        in_specs=[SMEM] + [VMEM] * (len(operands) - 2) + [ANY],
        out_specs=ANY,
        out_shape=jax.ShapeDtypeStruct(buffer.shape, buffer.dtype),
        scratch_shapes=[
            pltpu.VMEM((count, top2.shape[1]), buffer.dtype),
            pltpu.VMEM((count, width), buffer.dtype),
            pltpu.SemaphoreType.DMA((3,)),
        ],
        input_output_aliases={len(operands) - 1: 0},
        compiler_params=PARAMS,
        cost_estimate=COST,
    )(*operands)


def per_device(dosage, observed, counts):
    places = lax.axis_size("var")
    samples = dosage.shape[0] * lax.axis_size("samp")
    width = dosage.shape[1]
    place = jnp.stack(
        [
            (lax.axis_index("var") % 2).astype(jnp.int32),
            lax.axis_index("samp").astype(jnp.int32),
            counts[0],
        ]
    )

    def send(shard, pairs):
        return lax.ppermute(shard, "var", pairs)

    before = [(i + 1, i) for i in range(places - 1)]
    up = [(i, i + 2) for i in range(places - 2)]
    down = [(i + 2, i) for i in range(places - 2)]
    down_odd = [pair for pair in down if pair[0] % 2 == 1]
    to_even = [(i + 1, i) for i in range(0, places - 1, 2)]
    swap = to_even + [(i, i + 1) for i in range(0, places - 1, 2)]

    def mate(shard):
        return lax.ppermute(shard, "samp", [(0, 1), (1, 0)])

    sums, masked = stats(dosage, observed)
    made = score(place, masked, sums, mate(sums))
    direct, relayed, detoured = made[:3]
    here, away = made[3:-PARTS], made[-PARTS:]
    unset = jax.ShapeDtypeStruct((WIN, width // 2, width), jnp.bfloat16)

    upper, buffer = stack(here[0], mate(away[0]), (), (unset,))
    below0 = send(upper, up)
    above = send(relayed, down)
    across = send(detoured, swap)
    (direct,) = hold((across,), direct)
    next_direct = send(direct, before)
    (lower,) = stack(here[1], mate(away[1]))
    below1 = send(lower, up)
    rows = [upper, lower]
    own = [direct, mate(direct), detoured, mate(detoured)]
    (across,) = hold((above,), across)
    around = send(across, down_odd)

    (buffer,) = hold((below0,), buffer)
    made, buffer = far(place, buffer, [below0], own, samples)
    top2 = send(made, down)
    across, buffer, next_detoured = choose(place, around, across, (buffer,))
    above, buffer, swapped = choose(place, relayed, above, (buffer,))
    next_relayed = send(swapped, swap)
    high = []
    for piece in split(next_direct, (made,), 2):
        high += [piece, mate(piece)]
    high += [next_detoured, mate(next_detoured)]
    made, buffer = far(place, buffer, [below0], high, samples)
    top3 = send(made, down)
    buffer = tile(place, buffer, 0, 0, rows, own[:2], samples)
    buffer = tile(place, buffer, 0, 3, rows, own[2:], samples)
    buffer = tile(place, buffer, 0, 2, rows, [relayed, mate(relayed)], samples)

    (buffer,) = hold((below1, top2), buffer)
    made, buffer = far(place, buffer, [below1], high + own, samples)
    bottom = send(made, down)
    low = []
    for piece in split(next_relayed, (made, top3), 2):
        low += [piece, mate(piece)]
    made, buffer = far(place, buffer, [below0, below1], low, samples)
    side = send(made, down)
    buffer = tile(place, buffer, 1, 0, rows, high[:-2], samples)
    buffer = tile(place, buffer, 1, 3, rows, high[-2:], samples)
    buffer = tile(place, buffer, 1, 2, rows, low, samples)
    buffer = tile(place, buffer, 2, 2, rows, [above, mate(above)], samples)
    buffer = last(place, buffer, top2, top3, bottom, side)
    return buffer[None]


def solution(mesh):
    in_specs = (P("samp", ("region", "var")), P("samp", ("region", "var")), P(("region", "var")))
    out_specs = P(("region", "var"), None, "samp", None)
    return jax.shard_map(
        per_device, mesh=mesh, in_specs=in_specs, out_specs=out_specs, check_vma=False
    )
```

```python
import functools

import jax
import jax.numpy as jnp
from jax import lax
from jax.experimental import pallas as pl
from jax.experimental.pallas import tpu as pltpu
from jax.sharding import PartitionSpec as P

WIN = 4
PIECES = (4, 2, 2)
ROWS = (1, 1)
PARTS = 2
BLOCKS = 8
STATS_VMEM = 50
epsilon = 1e-05

SMEM = pl.BlockSpec(memory_space=pltpu.SMEM)
VMEM = pl.BlockSpec(memory_space=pltpu.VMEM)
ANY = pl.BlockSpec(memory_space=pl.ANY)
PARAMS = pltpu.CompilerParams(vmem_limit_bytes=32 * 1024 * 1024)
COST = pl.CostEstimate(flops=1000, bytes_accessed=1000, transcendentals=0)


def stats_kernel(dosage_hbm, observed_hbm, sums_ref, masked_ref, dosage_ref, observed_ref, sems):
    samples, width = dosage_ref.shape
    block = samples // BLOCKS
    copies = []
    for n in range(BLOCKS):
        at = pl.ds(n * block, block)
        pair = [
            pltpu.make_async_copy(observed_hbm.at[at], observed_ref.at[at], sems.at[0, n]),
            pltpu.make_async_copy(dosage_hbm.at[at], dosage_ref.at[at], sems.at[1, n]),
        ]
        for copy in pair:
            copy.start()
        copies.append(pair)

    def fold(terms):
        return jnp.sum(terms.reshape(block // 8, 8, width), axis=0)

    totals = [jnp.zeros((8, width), jnp.float32)] * 3
    for n in range(BLOCKS):
        for copy in copies[n]:
            copy.wait()
        at = slice(n * block, (n + 1) * block)
        values = dosage_ref[at, :].astype(jnp.float32)
        present = observed_ref[at, :] > 0
        kept = jnp.where(present, values, 0.0)
        masked_ref[at, :] = jnp.where(present, values, -1.0).astype(masked_ref.dtype)
        terms = [jnp.where(present, 1.0, 0.0), kept, kept * kept]
        totals = [total + fold(term) for total, term in zip(totals, terms)]
    for n in range(3):
        sums_ref[n : n + 1, :] = jnp.sum(totals[n], axis=0, keepdims=True)
    sums_ref[3:, :] = jnp.zeros((5, width), jnp.float32)


def stats(dosage, observed):
    samples, width = dosage.shape
    return pl.pallas_call(
        stats_kernel,
        in_specs=[pl.BlockSpec(memory_space=pltpu.HBM)] * 2,
        out_specs=[VMEM, VMEM],
        out_shape=[
            jax.ShapeDtypeStruct((8, width), jnp.float32),
            jax.ShapeDtypeStruct((samples, width), jnp.bfloat16),
        ],
        scratch_shapes=[
            pltpu.VMEM(dosage.shape, dosage.dtype),
            pltpu.VMEM(observed.shape, observed.dtype),
            pltpu.SemaphoreType.DMA((2, BLOCKS)),
        ],
        compiler_params=pltpu.CompilerParams(vmem_limit_bytes=STATS_VMEM * 1024 * 1024),
        cost_estimate=COST,
    )(dosage, observed)


def score_kernel(place_ref, masked_ref, sums_ref, sums_other_ref, *outs):
    pieces, again_ref = outs[: len(PIECES)], outs[len(PIECES)]
    rows_here, rows_away = outs[len(PIECES) + 1 : -PARTS], outs[-PARTS:]
    core = place_ref[1]
    size = masked_ref.shape[1] // 4
    starts = [sum(piece.shape[1] for piece in pieces[:n]) for n in range(len(pieces))]
    for step in range(4):
        columns = slice(step * size, (step + 1) * size)
        totals = [
            sums_ref[n : n + 1, columns] + sums_other_ref[n : n + 1, columns]
            for n in range(3)
        ]
        count = jnp.maximum(totals[0], 1.0)
        center = totals[1] / count
        spread = totals[2] / count - center * center
        factor = lax.rsqrt(spread + epsilon)
        masked = masked_ref[:, columns].astype(jnp.float32)
        scored = jnp.where(masked >= 0.0, (masked - center) * factor, 0.0)
        scored = scored.astype(jnp.bfloat16)
        for at, piece in zip((*starts, 0), (*pieces, again_ref)):
            low, high = max(step * size, at), min(step * size + size, at + piece.shape[1])
            if low < high:
                piece[:, low - at : high - at] = scored[:, low - step * size : high - step * size]
        turned = scored.T

        def put(parts, turned=turned, begin=step % 2 * size):
            at = 0
            for part in parts:
                low, high = max(begin, at), min(begin + size, at + part.shape[0])
                if low < high:
                    part[low - at : high - at, :] = turned[low - begin : high - begin, :]
                at += part.shape[0]

        here = core == step // 2
        pl.when(here)(functools.partial(put, rows_here))
        pl.when(jnp.logical_not(here))(functools.partial(put, rows_away))


def score(place, masked, sums, sums_other):
    samples, width = masked.shape
    return pl.pallas_call(
        score_kernel,
        in_specs=[SMEM, VMEM, VMEM, VMEM],
        out_specs=[VMEM] * (len(PIECES) + 1 + 2 * PARTS),
        out_shape=[
            jax.ShapeDtypeStruct((samples, width * eighths // 8), jnp.bfloat16) for eighths in (*PIECES, PIECES[0])
        ]
        + [
            jax.ShapeDtypeStruct((width // 2 * share // sum(ROWS), samples), jnp.bfloat16)
            for share in ROWS + ROWS
        ],
        compiler_params=PARAMS,
        cost_estimate=COST,
    )(place, masked, sums, sums_other)


def stack(here, arrived, passed=(), unset=()):
    count, samples = here.shape

    def kernel(here_ref, arrived_ref, *refs):
        out_ref = refs[len(passed)]
        out_ref[0:count, :] = here_ref[...]
        out_ref[count:, :] = arrived_ref[...]

    return pl.pallas_call(
        kernel,
        in_specs=[VMEM, VMEM] + [ANY] * len(passed),
        out_specs=[VMEM] + [ANY] * (len(passed) + len(unset)),
        out_shape=[jax.ShapeDtypeStruct((2 * count, samples), here.dtype)]
        + [jax.ShapeDtypeStruct(x.shape, x.dtype) for x in (*passed, *unset)],
        input_output_aliases={2 + n: 1 + n for n in range(len(passed))},
        compiler_params=PARAMS,
        cost_estimate=COST,
    )(here, arrived, *passed)


def chunks(rights):
    pairs = list(zip(rights[::2], rights[1::2]))
    while pairs:
        group = [pairs.pop(0)]
        while pairs and sum(mine.shape[1] for mine, _ in group) + pairs[0][0].shape[1] <= 256:
            group.append(pairs.pop(0))
        if len(group) > 1:
            yield tuple(jnp.concatenate([ref[...] for ref in side], axis=1) for side in zip(*group))
            continue
        mine, other = group[0]
        for begin in range(0, mine.shape[1], 256):
            yield mine[:, begin : begin + 256], other[:, begin : begin + 256]


def blocks(rows, rights, scale):
    left = 0
    for mine, other in chunks(rights):
        width, top = mine.shape[1], 0
        for row in rows:
            part = row.shape[0] // 2
            total = jnp.dot(row[0:part, :], mine, preferred_element_type=jnp.float32)
            total += jnp.dot(row[part:, :], other, preferred_element_type=jnp.float32)
            yield slice(top, top + part), slice(left, left + width), total * scale
            top += part
        left += width


def tile_kernel(k, parts, pieces, scale, place_ref, *refs):
    out_ref = refs[-1]
    keep = k < place_ref[2]
    for at, columns, block in blocks(refs[:parts], refs[parts : parts + pieces], scale):
        out_ref[0, at, columns] = jnp.where(keep, block, 0.0).astype(out_ref.dtype)


def tile(place, buffer, k, column, rows, rights, samples, after=()):
    count = sum(row.shape[0] for row in rows) // 2
    wide = sum(right.shape[1] for right in rights) // 2
    operands = [place, *rows, *rights, *after, buffer]
    return pl.pallas_call(
        functools.partial(tile_kernel, k, len(rows), len(rights), 1.0 / samples),
        grid=(1,),
        in_specs=[SMEM] + [VMEM] * (len(rows) + len(rights)) + [ANY] * (1 + len(after)),
        out_specs=pl.BlockSpec((1, count, wide), lambda i: (k, 0, column)),
        out_shape=jax.ShapeDtypeStruct(buffer.shape, buffer.dtype),
        input_output_aliases={len(operands) - 1: 0},
        compiler_params=PARAMS,
        cost_estimate=COST,
    )(*operands)


def far_kernel(scale, parts, pieces, place_ref, *refs):
    out_ref = refs[-2]
    for at, columns, block in blocks(refs[:parts], refs[parts : parts + pieces], scale):
        out_ref[at, columns] = block.astype(out_ref.dtype)


def far(place, buffer, rows, rights, samples):
    shape = (sum(row.shape[0] for row in rows) // 2, sum(right.shape[1] for right in rights) // 2)
    operands = [place, *rows, *rights, buffer]
    return pl.pallas_call(
        functools.partial(far_kernel, 1.0 / samples, len(rows), len(rights)),
        in_specs=[SMEM] + [VMEM] * (len(rows) + len(rights)) + [ANY],
        out_specs=[VMEM, ANY],
        out_shape=[
            jax.ShapeDtypeStruct(shape, jnp.bfloat16),
            jax.ShapeDtypeStruct(buffer.shape, buffer.dtype),
        ],
        input_output_aliases={len(operands) - 1: 1},
        compiler_params=PARAMS,
        cost_estimate=COST,
    )(*operands)


def choose_kernel(place_ref, odd_ref, even_ref, *refs):
    out_ref = refs[-1]

    @pl.when(place_ref[0] == 1)
    def _():
        out_ref[...] = odd_ref[...]

    @pl.when(place_ref[0] == 0)
    def _():
        out_ref[...] = even_ref[...]


def choose(place, if_odd, if_even, passed=(), after=()):
    operands = [if_even, *passed]
    return pl.pallas_call(
        choose_kernel,
        in_specs=[SMEM, VMEM, VMEM] + [ANY] * (len(passed) + len(after)),
        out_specs=[VMEM] + [ANY] * len(passed) + [VMEM],
        out_shape=[jax.ShapeDtypeStruct(x.shape, x.dtype) for x in (*operands, if_odd)],
        input_output_aliases={2 + n: n for n in range(len(operands))},
        compiler_params=PARAMS,
        cost_estimate=COST,
    )(place, if_odd, *operands, *after)


def hold(after, *passed):
    def kernel(*refs):
        pass

    return pl.pallas_call(
        kernel,
        in_specs=[ANY] * (len(after) + len(passed)),
        out_specs=[ANY] * len(passed),
        out_shape=[jax.ShapeDtypeStruct(x.shape, x.dtype) for x in passed],
        input_output_aliases={len(after) + n: n for n in range(len(passed))},
        compiler_params=PARAMS,
        cost_estimate=COST,
    )(*after, *passed)


def split_kernel(count, whole_ref, *refs):
    outs = refs[-count:]
    begin = 0
    for out in outs:
        out[...] = whole_ref[:, begin : begin + out.shape[1]]
        begin += out.shape[1]


def split(piece, after, count):
    samples, width = piece.shape
    return pl.pallas_call(
        functools.partial(split_kernel, count),
        in_specs=[VMEM] + [ANY] * len(after),
        out_specs=[VMEM] * count,
        out_shape=[jax.ShapeDtypeStruct((samples, width // count), piece.dtype)] * count,
        compiler_params=PARAMS,
        cost_estimate=COST,
    )(piece, *after)


def last_kernel(place_ref, top2, top3, bottom, side, out_ref, two, three, sems):
    keep2, keep3 = 2 < place_ref[2], 3 < place_ref[2]
    part, wide = top2.shape
    first, after = wide - wide * PIECES[2] // (PIECES[0] + PIECES[2]), side.shape[1]

    def kept(keep, block):
        return jnp.where(keep, block, 0.0).astype(out_ref.dtype)

    two[0:part, 0:wide] = kept(keep2, top2[...])
    two[part:, 0:wide] = kept(keep2, bottom[:, wide:])
    copies = [
        pltpu.make_async_copy(two.at[:, 0:first], out_ref.at[2, :, 0:first], sems.at[0]),
        pltpu.make_async_copy(two.at[:, first:], out_ref.at[2, :, first + after :], sems.at[1]),
        pltpu.make_async_copy(three, out_ref.at[3], sems.at[2]),
    ]
    copies[0].start()
    copies[1].start()
    for at, columns in ((0, slice(0, first)), (first, slice(first + after, None))):
        received = slice(at, first if at == 0 else wide)
        three[0:part, columns] = kept(keep3, top3[:, received])
        three[part:, columns] = kept(keep3, bottom[:, received])
    three[:, first : first + after] = kept(keep3, side[...])
    copies[2].start()
    for copy in copies:
        copy.wait()


def last(place, buffer, top2, top3, bottom, side):
    operands = [place, top2, top3, bottom, side, buffer]
    count, width = buffer.shape[1:]

    def kernel(*refs):
        n = len(operands)
        last_kernel(*refs[: n - 1], *refs[n:])

    return pl.pallas_call(
        kernel,
        in_specs=[SMEM] + [VMEM] * (len(operands) - 2) + [ANY],
        out_specs=ANY,
        out_shape=jax.ShapeDtypeStruct(buffer.shape, buffer.dtype),
        scratch_shapes=[
            pltpu.VMEM((count, top2.shape[1]), buffer.dtype),
            pltpu.VMEM((count, width), buffer.dtype),
            pltpu.SemaphoreType.DMA((3,)),
        ],
        input_output_aliases={len(operands) - 1: 0},
        compiler_params=PARAMS,
        cost_estimate=COST,
    )(*operands)


def per_device(dosage, observed, counts):
    places = lax.axis_size("var")
    samples = dosage.shape[0] * lax.axis_size("samp")
    width = dosage.shape[1]
    place = jnp.stack(
        [
            (lax.axis_index("var") % 2).astype(jnp.int32),
            lax.axis_index("samp").astype(jnp.int32),
            counts[0],
        ]
    )

    def send(shard, pairs):
        return lax.ppermute(shard, "var", pairs)

    before = [(i + 1, i) for i in range(places - 1)]
    up = [(i, i + 2) for i in range(places - 2)]
    down = [(i + 2, i) for i in range(places - 2)]
    down_odd = [pair for pair in down if pair[0] % 2 == 1]
    to_even = [(i + 1, i) for i in range(0, places - 1, 2)]
    swap = to_even + [(i, i + 1) for i in range(0, places - 1, 2)]

    def mate(shard):
        return lax.ppermute(shard, "samp", [(0, 1), (1, 0)])

    sums, masked = stats(dosage, observed)
    made = score(place, masked, sums, mate(sums))
    direct, relayed, detoured, sent = made[:4]
    here, away = made[4:-PARTS], made[-PARTS:]
    unset = jax.ShapeDtypeStruct((WIN, width // 2, width), jnp.bfloat16)

    upper, buffer = stack(here[0], mate(away[0]), (), (unset,))
    below0 = send(upper, up)
    above = send(relayed, down)
    across = send(detoured, swap)
    (sent,) = hold((across,), sent)
    next_direct = send(sent, before)
    (lower,) = stack(here[1], mate(away[1]))
    below1 = send(lower, up)
    rows = [upper, lower]
    own = [direct, mate(direct), detoured, mate(detoured)]
    (across,) = hold((above,), across)
    around = send(across, down_odd)

    buffer = tile(place, buffer, 0, 0, rows, own[:2], samples)
    buffer = tile(place, buffer, 0, 3, rows, own[2:], samples)
    (buffer,) = hold((below0,), buffer)
    made, buffer = far(place, buffer, [below0], own, samples)
    top2 = send(made, down)
    across, buffer, next_detoured = choose(place, around, across, (buffer,))
    above, buffer, swapped = choose(place, relayed, above, (buffer,))
    next_relayed = send(swapped, swap)
    high = []
    for piece in split(next_direct, (made,), 2):
        high += [piece, mate(piece)]
    high += [next_detoured, mate(next_detoured)]
    made, buffer = far(place, buffer, [below0], high, samples)
    top3 = send(made, down)

    (buffer,) = hold((below1, top2), buffer)
    made, buffer = far(place, buffer, [below1], high + own, samples)
    bottom = send(made, down)
    low = []
    for piece in split(next_relayed, (made, top3), 2):
        low += [piece, mate(piece)]
    made, buffer = far(place, buffer, [below0, below1], low, samples)
    side = send(made, down)
    buffer = tile(place, buffer, 1, 0, rows, high[:-2], samples)
    buffer = tile(place, buffer, 1, 3, rows, high[-2:], samples)
    buffer = tile(place, buffer, 0, 2, rows, [relayed, mate(relayed)], samples)
    buffer = tile(place, buffer, 1, 2, rows, low, samples)
    buffer = tile(place, buffer, 2, 2, rows, [above, mate(above)], samples)
    buffer = last(place, buffer, top2, top3, bottom, side)
    return buffer[None]


def solution(mesh):
    in_specs = (P("samp", ("region", "var")), P("samp", ("region", "var")), P(("region", "var")))
    out_specs = P(("region", "var"), None, "samp", None)
    return jax.shard_map(
        per_device, mesh=mesh, in_specs=in_specs, out_specs=out_specs, check_vma=False
    )
```

```python
import functools

import jax
import jax.numpy as jnp
from jax import lax
from jax.experimental import pallas as pl
from jax.experimental.pallas import tpu as pltpu
from jax.sharding import PartitionSpec as P

WIN = 4
PIECES = (4, 2, 2)
ROWS = (1, 1)
PARTS = 2
BLOCKS = 8
STATS_VMEM = 50
epsilon = 1e-05

SMEM = pl.BlockSpec(memory_space=pltpu.SMEM)
VMEM = pl.BlockSpec(memory_space=pltpu.VMEM)
ANY = pl.BlockSpec(memory_space=pl.ANY)
PARAMS = pltpu.CompilerParams(vmem_limit_bytes=32 * 1024 * 1024)
COST = pl.CostEstimate(flops=1000, bytes_accessed=1000, transcendentals=0)


def stats_kernel(dosage_hbm, observed_hbm, sums_ref, masked_ref, dosage_ref, observed_ref, sems):
    samples, width = dosage_ref.shape
    block = samples // BLOCKS
    copies = []
    for n in range(BLOCKS):
        at = pl.ds(n * block, block)
        pair = [
            pltpu.make_async_copy(observed_hbm.at[at], observed_ref.at[at], sems.at[0, n]),
            pltpu.make_async_copy(dosage_hbm.at[at], dosage_ref.at[at], sems.at[1, n]),
        ]
        for copy in pair:
            copy.start()
        copies.append(pair)

    def fold(terms):
        return jnp.sum(terms.reshape(block // 8, 8, width), axis=0)

    totals = [jnp.zeros((8, width), jnp.float32)] * 3
    for n in range(BLOCKS):
        for copy in copies[n]:
            copy.wait()
        at = slice(n * block, (n + 1) * block)
        values = dosage_ref[at, :].astype(jnp.float32)
        present = observed_ref[at, :] > 0
        kept = jnp.where(present, values, 0.0)
        masked_ref[at, :] = jnp.where(present, values, -1.0).astype(masked_ref.dtype)
        terms = [jnp.where(present, 1.0, 0.0), kept, kept * kept]
        totals = [total + fold(term) for total, term in zip(totals, terms)]
    for n in range(3):
        sums_ref[n : n + 1, :] = jnp.sum(totals[n], axis=0, keepdims=True)
    sums_ref[3:, :] = jnp.zeros((5, width), jnp.float32)


def stats(dosage, observed):
    samples, width = dosage.shape
    return pl.pallas_call(
        stats_kernel,
        in_specs=[pl.BlockSpec(memory_space=pltpu.HBM)] * 2,
        out_specs=[VMEM, VMEM],
        out_shape=[
            jax.ShapeDtypeStruct((8, width), jnp.float32),
            jax.ShapeDtypeStruct((samples, width), jnp.bfloat16),
        ],
        scratch_shapes=[
            pltpu.VMEM(dosage.shape, dosage.dtype),
            pltpu.VMEM(observed.shape, observed.dtype),
            pltpu.SemaphoreType.DMA((2, BLOCKS)),
        ],
        compiler_params=pltpu.CompilerParams(vmem_limit_bytes=STATS_VMEM * 1024 * 1024),
        cost_estimate=COST,
    )(dosage, observed)


def score_kernel(place_ref, masked_ref, sums_ref, sums_other_ref, *outs):
    pieces, again_ref = outs[: len(PIECES)], outs[len(PIECES)]
    rows_here, rows_away = outs[len(PIECES) + 1 : -PARTS], outs[-PARTS:]
    core = place_ref[1]
    size = masked_ref.shape[1] // 4
    starts = [sum(piece.shape[1] for piece in pieces[:n]) for n in range(len(pieces))]
    for step in range(4):
        columns = slice(step * size, (step + 1) * size)
        totals = [
            sums_ref[n : n + 1, columns] + sums_other_ref[n : n + 1, columns]
            for n in range(3)
        ]
        count = jnp.maximum(totals[0], 1.0)
        center = totals[1] / count
        spread = totals[2] / count - center * center
        factor = lax.rsqrt(spread + epsilon)
        masked = masked_ref[:, columns].astype(jnp.float32)
        scored = jnp.where(masked >= 0.0, (masked - center) * factor, 0.0)
        scored = scored.astype(jnp.bfloat16)
        for at, piece in zip((*starts, 0), (*pieces, again_ref)):
            low, high = max(step * size, at), min(step * size + size, at + piece.shape[1])
            if low < high:
                piece[:, low - at : high - at] = scored[:, low - step * size : high - step * size]
        turned = scored.T

        def put(parts, turned=turned, begin=step % 2 * size):
            at = 0
            for part in parts:
                low, high = max(begin, at), min(begin + size, at + part.shape[0])
                if low < high:
                    part[low - at : high - at, :] = turned[low - begin : high - begin, :]
                at += part.shape[0]

        here = core == step // 2
        pl.when(here)(functools.partial(put, rows_here))
        pl.when(jnp.logical_not(here))(functools.partial(put, rows_away))


def score(place, masked, sums, sums_other):
    samples, width = masked.shape
    return pl.pallas_call(
        score_kernel,
        in_specs=[SMEM, VMEM, VMEM, VMEM],
        out_specs=[VMEM] * (len(PIECES) + 1 + 2 * PARTS),
        out_shape=[
            jax.ShapeDtypeStruct((samples, width * eighths // 8), jnp.bfloat16) for eighths in (*PIECES, PIECES[0])
        ]
        + [
            jax.ShapeDtypeStruct((width // 2 * share // sum(ROWS), samples), jnp.bfloat16)
            for share in ROWS + ROWS
        ],
        compiler_params=PARAMS,
        cost_estimate=COST,
    )(place, masked, sums, sums_other)


def stack(here, arrived, passed=(), unset=()):
    count, samples = here.shape

    def kernel(here_ref, arrived_ref, *refs):
        out_ref = refs[len(passed)]
        out_ref[0:count, :] = here_ref[...]
        out_ref[count:, :] = arrived_ref[...]

    return pl.pallas_call(
        kernel,
        in_specs=[VMEM, VMEM] + [ANY] * len(passed),
        out_specs=[VMEM] + [ANY] * (len(passed) + len(unset)),
        out_shape=[jax.ShapeDtypeStruct((2 * count, samples), here.dtype)]
        + [jax.ShapeDtypeStruct(x.shape, x.dtype) for x in (*passed, *unset)],
        input_output_aliases={2 + n: 1 + n for n in range(len(passed))},
        compiler_params=PARAMS,
        cost_estimate=COST,
    )(here, arrived, *passed)


def chunks(rights):
    pairs = list(zip(rights[::2], rights[1::2]))
    while pairs:
        group = [pairs.pop(0)]
        while pairs and sum(mine.shape[1] for mine, _ in group) + pairs[0][0].shape[1] <= 256:
            group.append(pairs.pop(0))
        if len(group) > 1:
            yield tuple(jnp.concatenate([ref[...] for ref in side], axis=1) for side in zip(*group))
            continue
        mine, other = group[0]
        for begin in range(0, mine.shape[1], 256):
            yield mine[:, begin : begin + 256], other[:, begin : begin + 256]


def blocks(rows, rights, scale):
    left = 0
    for mine, other in chunks(rights):
        width, top = mine.shape[1], 0
        for row in rows:
            part = row.shape[0] // 2
            total = jnp.dot(row[0:part, :], mine, preferred_element_type=jnp.float32)
            total += jnp.dot(row[part:, :], other, preferred_element_type=jnp.float32)
            yield slice(top, top + part), slice(left, left + width), total * scale
            top += part
        left += width


def tile_kernel(k, parts, pieces, scale, place_ref, *refs):
    out_ref = refs[-1]
    keep = k < place_ref[2]
    for at, columns, block in blocks(refs[:parts], refs[parts : parts + pieces], scale):
        out_ref[0, at, columns] = jnp.where(keep, block, 0.0).astype(out_ref.dtype)


def tile(place, buffer, k, column, rows, rights, samples, after=()):
    count = sum(row.shape[0] for row in rows) // 2
    wide = sum(right.shape[1] for right in rights) // 2
    operands = [place, *rows, *rights, *after, buffer]
    return pl.pallas_call(
        functools.partial(tile_kernel, k, len(rows), len(rights), 1.0 / samples),
        grid=(1,),
        in_specs=[SMEM] + [VMEM] * (len(rows) + len(rights)) + [ANY] * (1 + len(after)),
        out_specs=pl.BlockSpec((1, count, wide), lambda i: (k, 0, column)),
        out_shape=jax.ShapeDtypeStruct(buffer.shape, buffer.dtype),
        input_output_aliases={len(operands) - 1: 0},
        compiler_params=PARAMS,
        cost_estimate=COST,
    )(*operands)


def far_kernel(scale, parts, pieces, place_ref, *refs):
    out_ref = refs[-2]
    for at, columns, block in blocks(refs[:parts], refs[parts : parts + pieces], scale):
        out_ref[at, columns] = block.astype(out_ref.dtype)


def far(place, buffer, rows, rights, samples):
    shape = (sum(row.shape[0] for row in rows) // 2, sum(right.shape[1] for right in rights) // 2)
    operands = [place, *rows, *rights, buffer]
    return pl.pallas_call(
        functools.partial(far_kernel, 1.0 / samples, len(rows), len(rights)),
        in_specs=[SMEM] + [VMEM] * (len(rows) + len(rights)) + [ANY],
        out_specs=[VMEM, ANY],
        out_shape=[
            jax.ShapeDtypeStruct(shape, jnp.bfloat16),
            jax.ShapeDtypeStruct(buffer.shape, buffer.dtype),
        ],
        input_output_aliases={len(operands) - 1: 1},
        compiler_params=PARAMS,
        cost_estimate=COST,
    )(*operands)


def choose_kernel(place_ref, odd_ref, even_ref, *refs):
    out_ref = refs[-1]

    @pl.when(place_ref[0] == 1)
    def _():
        out_ref[...] = odd_ref[...]

    @pl.when(place_ref[0] == 0)
    def _():
        out_ref[...] = even_ref[...]


def choose(place, if_odd, if_even, passed=(), after=()):
    operands = [if_even, *passed]
    return pl.pallas_call(
        choose_kernel,
        in_specs=[SMEM, VMEM, VMEM] + [ANY] * (len(passed) + len(after)),
        out_specs=[VMEM] + [ANY] * len(passed) + [VMEM],
        out_shape=[jax.ShapeDtypeStruct(x.shape, x.dtype) for x in (*operands, if_odd)],
        input_output_aliases={2 + n: n for n in range(len(operands))},
        compiler_params=PARAMS,
        cost_estimate=COST,
    )(place, if_odd, *operands, *after)


def hold(after, *passed):
    def kernel(*refs):
        pass

    return pl.pallas_call(
        kernel,
        in_specs=[ANY] * (len(after) + len(passed)),
        out_specs=[ANY] * len(passed),
        out_shape=[jax.ShapeDtypeStruct(x.shape, x.dtype) for x in passed],
        input_output_aliases={len(after) + n: n for n in range(len(passed))},
        compiler_params=PARAMS,
        cost_estimate=COST,
    )(*after, *passed)


def split_kernel(count, whole_ref, *refs):
    outs = refs[-count:]
    begin = 0
    for out in outs:
        out[...] = whole_ref[:, begin : begin + out.shape[1]]
        begin += out.shape[1]


def split(piece, after, count):
    samples, width = piece.shape
    return pl.pallas_call(
        functools.partial(split_kernel, count),
        in_specs=[VMEM] + [ANY] * len(after),
        out_specs=[VMEM] * count,
        out_shape=[jax.ShapeDtypeStruct((samples, width // count), piece.dtype)] * count,
        compiler_params=PARAMS,
        cost_estimate=COST,
    )(piece, *after)


def last_kernel(place_ref, top2, top3, bottom, side, out_ref, two, three, sems):
    keep2, keep3 = 2 < place_ref[2], 3 < place_ref[2]
    part, wide = top2.shape
    first, after = wide - wide * PIECES[2] // (PIECES[0] + PIECES[2]), side.shape[1]

    def kept(keep, block):
        return jnp.where(keep, block, 0.0).astype(out_ref.dtype)

    two[0:part, 0:wide] = kept(keep2, top2[...])
    two[part:, 0:wide] = kept(keep2, bottom[:, wide:])
    copies = [
        pltpu.make_async_copy(two.at[:, 0:first], out_ref.at[2, :, 0:first], sems.at[0]),
        pltpu.make_async_copy(two.at[:, first:], out_ref.at[2, :, first + after :], sems.at[1]),
        pltpu.make_async_copy(three, out_ref.at[3], sems.at[2]),
    ]
    copies[0].start()
    copies[1].start()
    for at, columns in ((0, slice(0, first)), (first, slice(first + after, None))):
        received = slice(at, first if at == 0 else wide)
        three[0:part, columns] = kept(keep3, top3[:, received])
        three[part:, columns] = kept(keep3, bottom[:, received])
    three[:, first : first + after] = kept(keep3, side[...])
    copies[2].start()
    for copy in copies:
        copy.wait()


def last(place, buffer, top2, top3, bottom, side):
    operands = [place, top2, top3, bottom, side, buffer]
    count, width = buffer.shape[1:]

    def kernel(*refs):
        n = len(operands)
        last_kernel(*refs[: n - 1], *refs[n:])

    return pl.pallas_call(
        kernel,
        in_specs=[SMEM] + [VMEM] * (len(operands) - 2) + [ANY],
        out_specs=ANY,
        out_shape=jax.ShapeDtypeStruct(buffer.shape, buffer.dtype),
        scratch_shapes=[
            pltpu.VMEM((count, top2.shape[1]), buffer.dtype),
            pltpu.VMEM((count, width), buffer.dtype),
            pltpu.SemaphoreType.DMA((3,)),
        ],
        input_output_aliases={len(operands) - 1: 0},
        compiler_params=PARAMS,
        cost_estimate=COST,
    )(*operands)


def per_device(dosage, observed, counts):
    places = lax.axis_size("var")
    samples = dosage.shape[0] * lax.axis_size("samp")
    width = dosage.shape[1]
    place = jnp.stack(
        [
            (lax.axis_index("var") % 2).astype(jnp.int32),
            lax.axis_index("samp").astype(jnp.int32),
            counts[0],
        ]
    )

    def send(shard, pairs):
        return lax.ppermute(shard, "var", pairs)

    before = [(i + 1, i) for i in range(places - 1)]
    up = [(i, i + 2) for i in range(places - 2)]
    down = [(i + 2, i) for i in range(places - 2)]
    down_odd = [pair for pair in down if pair[0] % 2 == 1]
    to_even = [(i + 1, i) for i in range(0, places - 1, 2)]
    swap = to_even + [(i, i + 1) for i in range(0, places - 1, 2)]

    def mate(shard):
        return lax.ppermute(shard, "samp", [(0, 1), (1, 0)])

    sums, masked = stats(dosage, observed)
    made = score(place, masked, sums, mate(sums))
    direct, relayed, detoured, sent = made[:4]
    here, away = made[4:-PARTS], made[-PARTS:]
    unset = jax.ShapeDtypeStruct((WIN, width // 2, width), jnp.bfloat16)

    upper, buffer = stack(here[0], mate(away[0]), (), (unset,))
    below0 = send(upper, up)
    above = send(relayed, down)
    across = send(detoured, swap)
    next_direct = send(sent, before)
    (lower,) = stack(here[1], mate(away[1]))
    below1 = send(lower, up)
    rows = [upper, lower]
    own = [direct, mate(direct), detoured, mate(detoured)]
    (across,) = hold((above,), across)
    around = send(across, down_odd)

    buffer = tile(place, buffer, 0, 0, rows, own[:2], samples)
    buffer = tile(place, buffer, 0, 3, rows, own[2:], samples)
    (buffer,) = hold((below0,), buffer)
    made, buffer = far(place, buffer, [below0], own, samples)
    top2 = send(made, down)
    across, buffer, next_detoured = choose(place, around, across, (buffer,))
    above, buffer, swapped = choose(place, relayed, above, (buffer,))
    next_relayed = send(swapped, swap)
    high = []
    for piece in split(next_direct, (made,), 2):
        high += [piece, mate(piece)]
    high += [next_detoured, mate(next_detoured)]
    made, buffer = far(place, buffer, [below0], high, samples)
    top3 = send(made, down)

    (buffer,) = hold((below1, top2), buffer)
    made, buffer = far(place, buffer, [below1], high + own, samples)
    bottom = send(made, down)
    low = []
    for piece in split(next_relayed, (made, top3), 2):
        low += [piece, mate(piece)]
    made, buffer = far(place, buffer, [below0, below1], low, samples)
    side = send(made, down)
    buffer = tile(place, buffer, 1, 0, rows, high[:-2], samples)
    buffer = tile(place, buffer, 1, 3, rows, high[-2:], samples)
    buffer = tile(place, buffer, 0, 2, rows, [relayed, mate(relayed)], samples)
    buffer = tile(place, buffer, 1, 2, rows, low, samples)
    buffer = tile(place, buffer, 2, 2, rows, [above, mate(above)], samples)
    buffer = last(place, buffer, top2, top3, bottom, side)
    return buffer[None]


def solution(mesh):
    in_specs = (P("samp", ("region", "var")), P("samp", ("region", "var")), P(("region", "var")))
    out_specs = P(("region", "var"), None, "samp", None)
    return jax.shard_map(
        per_device, mesh=mesh, in_specs=in_specs, out_specs=out_specs, check_vma=False
    )
```

```python
import functools

import jax
import jax.numpy as jnp
from jax import lax
from jax.experimental import pallas as pl
from jax.experimental.pallas import tpu as pltpu
from jax.sharding import PartitionSpec as P

WIN = 4
PIECES = (4, 2, 2)
ROWS = (1, 1)
PARTS = 2
BLOCKS = 16
STATS_VMEM = 50
epsilon = 1e-05

SMEM = pl.BlockSpec(memory_space=pltpu.SMEM)
VMEM = pl.BlockSpec(memory_space=pltpu.VMEM)
ANY = pl.BlockSpec(memory_space=pl.ANY)
PARAMS = pltpu.CompilerParams(vmem_limit_bytes=32 * 1024 * 1024)
COST = pl.CostEstimate(flops=1000, bytes_accessed=1000, transcendentals=0)


def stats_kernel(dosage_hbm, observed_hbm, sums_ref, masked_ref, dosage_ref, observed_ref, sems):
    samples, width = dosage_ref.shape
    block = samples // BLOCKS
    copies = []
    for n in range(BLOCKS):
        at = pl.ds(n * block, block)
        pair = [
            pltpu.make_async_copy(observed_hbm.at[at], observed_ref.at[at], sems.at[0, n]),
            pltpu.make_async_copy(dosage_hbm.at[at], dosage_ref.at[at], sems.at[1, n]),
        ]
        for copy in pair:
            copy.start()
        copies.append(pair)

    def fold(terms):
        return jnp.sum(terms.reshape(block // 8, 8, width), axis=0)

    totals = [jnp.zeros((8, width), jnp.float32)] * 3
    for n in range(BLOCKS):
        for copy in copies[n]:
            copy.wait()
        at = slice(n * block, (n + 1) * block)
        values = dosage_ref[at, :].astype(jnp.float32)
        present = observed_ref[at, :] > 0
        kept = jnp.where(present, values, 0.0)
        masked_ref[at, :] = jnp.where(present, values, -1.0).astype(masked_ref.dtype)
        terms = [jnp.where(present, 1.0, 0.0), kept, kept * kept]
        totals = [total + fold(term) for total, term in zip(totals, terms)]
    for n in range(3):
        sums_ref[n : n + 1, :] = jnp.sum(totals[n], axis=0, keepdims=True)
    sums_ref[3:, :] = jnp.zeros((5, width), jnp.float32)


def stats(dosage, observed):
    samples, width = dosage.shape
    return pl.pallas_call(
        stats_kernel,
        in_specs=[pl.BlockSpec(memory_space=pltpu.HBM)] * 2,
        out_specs=[VMEM, VMEM],
        out_shape=[
            jax.ShapeDtypeStruct((8, width), jnp.float32),
            jax.ShapeDtypeStruct((samples, width), jnp.bfloat16),
        ],
        scratch_shapes=[
            pltpu.VMEM(dosage.shape, dosage.dtype),
            pltpu.VMEM(observed.shape, observed.dtype),
            pltpu.SemaphoreType.DMA((2, BLOCKS)),
        ],
        compiler_params=pltpu.CompilerParams(vmem_limit_bytes=STATS_VMEM * 1024 * 1024),
        cost_estimate=COST,
    )(dosage, observed)


def score_kernel(place_ref, masked_ref, sums_ref, sums_other_ref, *outs):
    pieces, again_ref = outs[: len(PIECES)], outs[len(PIECES)]
    rows_here, rows_away = outs[len(PIECES) + 1 : -PARTS], outs[-PARTS:]
    core = place_ref[1]
    size = masked_ref.shape[1] // 4
    starts = [sum(piece.shape[1] for piece in pieces[:n]) for n in range(len(pieces))]
    for step in range(4):
        columns = slice(step * size, (step + 1) * size)
        totals = [
            sums_ref[n : n + 1, columns] + sums_other_ref[n : n + 1, columns]
            for n in range(3)
        ]
        count = jnp.maximum(totals[0], 1.0)
        center = totals[1] / count
        spread = totals[2] / count - center * center
        factor = lax.rsqrt(spread + epsilon)
        masked = masked_ref[:, columns].astype(jnp.float32)
        scored = jnp.where(masked >= 0.0, (masked - center) * factor, 0.0)
        scored = scored.astype(jnp.bfloat16)
        for at, piece in zip((*starts, 0), (*pieces, again_ref)):
            low, high = max(step * size, at), min(step * size + size, at + piece.shape[1])
            if low < high:
                piece[:, low - at : high - at] = scored[:, low - step * size : high - step * size]
        turned = scored.T

        def put(parts, turned=turned, begin=step % 2 * size):
            at = 0
            for part in parts:
                low, high = max(begin, at), min(begin + size, at + part.shape[0])
                if low < high:
                    part[low - at : high - at, :] = turned[low - begin : high - begin, :]
                at += part.shape[0]

        here = core == step // 2
        pl.when(here)(functools.partial(put, rows_here))
        pl.when(jnp.logical_not(here))(functools.partial(put, rows_away))


def score(place, masked, sums, sums_other):
    samples, width = masked.shape
    return pl.pallas_call(
        score_kernel,
        in_specs=[SMEM, VMEM, VMEM, VMEM],
        out_specs=[VMEM] * (len(PIECES) + 1 + 2 * PARTS),
        out_shape=[
            jax.ShapeDtypeStruct((samples, width * eighths // 8), jnp.bfloat16) for eighths in (*PIECES, PIECES[0])
        ]
        + [
            jax.ShapeDtypeStruct((width // 2 * share // sum(ROWS), samples), jnp.bfloat16)
            for share in ROWS + ROWS
        ],
        compiler_params=PARAMS,
        cost_estimate=COST,
    )(place, masked, sums, sums_other)


def stack(here, arrived, passed=(), unset=()):
    count, samples = here.shape

    def kernel(here_ref, arrived_ref, *refs):
        out_ref = refs[len(passed)]
        out_ref[0:count, :] = here_ref[...]
        out_ref[count:, :] = arrived_ref[...]

    return pl.pallas_call(
        kernel,
        in_specs=[VMEM, VMEM] + [ANY] * len(passed),
        out_specs=[VMEM] + [ANY] * (len(passed) + len(unset)),
        out_shape=[jax.ShapeDtypeStruct((2 * count, samples), here.dtype)]
        + [jax.ShapeDtypeStruct(x.shape, x.dtype) for x in (*passed, *unset)],
        input_output_aliases={2 + n: 1 + n for n in range(len(passed))},
        compiler_params=PARAMS,
        cost_estimate=COST,
    )(here, arrived, *passed)


def chunks(rights):
    pairs = list(zip(rights[::2], rights[1::2]))
    while pairs:
        group = [pairs.pop(0)]
        while pairs and sum(mine.shape[1] for mine, _ in group) + pairs[0][0].shape[1] <= 256:
            group.append(pairs.pop(0))
        if len(group) > 1:
            yield tuple(jnp.concatenate([ref[...] for ref in side], axis=1) for side in zip(*group))
            continue
        mine, other = group[0]
        for begin in range(0, mine.shape[1], 256):
            yield mine[:, begin : begin + 256], other[:, begin : begin + 256]


def blocks(rows, rights, scale):
    left = 0
    for mine, other in chunks(rights):
        width, top = mine.shape[1], 0
        for row in rows:
            part = row.shape[0] // 2
            total = jnp.dot(row[0:part, :], mine, preferred_element_type=jnp.float32)
            total += jnp.dot(row[part:, :], other, preferred_element_type=jnp.float32)
            yield slice(top, top + part), slice(left, left + width), total * scale
            top += part
        left += width


def tile_kernel(k, parts, pieces, scale, place_ref, *refs):
    out_ref = refs[-1]
    keep = k < place_ref[2]
    for at, columns, block in blocks(refs[:parts], refs[parts : parts + pieces], scale):
        out_ref[0, at, columns] = jnp.where(keep, block, 0.0).astype(out_ref.dtype)


def tile(place, buffer, k, column, rows, rights, samples, after=()):
    count = sum(row.shape[0] for row in rows) // 2
    wide = sum(right.shape[1] for right in rights) // 2
    operands = [place, *rows, *rights, *after, buffer]
    return pl.pallas_call(
        functools.partial(tile_kernel, k, len(rows), len(rights), 1.0 / samples),
        grid=(1,),
        in_specs=[SMEM] + [VMEM] * (len(rows) + len(rights)) + [ANY] * (1 + len(after)),
        out_specs=pl.BlockSpec((1, count, wide), lambda i: (k, 0, column)),
        out_shape=jax.ShapeDtypeStruct(buffer.shape, buffer.dtype),
        input_output_aliases={len(operands) - 1: 0},
        compiler_params=PARAMS,
        cost_estimate=COST,
    )(*operands)


def far_kernel(scale, parts, pieces, place_ref, *refs):
    out_ref = refs[-2]
    for at, columns, block in blocks(refs[:parts], refs[parts : parts + pieces], scale):
        out_ref[at, columns] = block.astype(out_ref.dtype)


def far(place, buffer, rows, rights, samples):
    shape = (sum(row.shape[0] for row in rows) // 2, sum(right.shape[1] for right in rights) // 2)
    operands = [place, *rows, *rights, buffer]
    return pl.pallas_call(
        functools.partial(far_kernel, 1.0 / samples, len(rows), len(rights)),
        in_specs=[SMEM] + [VMEM] * (len(rows) + len(rights)) + [ANY],
        out_specs=[VMEM, ANY],
        out_shape=[
            jax.ShapeDtypeStruct(shape, jnp.bfloat16),
            jax.ShapeDtypeStruct(buffer.shape, buffer.dtype),
        ],
        input_output_aliases={len(operands) - 1: 1},
        compiler_params=PARAMS,
        cost_estimate=COST,
    )(*operands)


def choose_kernel(place_ref, odd_ref, even_ref, *refs):
    out_ref = refs[-1]

    @pl.when(place_ref[0] == 1)
    def _():
        out_ref[...] = odd_ref[...]

    @pl.when(place_ref[0] == 0)
    def _():
        out_ref[...] = even_ref[...]


def choose(place, if_odd, if_even, passed=(), after=()):
    operands = [if_even, *passed]
    return pl.pallas_call(
        choose_kernel,
        in_specs=[SMEM, VMEM, VMEM] + [ANY] * (len(passed) + len(after)),
        out_specs=[VMEM] + [ANY] * len(passed) + [VMEM],
        out_shape=[jax.ShapeDtypeStruct(x.shape, x.dtype) for x in (*operands, if_odd)],
        input_output_aliases={2 + n: n for n in range(len(operands))},
        compiler_params=PARAMS,
        cost_estimate=COST,
    )(place, if_odd, *operands, *after)


def hold(after, *passed):
    def kernel(*refs):
        pass

    return pl.pallas_call(
        kernel,
        in_specs=[ANY] * (len(after) + len(passed)),
        out_specs=[ANY] * len(passed),
        out_shape=[jax.ShapeDtypeStruct(x.shape, x.dtype) for x in passed],
        input_output_aliases={len(after) + n: n for n in range(len(passed))},
        compiler_params=PARAMS,
        cost_estimate=COST,
    )(*after, *passed)


def split_kernel(count, whole_ref, *refs):
    outs = refs[-count:]
    begin = 0
    for out in outs:
        out[...] = whole_ref[:, begin : begin + out.shape[1]]
        begin += out.shape[1]


def split(piece, after, count):
    samples, width = piece.shape
    return pl.pallas_call(
        functools.partial(split_kernel, count),
        in_specs=[VMEM] + [ANY] * len(after),
        out_specs=[VMEM] * count,
        out_shape=[jax.ShapeDtypeStruct((samples, width // count), piece.dtype)] * count,
        compiler_params=PARAMS,
        cost_estimate=COST,
    )(piece, *after)


def put_kernel(place_ref, top2, top3, bottom, out_ref, two, three, sems):
    part, wide = top2.shape
    first = wide * PIECES[0] // (PIECES[0] + PIECES[2])
    end = out_ref.shape[2]
    after = end - wide + first
    copies = []
    for k, scratch, upper, lower in (
        (2, two, top2, bottom[:, wide:]),
        (3, three, top3, bottom[:, 0:wide]),
    ):
        keep = k < place_ref[2]
        scratch[0:part, :] = jnp.where(keep, upper[...], 0.0).astype(scratch.dtype)
        scratch[part:, :] = jnp.where(keep, lower, 0.0).astype(scratch.dtype)
        for n, (here, there) in enumerate(
            ((pl.ds(0, first), pl.ds(0, first)), (pl.ds(first, wide - first), pl.ds(after, end - after)))
        ):
            copy = pltpu.make_async_copy(
                scratch.at[:, here], out_ref.at[k, :, there], sems.at[k - 2, n]
            )
            copy.start()
            copies.append(copy)
    for copy in copies:
        copy.wait()


def put(place, buffer, top2, top3, bottom):
    operands = [place, top2, top3, bottom, buffer]
    shape = (buffer.shape[1], top2.shape[1])

    def kernel(*refs):
        n = len(operands)
        put_kernel(*refs[: n - 1], *refs[n:])

    return pl.pallas_call(
        kernel,
        in_specs=[SMEM] + [VMEM] * (len(operands) - 2) + [ANY],
        out_specs=ANY,
        out_shape=jax.ShapeDtypeStruct(buffer.shape, buffer.dtype),
        scratch_shapes=[
            pltpu.VMEM(shape, buffer.dtype),
            pltpu.VMEM(shape, buffer.dtype),
            pltpu.SemaphoreType.DMA((2, 2)),
        ],
        input_output_aliases={len(operands) - 1: 0},
        compiler_params=PARAMS,
        cost_estimate=COST,
    )(*operands)


def last_kernel(place_ref, side, buffer_ref, out_ref):
    out_ref[0] = jnp.where(3 < place_ref[2], side[...], 0.0).astype(out_ref.dtype)


def last(place, buffer, side, column):
    count, width = side.shape
    return pl.pallas_call(
        last_kernel,
        grid=(1,),
        in_specs=[SMEM, VMEM, ANY],
        out_specs=pl.BlockSpec((1, count, width), lambda i: (3, 0, column)),
        out_shape=jax.ShapeDtypeStruct(buffer.shape, buffer.dtype),
        input_output_aliases={2: 0},
        compiler_params=PARAMS,
        cost_estimate=COST,
    )(place, side, buffer)


def per_device(dosage, observed, counts):
    places = lax.axis_size("var")
    samples = dosage.shape[0] * lax.axis_size("samp")
    width = dosage.shape[1]
    place = jnp.stack(
        [
            (lax.axis_index("var") % 2).astype(jnp.int32),
            lax.axis_index("samp").astype(jnp.int32),
            counts[0],
        ]
    )

    def send(shard, pairs):
        return lax.ppermute(shard, "var", pairs)

    before = [(i + 1, i) for i in range(places - 1)]
    up = [(i, i + 2) for i in range(places - 2)]
    down = [(i + 2, i) for i in range(places - 2)]
    down_odd = [pair for pair in down if pair[0] % 2 == 1]
    to_even = [(i + 1, i) for i in range(0, places - 1, 2)]
    swap = to_even + [(i, i + 1) for i in range(0, places - 1, 2)]

    def mate(shard):
        return lax.ppermute(shard, "samp", [(0, 1), (1, 0)])

    sums, masked = stats(dosage, observed)
    made = score(place, masked, sums, mate(sums))
    direct, relayed, detoured, sent = made[:4]
    here, away = made[4:-PARTS], made[-PARTS:]
    unset = jax.ShapeDtypeStruct((WIN, width // 2, width), jnp.bfloat16)

    upper, buffer = stack(here[0], mate(away[0]), (), (unset,))
    below0 = send(upper, up)
    above = send(relayed, down)
    across = send(detoured, swap)
    (sent,) = hold((across,), sent)
    next_direct = send(sent, before)
    (lower,) = stack(here[1], mate(away[1]))
    below1 = send(lower, up)
    rows = [upper, lower]
    own = [direct, mate(direct), detoured, mate(detoured)]
    (across,) = hold((above,), across)
    around = send(across, down_odd)

    buffer = tile(place, buffer, 0, 0, rows, own[:2], samples)
    buffer = tile(place, buffer, 0, 3, rows, own[2:], samples)
    (buffer,) = hold((below0,), buffer)
    made, buffer = far(place, buffer, [below0], own, samples)
    top2 = send(made, down)
    across, buffer, next_detoured = choose(place, around, across, (buffer,))
    above, buffer, swapped = choose(place, relayed, above, (buffer,))
    next_relayed = send(swapped, swap)
    high = []
    for piece in split(next_direct, (made,), 2):
        high += [piece, mate(piece)]
    high += [next_detoured, mate(next_detoured)]
    made, buffer = far(place, buffer, [below0], high, samples)
    top3 = send(made, down)

    (buffer,) = hold((below1, top2), buffer)
    made, buffer = far(place, buffer, [below1], high + own, samples)
    bottom = send(made, down)
    low = []
    for piece in split(next_relayed, (made, top3), 2):
        low += [piece, mate(piece)]
    made, buffer = far(place, buffer, [below0, below1], low, samples)
    side = send(made, down)
    buffer = tile(place, buffer, 1, 0, rows, high[:-2], samples)
    buffer = tile(place, buffer, 1, 3, rows, high[-2:], samples)
    buffer = tile(place, buffer, 0, 2, rows, [relayed, mate(relayed)], samples)
    buffer = tile(place, buffer, 1, 2, rows, low, samples)
    buffer = tile(place, buffer, 2, 2, rows, [above, mate(above)], samples)
    buffer = put(place, buffer, top2, top3, bottom)
    buffer = last(place, buffer, side, 2)
    return buffer[None]


def solution(mesh):
    in_specs = (P("samp", ("region", "var")), P("samp", ("region", "var")), P(("region", "var")))
    out_specs = P(("region", "var"), None, "samp", None)
    return jax.shard_map(
        per_device, mesh=mesh, in_specs=in_specs, out_specs=out_specs, check_vma=False
    )
```

```python
import functools

import jax
import jax.numpy as jnp
from jax import lax
from jax.experimental import pallas as pl
from jax.experimental.pallas import tpu as pltpu
from jax.sharding import PartitionSpec as P

WIN = 4
PIECES = (3, 3, 2)
ROWS = (9, 7)
PARTS = 2
BLOCKS = 8
STATS_VMEM = 50
epsilon = 1e-05

SMEM = pl.BlockSpec(memory_space=pltpu.SMEM)
VMEM = pl.BlockSpec(memory_space=pltpu.VMEM)
ANY = pl.BlockSpec(memory_space=pl.ANY)
PARAMS = pltpu.CompilerParams(vmem_limit_bytes=32 * 1024 * 1024)
COST = pl.CostEstimate(flops=1000, bytes_accessed=1000, transcendentals=0)


def stats_kernel(dosage_hbm, observed_hbm, sums_ref, masked_ref, dosage_ref, observed_ref, sems):
    samples, width = dosage_ref.shape
    block = samples // BLOCKS
    copies = []
    for n in range(BLOCKS):
        at = pl.ds(n * block, block)
        pair = [
            pltpu.make_async_copy(observed_hbm.at[at], observed_ref.at[at], sems.at[0, n]),
            pltpu.make_async_copy(dosage_hbm.at[at], dosage_ref.at[at], sems.at[1, n]),
        ]
        for copy in pair:
            copy.start()
        copies.append(pair)

    def fold(terms):
        return jnp.sum(terms.reshape(block // 8, 8, width), axis=0)

    totals = [jnp.zeros((8, width), jnp.float32)] * 3
    for n in range(BLOCKS):
        for copy in copies[n]:
            copy.wait()
        at = slice(n * block, (n + 1) * block)
        values = dosage_ref[at, :].astype(jnp.float32)
        present = observed_ref[at, :] > 0
        kept = jnp.where(present, values, 0.0)
        masked_ref[at, :] = jnp.where(present, values, -1.0).astype(masked_ref.dtype)
        terms = [jnp.where(present, 1.0, 0.0), kept, kept * kept]
        totals = [total + fold(term) for total, term in zip(totals, terms)]
    for n in range(3):
        sums_ref[n : n + 1, :] = jnp.sum(totals[n], axis=0, keepdims=True)
    sums_ref[3:, :] = jnp.zeros((5, width), jnp.float32)


def stats(dosage, observed):
    samples, width = dosage.shape
    return pl.pallas_call(
        stats_kernel,
        in_specs=[pl.BlockSpec(memory_space=pltpu.HBM)] * 2,
        out_specs=[VMEM, VMEM],
        out_shape=[
            jax.ShapeDtypeStruct((8, width), jnp.float32),
            jax.ShapeDtypeStruct((samples, width), jnp.bfloat16),
        ],
        scratch_shapes=[
            pltpu.VMEM(dosage.shape, dosage.dtype),
            pltpu.VMEM(observed.shape, observed.dtype),
            pltpu.SemaphoreType.DMA((2, BLOCKS)),
        ],
        compiler_params=pltpu.CompilerParams(vmem_limit_bytes=STATS_VMEM * 1024 * 1024),
        cost_estimate=COST,
    )(dosage, observed)


def score_kernel(place_ref, masked_ref, sums_ref, sums_other_ref, *outs):
    pieces, again_ref = outs[: len(PIECES)], outs[len(PIECES)]
    rows_here, rows_away = outs[len(PIECES) + 1 : -PARTS], outs[-PARTS:]
    core = place_ref[1]
    size = masked_ref.shape[1] // 4
    starts = [sum(piece.shape[1] for piece in pieces[:n]) for n in range(len(pieces))]
    for step in range(4):
        columns = slice(step * size, (step + 1) * size)
        totals = [
            sums_ref[n : n + 1, columns] + sums_other_ref[n : n + 1, columns]
            for n in range(3)
        ]
        count = jnp.maximum(totals[0], 1.0)
        center = totals[1] / count
        spread = totals[2] / count - center * center
        factor = lax.rsqrt(spread + epsilon)
        masked = masked_ref[:, columns].astype(jnp.float32)
        scored = jnp.where(masked >= 0.0, (masked - center) * factor, 0.0)
        scored = scored.astype(jnp.bfloat16)
        for at, piece in zip((*starts, 0), (*pieces, again_ref)):
            low, high = max(step * size, at), min(step * size + size, at + piece.shape[1])
            if low < high:
                piece[:, low - at : high - at] = scored[:, low - step * size : high - step * size]
        turned = scored.T

        def put(parts, turned=turned, begin=step % 2 * size):
            at = 0
            for part in parts:
                low, high = max(begin, at), min(begin + size, at + part.shape[0])
                if low < high:
                    part[low - at : high - at, :] = turned[low - begin : high - begin, :]
                at += part.shape[0]

        here = core == step // 2
        pl.when(here)(functools.partial(put, rows_here))
        pl.when(jnp.logical_not(here))(functools.partial(put, rows_away))


def score(place, masked, sums, sums_other):
    samples, width = masked.shape
    return pl.pallas_call(
        score_kernel,
        in_specs=[SMEM, VMEM, VMEM, VMEM],
        out_specs=[VMEM] * (len(PIECES) + 1 + 2 * PARTS),
        out_shape=[
            jax.ShapeDtypeStruct((samples, width * eighths // 8), jnp.bfloat16) for eighths in (*PIECES, PIECES[0])
        ]
        + [
            jax.ShapeDtypeStruct((width // 2 * share // sum(ROWS), samples), jnp.bfloat16)
            for share in ROWS + ROWS
        ],
        compiler_params=PARAMS,
        cost_estimate=COST,
    )(place, masked, sums, sums_other)


def stack(here, arrived, passed=(), unset=()):
    count, samples = here.shape

    def kernel(here_ref, arrived_ref, *refs):
        out_ref = refs[len(passed)]
        out_ref[0:count, :] = here_ref[...]
        out_ref[count:, :] = arrived_ref[...]

    return pl.pallas_call(
        kernel,
        in_specs=[VMEM, VMEM] + [ANY] * len(passed),
        out_specs=[VMEM] + [ANY] * (len(passed) + len(unset)),
        out_shape=[jax.ShapeDtypeStruct((2 * count, samples), here.dtype)]
        + [jax.ShapeDtypeStruct(x.shape, x.dtype) for x in (*passed, *unset)],
        input_output_aliases={2 + n: 1 + n for n in range(len(passed))},
        compiler_params=PARAMS,
        cost_estimate=COST,
    )(here, arrived, *passed)


def chunks(rights):
    pairs = list(zip(rights[::2], rights[1::2]))
    while pairs:
        group = [pairs.pop(0)]
        while pairs and sum(mine.shape[1] for mine, _ in group) + pairs[0][0].shape[1] <= 256:
            group.append(pairs.pop(0))
        if len(group) > 1:
            yield tuple(jnp.concatenate([ref[...] for ref in side], axis=1) for side in zip(*group))
            continue
        mine, other = group[0]
        for begin in range(0, mine.shape[1], 256):
            yield mine[:, begin : begin + 256], other[:, begin : begin + 256]


def blocks(rows, rights, scale):
    left = 0
    for mine, other in chunks(rights):
        width, top = mine.shape[1], 0
        for row in rows:
            part = row.shape[0] // 2
            total = jnp.dot(row[0:part, :], mine, preferred_element_type=jnp.float32)
            total += jnp.dot(row[part:, :], other, preferred_element_type=jnp.float32)
            yield slice(top, top + part), slice(left, left + width), total * scale
            top += part
        left += width


def tile_kernel(k, parts, pieces, scale, place_ref, *refs):
    out_ref = refs[-1]
    keep = k < place_ref[2]
    for at, columns, block in blocks(refs[:parts], refs[parts : parts + pieces], scale):
        out_ref[0, at, columns] = jnp.where(keep, block, 0.0).astype(out_ref.dtype)


def tile(place, buffer, k, column, rows, rights, samples, after=()):
    count = sum(row.shape[0] for row in rows) // 2
    wide = sum(right.shape[1] for right in rights) // 2
    operands = [place, *rows, *rights, *after, buffer]
    return pl.pallas_call(
        functools.partial(tile_kernel, k, len(rows), len(rights), 1.0 / samples),
        grid=(1,),
        in_specs=[SMEM] + [VMEM] * (len(rows) + len(rights)) + [ANY] * (1 + len(after)),
        out_specs=pl.BlockSpec((1, count, wide), lambda i: (k, 0, column)),
        out_shape=jax.ShapeDtypeStruct(buffer.shape, buffer.dtype),
        input_output_aliases={len(operands) - 1: 0},
        compiler_params=PARAMS,
        cost_estimate=COST,
    )(*operands)


def far_kernel(scale, parts, pieces, place_ref, *refs):
    out_ref = refs[-2]
    for at, columns, block in blocks(refs[:parts], refs[parts : parts + pieces], scale):
        out_ref[at, columns] = block.astype(out_ref.dtype)


def far(place, buffer, rows, rights, samples):
    shape = (sum(row.shape[0] for row in rows) // 2, sum(right.shape[1] for right in rights) // 2)
    operands = [place, *rows, *rights, buffer]
    return pl.pallas_call(
        functools.partial(far_kernel, 1.0 / samples, len(rows), len(rights)),
        in_specs=[SMEM] + [VMEM] * (len(rows) + len(rights)) + [ANY],
        out_specs=[VMEM, ANY],
        out_shape=[
            jax.ShapeDtypeStruct(shape, jnp.bfloat16),
            jax.ShapeDtypeStruct(buffer.shape, buffer.dtype),
        ],
        input_output_aliases={len(operands) - 1: 1},
        compiler_params=PARAMS,
        cost_estimate=COST,
    )(*operands)


def choose_kernel(place_ref, odd_ref, even_ref, *refs):
    out_ref = refs[-1]

    @pl.when(place_ref[0] == 1)
    def _():
        out_ref[...] = odd_ref[...]

    @pl.when(place_ref[0] == 0)
    def _():
        out_ref[...] = even_ref[...]


def choose(place, if_odd, if_even, passed=(), after=()):
    operands = [if_even, *passed]
    return pl.pallas_call(
        choose_kernel,
        in_specs=[SMEM, VMEM, VMEM] + [ANY] * (len(passed) + len(after)),
        out_specs=[VMEM] + [ANY] * len(passed) + [VMEM],
        out_shape=[jax.ShapeDtypeStruct(x.shape, x.dtype) for x in (*operands, if_odd)],
        input_output_aliases={2 + n: n for n in range(len(operands))},
        compiler_params=PARAMS,
        cost_estimate=COST,
    )(place, if_odd, *operands, *after)


def hold(after, *passed):
    def kernel(*refs):
        pass

    return pl.pallas_call(
        kernel,
        in_specs=[ANY] * (len(after) + len(passed)),
        out_specs=[ANY] * len(passed),
        out_shape=[jax.ShapeDtypeStruct(x.shape, x.dtype) for x in passed],
        input_output_aliases={len(after) + n: n for n in range(len(passed))},
        compiler_params=PARAMS,
        cost_estimate=COST,
    )(*after, *passed)


def split_kernel(count, whole_ref, *refs):
    outs = refs[-count:]
    begin = 0
    for out in outs:
        out[...] = whole_ref[:, begin : begin + out.shape[1]]
        begin += out.shape[1]


def split(piece, after, count):
    samples, width = piece.shape
    return pl.pallas_call(
        functools.partial(split_kernel, count),
        in_specs=[VMEM] + [ANY] * len(after),
        out_specs=[VMEM] * count,
        out_shape=[jax.ShapeDtypeStruct((samples, width // count), piece.dtype)] * count,
        compiler_params=PARAMS,
        cost_estimate=COST,
    )(piece, *after)


def put_kernel(place_ref, top2, top3, bottom, out_ref, two, three, sems):
    part, wide = top2.shape
    first = wide * PIECES[0] // (PIECES[0] + PIECES[2])
    end = out_ref.shape[2]
    after = end - wide + first
    copies = []
    for k, scratch, upper, lower in (
        (2, two, top2, bottom[:, wide:]),
        (3, three, top3, bottom[:, 0:wide]),
    ):
        keep = k < place_ref[2]
        scratch[0:part, :] = jnp.where(keep, upper[...], 0.0).astype(scratch.dtype)
        scratch[part:, :] = jnp.where(keep, lower, 0.0).astype(scratch.dtype)
        for n, (here, there) in enumerate(
            ((pl.ds(0, first), pl.ds(0, first)), (pl.ds(first, wide - first), pl.ds(after, end - after)))
        ):
            copy = pltpu.make_async_copy(
                scratch.at[:, here], out_ref.at[k, :, there], sems.at[k - 2, n]
            )
            copy.start()
            copies.append(copy)
    for copy in copies:
        copy.wait()


def put(place, buffer, top2, top3, bottom, passed):
    operands = [place, top2, top3, bottom, passed, buffer]
    shape = (buffer.shape[1], top2.shape[1])

    def kernel(*refs):
        n = len(operands)
        put_kernel(*refs[: n - 2], *refs[n + 1 :])

    return pl.pallas_call(
        kernel,
        in_specs=[SMEM] + [VMEM] * (len(operands) - 3) + [ANY] * 2,
        out_specs=[ANY] * 2,
        out_shape=[jax.ShapeDtypeStruct(x.shape, x.dtype) for x in (passed, buffer)],
        scratch_shapes=[
            pltpu.VMEM(shape, buffer.dtype),
            pltpu.VMEM(shape, buffer.dtype),
            pltpu.SemaphoreType.DMA((2, 2)),
        ],
        input_output_aliases={len(operands) - 2: 0, len(operands) - 1: 1},
        compiler_params=PARAMS,
        cost_estimate=COST,
    )(*operands)


def last_kernel(place_ref, side, buffer_ref, out_ref):
    out_ref[0] = jnp.where(3 < place_ref[2], side[...], 0.0).astype(out_ref.dtype)


def last(place, buffer, side, column):
    count, width = side.shape
    return pl.pallas_call(
        last_kernel,
        grid=(1,),
        in_specs=[SMEM, VMEM, ANY],
        out_specs=pl.BlockSpec((1, count, width), lambda i: (3, 0, column)),
        out_shape=jax.ShapeDtypeStruct(buffer.shape, buffer.dtype),
        input_output_aliases={2: 0},
        compiler_params=PARAMS,
        cost_estimate=COST,
    )(place, side, buffer)


def per_device(dosage, observed, counts):
    places = lax.axis_size("var")
    samples = dosage.shape[0] * lax.axis_size("samp")
    width = dosage.shape[1]
    place = jnp.stack(
        [
            (lax.axis_index("var") % 2).astype(jnp.int32),
            lax.axis_index("samp").astype(jnp.int32),
            counts[0],
        ]
    )

    def send(shard, pairs):
        return lax.ppermute(shard, "var", pairs)

    before = [(i + 1, i) for i in range(places - 1)]
    up = [(i, i + 2) for i in range(places - 2)]
    down = [(i + 2, i) for i in range(places - 2)]
    down_odd = [pair for pair in down if pair[0] % 2 == 1]
    to_even = [(i + 1, i) for i in range(0, places - 1, 2)]
    swap = to_even + [(i, i + 1) for i in range(0, places - 1, 2)]

    def mate(shard):
        return lax.ppermute(shard, "samp", [(0, 1), (1, 0)])

    sums, masked = stats(dosage, observed)
    made = score(place, masked, sums, mate(sums))
    direct, relayed, detoured, sent = made[:4]
    here, away = made[4:-PARTS], made[-PARTS:]
    unset = jax.ShapeDtypeStruct((WIN, width // 2, width), jnp.bfloat16)

    upper, buffer = stack(here[0], mate(away[0]), (), (unset,))
    below0 = send(upper, up)
    above = send(relayed, down)
    across = send(detoured, swap)
    (sent,) = hold((across,), sent)
    next_direct = send(sent, before)
    (lower,) = stack(here[1], mate(away[1]))
    below1 = send(lower, up)
    rows = [upper, lower]
    own = [direct, mate(direct), detoured, mate(detoured)]
    (across,) = hold((above,), across)
    around = send(across, down_odd)

    buffer = tile(place, buffer, 0, 0, rows, own[:2], samples)
    buffer = tile(place, buffer, 0, 3, rows, own[2:], samples)
    (buffer,) = hold((below0,), buffer)
    made, buffer = far(place, buffer, [below0], own, samples)
    top2 = send(made, down)
    across, buffer, next_detoured = choose(place, around, across, (buffer,))
    above, buffer, swapped = choose(place, relayed, above, (buffer,))
    next_relayed = send(swapped, swap)
    high = []
    for piece in split(next_direct, (made, next_detoured, swapped), 3):
        high += [piece, mate(piece)]
    high += [next_detoured, mate(next_detoured)]
    made, buffer = far(place, buffer, [below0], high, samples)
    top3 = send(made, down)

    (buffer,) = hold((below1, top2), buffer)
    made, buffer = far(place, buffer, [below1], high + own, samples)
    bottom = send(made, down)
    low = []
    for piece in split(next_relayed, (made, top3), 3):
        low += [piece, mate(piece)]
    made, buffer = far(place, buffer, [below0, below1], low, samples)
    side = send(made, down)
    buffer = tile(place, buffer, 1, 0, rows, high[:-2], samples)
    buffer = tile(place, buffer, 1, 3, rows, high[-2:], samples)
    buffer = tile(place, buffer, 0, 1, rows, [relayed, mate(relayed)], samples)
    buffer = tile(place, buffer, 1, 1, rows, low, samples)
    pieces = list(split(above, (), 3))
    pieces[2], buffer = put(place, buffer, top2, top3, bottom, pieces[2])
    home = [array for piece in pieces for array in (piece, mate(piece))]
    buffer = tile(place, buffer, 2, 1, rows, home, samples)
    buffer = last(place, buffer, side, 1)
    return buffer[None]


def solution(mesh):
    in_specs = (P("samp", ("region", "var")), P("samp", ("region", "var")), P(("region", "var")))
    out_specs = P(("region", "var"), None, "samp", None)
    return jax.shard_map(
        per_device, mesh=mesh, in_specs=in_specs, out_specs=out_specs, check_vma=False
    )
```

```python
import functools

import jax
import jax.numpy as jnp
from jax import lax
from jax.experimental import pallas as pl
from jax.experimental.pallas import tpu as pltpu
from jax.sharding import PartitionSpec as P

WIN = 4
PIECES = (3, 3, 2)
ROWS = (9, 7)
PARTS = 2
BLOCKS = 8
STATS_VMEM = 50
epsilon = 1e-05

SMEM = pl.BlockSpec(memory_space=pltpu.SMEM)
VMEM = pl.BlockSpec(memory_space=pltpu.VMEM)
ANY = pl.BlockSpec(memory_space=pl.ANY)
PARAMS = pltpu.CompilerParams(vmem_limit_bytes=32 * 1024 * 1024)
COST = pl.CostEstimate(flops=1000, bytes_accessed=1000, transcendentals=0)


def stats_kernel(dosage_hbm, observed_hbm, sums_ref, masked_ref, dosage_ref, observed_ref, sems):
    samples, width = dosage_ref.shape
    block = samples // BLOCKS
    copies = []
    for n in range(BLOCKS):
        at = pl.ds(n * block, block)
        pair = [
            pltpu.make_async_copy(observed_hbm.at[at], observed_ref.at[at], sems.at[0, n]),
            pltpu.make_async_copy(dosage_hbm.at[at], dosage_ref.at[at], sems.at[1, n]),
        ]
        for copy in pair:
            copy.start()
        copies.append(pair)

    def fold(terms):
        return jnp.sum(terms.reshape(block // 8, 8, width), axis=0)

    totals = [jnp.zeros((8, width), jnp.float32)] * 3
    for n in range(BLOCKS):
        for copy in copies[n]:
            copy.wait()
        at = slice(n * block, (n + 1) * block)
        values = dosage_ref[at, :].astype(jnp.float32)
        present = observed_ref[at, :] > 0
        kept = jnp.where(present, values, 0.0)
        masked_ref[at, :] = jnp.where(present, values, -1.0).astype(masked_ref.dtype)
        terms = [jnp.where(present, 1.0, 0.0), kept, kept * kept]
        totals = [total + fold(term) for total, term in zip(totals, terms)]
    for n in range(3):
        sums_ref[n : n + 1, :] = jnp.sum(totals[n], axis=0, keepdims=True)
    sums_ref[3:, :] = jnp.zeros((5, width), jnp.float32)


def stats(dosage, observed):
    samples, width = dosage.shape
    return pl.pallas_call(
        stats_kernel,
        in_specs=[pl.BlockSpec(memory_space=pltpu.HBM)] * 2,
        out_specs=[VMEM, VMEM],
        out_shape=[
            jax.ShapeDtypeStruct((8, width), jnp.float32),
            jax.ShapeDtypeStruct((samples, width), jnp.bfloat16),
        ],
        scratch_shapes=[
            pltpu.VMEM(dosage.shape, dosage.dtype),
            pltpu.VMEM(observed.shape, observed.dtype),
            pltpu.SemaphoreType.DMA((2, BLOCKS)),
        ],
        compiler_params=pltpu.CompilerParams(vmem_limit_bytes=STATS_VMEM * 1024 * 1024),
        cost_estimate=COST,
    )(dosage, observed)


def score_kernel(place_ref, masked_ref, sums_ref, sums_other_ref, *outs):
    pieces, again_ref = outs[: len(PIECES)], outs[len(PIECES)]
    rows_here, rows_away = outs[len(PIECES) + 1 : -PARTS], outs[-PARTS:]
    core = place_ref[1]
    size = masked_ref.shape[1] // 4
    starts = [sum(piece.shape[1] for piece in pieces[:n]) for n in range(len(pieces))]
    for step in range(4):
        columns = slice(step * size, (step + 1) * size)
        totals = [
            sums_ref[n : n + 1, columns] + sums_other_ref[n : n + 1, columns]
            for n in range(3)
        ]
        count = jnp.maximum(totals[0], 1.0)
        center = totals[1] / count
        spread = totals[2] / count - center * center
        factor = lax.rsqrt(spread + epsilon)
        masked = masked_ref[:, columns].astype(jnp.float32)
        scored = jnp.where(masked >= 0.0, (masked - center) * factor, 0.0)
        scored = scored.astype(jnp.bfloat16)
        for at, piece in zip((*starts, 0), (*pieces, again_ref)):
            low, high = max(step * size, at), min(step * size + size, at + piece.shape[1])
            if low < high:
                piece[:, low - at : high - at] = scored[:, low - step * size : high - step * size]
        turned = scored.T

        def put(parts, turned=turned, begin=step % 2 * size):
            at = 0
            for part in parts:
                low, high = max(begin, at), min(begin + size, at + part.shape[0])
                if low < high:
                    part[low - at : high - at, :] = turned[low - begin : high - begin, :]
                at += part.shape[0]

        here = core == step // 2
        pl.when(here)(functools.partial(put, rows_here))
        pl.when(jnp.logical_not(here))(functools.partial(put, rows_away))


def score(place, masked, sums, sums_other):
    samples, width = masked.shape
    return pl.pallas_call(
        score_kernel,
        in_specs=[SMEM, VMEM, VMEM, VMEM],
        out_specs=[VMEM] * (len(PIECES) + 1 + 2 * PARTS),
        out_shape=[
            jax.ShapeDtypeStruct((samples, width * eighths // 8), jnp.bfloat16) for eighths in (*PIECES, PIECES[0])
        ]
        + [
            jax.ShapeDtypeStruct((width // 2 * share // sum(ROWS), samples), jnp.bfloat16)
            for share in ROWS + ROWS
        ],
        compiler_params=PARAMS,
        cost_estimate=COST,
    )(place, masked, sums, sums_other)


def stack(here, arrived, passed=(), unset=()):
    count, samples = here.shape

    def kernel(here_ref, arrived_ref, *refs):
        out_ref = refs[len(passed)]
        out_ref[0:count, :] = here_ref[...]
        out_ref[count:, :] = arrived_ref[...]

    return pl.pallas_call(
        kernel,
        in_specs=[VMEM, VMEM] + [ANY] * len(passed),
        out_specs=[VMEM] + [ANY] * (len(passed) + len(unset)),
        out_shape=[jax.ShapeDtypeStruct((2 * count, samples), here.dtype)]
        + [jax.ShapeDtypeStruct(x.shape, x.dtype) for x in (*passed, *unset)],
        input_output_aliases={2 + n: 1 + n for n in range(len(passed))},
        compiler_params=PARAMS,
        cost_estimate=COST,
    )(here, arrived, *passed)


def chunks(rights):
    pairs = list(zip(rights[::2], rights[1::2]))
    while pairs:
        group = [pairs.pop(0)]
        while pairs and sum(mine.shape[1] for mine, _ in group) + pairs[0][0].shape[1] <= 256:
            group.append(pairs.pop(0))
        if len(group) > 1:
            yield tuple(jnp.concatenate([ref[...] for ref in side], axis=1) for side in zip(*group))
            continue
        mine, other = group[0]
        for begin in range(0, mine.shape[1], 256):
            yield mine[:, begin : begin + 256], other[:, begin : begin + 256]


def blocks(rows, rights, scale):
    left = 0
    for mine, other in chunks(rights):
        width, top = mine.shape[1], 0
        for row in rows:
            part = row.shape[0] // 2
            total = jnp.dot(row[0:part, :], mine, preferred_element_type=jnp.float32)
            total += jnp.dot(row[part:, :], other, preferred_element_type=jnp.float32)
            yield slice(top, top + part), slice(left, left + width), total * scale
            top += part
        left += width


def tile_kernel(k, parts, pieces, scale, place_ref, *refs):
    out_ref = refs[-1]
    keep = k < place_ref[2]
    for at, columns, block in blocks(refs[:parts], refs[parts : parts + pieces], scale):
        out_ref[0, at, columns] = jnp.where(keep, block, 0.0).astype(out_ref.dtype)


def tile(place, buffer, k, column, rows, rights, samples, after=()):
    count = sum(row.shape[0] for row in rows) // 2
    wide = sum(right.shape[1] for right in rights) // 2
    operands = [place, *rows, *rights, *after, buffer]
    return pl.pallas_call(
        functools.partial(tile_kernel, k, len(rows), len(rights), 1.0 / samples),
        grid=(1,),
        in_specs=[SMEM] + [VMEM] * (len(rows) + len(rights)) + [ANY] * (1 + len(after)),
        out_specs=pl.BlockSpec((1, count, wide), lambda i: (k, 0, column)),
        out_shape=jax.ShapeDtypeStruct(buffer.shape, buffer.dtype),
        input_output_aliases={len(operands) - 1: 0},
        compiler_params=PARAMS,
        cost_estimate=COST,
    )(*operands)


def far_kernel(scale, parts, pieces, place_ref, *refs):
    out_ref = refs[-2]
    for at, columns, block in blocks(refs[:parts], refs[parts : parts + pieces], scale):
        out_ref[at, columns] = block.astype(out_ref.dtype)


def far(place, buffer, rows, rights, samples):
    shape = (sum(row.shape[0] for row in rows) // 2, sum(right.shape[1] for right in rights) // 2)
    operands = [place, *rows, *rights, buffer]
    return pl.pallas_call(
        functools.partial(far_kernel, 1.0 / samples, len(rows), len(rights)),
        in_specs=[SMEM] + [VMEM] * (len(rows) + len(rights)) + [ANY],
        out_specs=[VMEM, ANY],
        out_shape=[
            jax.ShapeDtypeStruct(shape, jnp.bfloat16),
            jax.ShapeDtypeStruct(buffer.shape, buffer.dtype),
        ],
        input_output_aliases={len(operands) - 1: 1},
        compiler_params=PARAMS,
        cost_estimate=COST,
    )(*operands)


def choose_kernel(place_ref, odd_ref, even_ref, *refs):
    out_ref = refs[-1]

    @pl.when(place_ref[0] == 1)
    def _():
        out_ref[...] = odd_ref[...]

    @pl.when(place_ref[0] == 0)
    def _():
        out_ref[...] = even_ref[...]


def choose(place, if_odd, if_even, passed=(), after=()):
    operands = [if_even, *passed]
    return pl.pallas_call(
        choose_kernel,
        in_specs=[SMEM, VMEM, VMEM] + [ANY] * (len(passed) + len(after)),
        out_specs=[VMEM] + [ANY] * len(passed) + [VMEM],
        out_shape=[jax.ShapeDtypeStruct(x.shape, x.dtype) for x in (*operands, if_odd)],
        input_output_aliases={2 + n: n for n in range(len(operands))},
        compiler_params=PARAMS,
        cost_estimate=COST,
    )(place, if_odd, *operands, *after)


def hold(after, *passed):
    def kernel(*refs):
        pass

    return pl.pallas_call(
        kernel,
        in_specs=[ANY] * (len(after) + len(passed)),
        out_specs=[ANY] * len(passed),
        out_shape=[jax.ShapeDtypeStruct(x.shape, x.dtype) for x in passed],
        input_output_aliases={len(after) + n: n for n in range(len(passed))},
        compiler_params=PARAMS,
        cost_estimate=COST,
    )(*after, *passed)


def split_kernel(count, whole_ref, *refs):
    outs = refs[-count:]
    begin = 0
    for out in outs:
        out[...] = whole_ref[:, begin : begin + out.shape[1]]
        begin += out.shape[1]


def split(piece, after, count):
    samples, width = piece.shape
    return pl.pallas_call(
        functools.partial(split_kernel, count),
        in_specs=[VMEM] + [ANY] * len(after),
        out_specs=[VMEM] * count,
        out_shape=[jax.ShapeDtypeStruct((samples, width // count), piece.dtype)] * count,
        compiler_params=PARAMS,
        cost_estimate=COST,
    )(piece, *after)


def put_kernel(place_ref, top2, top3, bottom, out_ref, two, three, sems):
    part, wide = top2.shape
    first = wide * PIECES[0] // (PIECES[0] + PIECES[2])
    end = out_ref.shape[2]
    after = end - wide + first
    copies = []
    for k, scratch, upper, lower in (
        (2, two, top2, bottom[:, wide:]),
        (3, three, top3, bottom[:, 0:wide]),
    ):
        keep = k < place_ref[2]
        scratch[0:part, :] = jnp.where(keep, upper[...], 0.0).astype(scratch.dtype)
        scratch[part:, :] = jnp.where(keep, lower, 0.0).astype(scratch.dtype)
        for n, (here, there) in enumerate(
            ((pl.ds(0, first), pl.ds(0, first)), (pl.ds(first, wide - first), pl.ds(after, end - after)))
        ):
            copy = pltpu.make_async_copy(
                scratch.at[:, here], out_ref.at[k, :, there], sems.at[k - 2, n]
            )
            copy.start()
            copies.append(copy)
    for copy in copies:
        copy.wait()


def put(place, buffer, top2, top3, bottom, passed):
    operands = [place, top2, top3, bottom, passed, buffer]
    shape = (buffer.shape[1], top2.shape[1])

    def kernel(*refs):
        n = len(operands)
        put_kernel(*refs[: n - 2], *refs[n + 1 :])

    return pl.pallas_call(
        kernel,
        in_specs=[SMEM] + [VMEM] * (len(operands) - 3) + [ANY] * 2,
        out_specs=[ANY] * 2,
        out_shape=[jax.ShapeDtypeStruct(x.shape, x.dtype) for x in (passed, buffer)],
        scratch_shapes=[
            pltpu.VMEM(shape, buffer.dtype),
            pltpu.VMEM(shape, buffer.dtype),
            pltpu.SemaphoreType.DMA((2, 2)),
        ],
        input_output_aliases={len(operands) - 2: 0, len(operands) - 1: 1},
        compiler_params=PARAMS,
        cost_estimate=COST,
    )(*operands)


def last_kernel(place_ref, side, buffer_ref, out_ref):
    out_ref[0] = jnp.where(3 < place_ref[2], side[...], 0.0).astype(out_ref.dtype)


def last(place, buffer, side, column):
    count, width = side.shape
    return pl.pallas_call(
        last_kernel,
        grid=(1,),
        in_specs=[SMEM, VMEM, ANY],
        out_specs=pl.BlockSpec((1, count, width), lambda i: (3, 0, column)),
        out_shape=jax.ShapeDtypeStruct(buffer.shape, buffer.dtype),
        input_output_aliases={2: 0},
        compiler_params=PARAMS,
        cost_estimate=COST,
    )(place, side, buffer)


def per_device(dosage, observed, counts):
    places = lax.axis_size("var")
    samples = dosage.shape[0] * lax.axis_size("samp")
    width = dosage.shape[1]
    place = jnp.stack(
        [
            (lax.axis_index("var") % 2).astype(jnp.int32),
            lax.axis_index("samp").astype(jnp.int32),
            counts[0],
        ]
    )

    def send(shard, pairs):
        return lax.ppermute(shard, "var", pairs)

    before = [(i + 1, i) for i in range(places - 1)]
    up = [(i, i + 2) for i in range(places - 2)]
    down = [(i + 2, i) for i in range(places - 2)]
    down_odd = [pair for pair in down if pair[0] % 2 == 1]
    to_even = [(i + 1, i) for i in range(0, places - 1, 2)]
    swap = to_even + [(i, i + 1) for i in range(0, places - 1, 2)]

    def mate(shard):
        return lax.ppermute(shard, "samp", [(0, 1), (1, 0)])

    sums, masked = stats(dosage, observed)
    made = score(place, masked, sums, mate(sums))
    direct, relayed, detoured, sent = made[:4]
    here, away = made[4:-PARTS], made[-PARTS:]
    unset = jax.ShapeDtypeStruct((WIN, width // 2, width), jnp.bfloat16)

    upper, buffer = stack(here[0], mate(away[0]), (), (unset,))
    below0 = send(upper, up)
    above = send(relayed, down)
    across = send(detoured, swap)
    (sent,) = hold((across,), sent)
    next_direct = send(sent, before)
    (lower,) = stack(here[1], mate(away[1]))
    below1 = send(lower, up)
    rows = [upper, lower]
    own = [direct, mate(direct), detoured, mate(detoured)]
    (across,) = hold((above,), across)
    around = send(across, down_odd)

    buffer = tile(place, buffer, 0, 0, rows, own[:2], samples)
    buffer = tile(place, buffer, 0, 3, rows, own[2:], samples)
    (buffer,) = hold((below0,), buffer)
    made, buffer = far(place, buffer, [below0], own, samples)
    top2 = send(made, down)
    across, buffer, next_detoured = choose(place, around, across, (buffer,))
    above, buffer, swapped = choose(place, relayed, above, (buffer,))
    next_relayed = send(swapped, swap)
    high = []
    for piece in split(next_direct, (made, next_detoured, swapped), 3):
        high += [piece, mate(piece)]
    high += [next_detoured, mate(next_detoured)]
    made, buffer = far(place, buffer, [below0], high, samples)
    top3 = send(made, down)
    buffer = tile(place, buffer, 1, 0, rows, high[:-2], samples)
    buffer = tile(place, buffer, 0, 1, rows, [relayed, mate(relayed)], samples)

    (buffer,) = hold((below1, top2), buffer)
    made, buffer = far(place, buffer, [below1], high + own, samples)
    bottom = send(made, down)
    low = []
    for piece in split(next_relayed, (made, top3), 3):
        low += [piece, mate(piece)]
    made, buffer = far(place, buffer, [below0, below1], low, samples)
    side = send(made, down)
    buffer = tile(place, buffer, 1, 3, rows, high[-2:], samples)
    buffer = tile(place, buffer, 1, 1, rows, low, samples)
    pieces = list(split(above, (), 3))
    pieces[2], buffer = put(place, buffer, top2, top3, bottom, pieces[2])
    home = [array for piece in pieces for array in (piece, mate(piece))]
    buffer = tile(place, buffer, 2, 1, rows, home, samples)
    buffer = last(place, buffer, side, 1)
    return buffer[None]


def solution(mesh):
    in_specs = (P("samp", ("region", "var")), P("samp", ("region", "var")), P(("region", "var")))
    out_specs = P(("region", "var"), None, "samp", None)
    return jax.shard_map(
        per_device, mesh=mesh, in_specs=in_specs, out_specs=out_specs, check_vma=False
    )
```

```python
import functools

import jax
import jax.numpy as jnp
from jax import lax
from jax.experimental import pallas as pl
from jax.experimental.pallas import tpu as pltpu
from jax.sharding import PartitionSpec as P

WIN = 4
PIECES = (3, 3, 2)
ROWS = (17, 15)
PARTS = 2
BLOCKS = 8
STATS_VMEM = 50
epsilon = 1e-05

SMEM = pl.BlockSpec(memory_space=pltpu.SMEM)
VMEM = pl.BlockSpec(memory_space=pltpu.VMEM)
ANY = pl.BlockSpec(memory_space=pl.ANY)
PARAMS = pltpu.CompilerParams(vmem_limit_bytes=32 * 1024 * 1024)
COST = pl.CostEstimate(flops=1000, bytes_accessed=1000, transcendentals=0)


def stats_kernel(dosage_hbm, observed_hbm, sums_ref, masked_ref, dosage_ref, observed_ref, sems):
    samples, width = dosage_ref.shape
    block = samples // BLOCKS
    copies = []
    for n in range(BLOCKS):
        at = pl.ds(n * block, block)
        pair = [
            pltpu.make_async_copy(observed_hbm.at[at], observed_ref.at[at], sems.at[0, n]),
            pltpu.make_async_copy(dosage_hbm.at[at], dosage_ref.at[at], sems.at[1, n]),
        ]
        for copy in pair:
            copy.start()
        copies.append(pair)

    def fold(terms):
        return jnp.sum(terms.reshape(block // 8, 8, width), axis=0)

    totals = [jnp.zeros((8, width), jnp.float32)] * 3
    for n in range(BLOCKS):
        for copy in copies[n]:
            copy.wait()
        at = slice(n * block, (n + 1) * block)
        values = dosage_ref[at, :].astype(jnp.float32)
        present = observed_ref[at, :] > 0
        kept = jnp.where(present, values, 0.0)
        masked_ref[at, :] = jnp.where(present, values, -1.0).astype(masked_ref.dtype)
        terms = [jnp.where(present, 1.0, 0.0), kept, kept * kept]
        totals = [total + fold(term) for total, term in zip(totals, terms)]
    for n in range(3):
        sums_ref[n : n + 1, :] = jnp.sum(totals[n], axis=0, keepdims=True)
    sums_ref[3:, :] = jnp.zeros((5, width), jnp.float32)


def stats(dosage, observed):
    samples, width = dosage.shape
    return pl.pallas_call(
        stats_kernel,
        in_specs=[pl.BlockSpec(memory_space=pltpu.HBM)] * 2,
        out_specs=[VMEM, VMEM],
        out_shape=[
            jax.ShapeDtypeStruct((8, width), jnp.float32),
            jax.ShapeDtypeStruct((samples, width), jnp.bfloat16),
        ],
        scratch_shapes=[
            pltpu.VMEM(dosage.shape, dosage.dtype),
            pltpu.VMEM(observed.shape, observed.dtype),
            pltpu.SemaphoreType.DMA((2, BLOCKS)),
        ],
        compiler_params=pltpu.CompilerParams(vmem_limit_bytes=STATS_VMEM * 1024 * 1024),
        cost_estimate=COST,
    )(dosage, observed)


def score_kernel(place_ref, masked_ref, sums_ref, sums_other_ref, *outs):
    pieces, again_ref = outs[: len(PIECES)], outs[len(PIECES)]
    rows_here, rows_away = outs[len(PIECES) + 1 : -PARTS], outs[-PARTS:]
    core = place_ref[1]
    size = masked_ref.shape[1] // 4
    starts = [sum(piece.shape[1] for piece in pieces[:n]) for n in range(len(pieces))]
    for step in range(4):
        columns = slice(step * size, (step + 1) * size)
        totals = [
            sums_ref[n : n + 1, columns] + sums_other_ref[n : n + 1, columns]
            for n in range(3)
        ]
        count = jnp.maximum(totals[0], 1.0)
        center = totals[1] / count
        spread = totals[2] / count - center * center
        factor = lax.rsqrt(spread + epsilon)
        masked = masked_ref[:, columns].astype(jnp.float32)
        scored = jnp.where(masked >= 0.0, (masked - center) * factor, 0.0)
        scored = scored.astype(jnp.bfloat16)
        for at, piece in zip((*starts, 0), (*pieces, again_ref)):
            low, high = max(step * size, at), min(step * size + size, at + piece.shape[1])
            if low < high:
                piece[:, low - at : high - at] = scored[:, low - step * size : high - step * size]
        turned = scored.T

        def put(parts, turned=turned, begin=step % 2 * size):
            at = 0
            for part in parts:
                low, high = max(begin, at), min(begin + size, at + part.shape[0])
                if low < high:
                    part[low - at : high - at, :] = turned[low - begin : high - begin, :]
                at += part.shape[0]

        here = core == step // 2
        pl.when(here)(functools.partial(put, rows_here))
        pl.when(jnp.logical_not(here))(functools.partial(put, rows_away))


def score(place, masked, sums, sums_other):
    samples, width = masked.shape
    return pl.pallas_call(
        score_kernel,
        in_specs=[SMEM, VMEM, VMEM, VMEM],
        out_specs=[VMEM] * (len(PIECES) + 1 + 2 * PARTS),
        out_shape=[
            jax.ShapeDtypeStruct((samples, width * eighths // 8), jnp.bfloat16) for eighths in (*PIECES, PIECES[0])
        ]
        + [
            jax.ShapeDtypeStruct((width // 2 * share // sum(ROWS), samples), jnp.bfloat16)
            for share in ROWS + ROWS
        ],
        compiler_params=PARAMS,
        cost_estimate=COST,
    )(place, masked, sums, sums_other)


def stack(here, arrived, passed=(), unset=()):
    count, samples = here.shape

    def kernel(here_ref, arrived_ref, *refs):
        out_ref = refs[len(passed)]
        out_ref[0:count, :] = here_ref[...]
        out_ref[count:, :] = arrived_ref[...]

    return pl.pallas_call(
        kernel,
        in_specs=[VMEM, VMEM] + [ANY] * len(passed),
        out_specs=[VMEM] + [ANY] * (len(passed) + len(unset)),
        out_shape=[jax.ShapeDtypeStruct((2 * count, samples), here.dtype)]
        + [jax.ShapeDtypeStruct(x.shape, x.dtype) for x in (*passed, *unset)],
        input_output_aliases={2 + n: 1 + n for n in range(len(passed))},
        compiler_params=PARAMS,
        cost_estimate=COST,
    )(here, arrived, *passed)


def chunks(rights):
    pairs = list(zip(rights[::2], rights[1::2]))
    while pairs:
        group = [pairs.pop(0)]
        while pairs and sum(mine.shape[1] for mine, _ in group) + pairs[0][0].shape[1] <= 256:
            group.append(pairs.pop(0))
        if len(group) > 1:
            yield tuple(jnp.concatenate([ref[...] for ref in side], axis=1) for side in zip(*group))
            continue
        mine, other = group[0]
        for begin in range(0, mine.shape[1], 256):
            yield mine[:, begin : begin + 256], other[:, begin : begin + 256]


def blocks(rows, rights, scale):
    left = 0
    for mine, other in chunks(rights):
        width, top = mine.shape[1], 0
        for row in rows:
            part = row.shape[0] // 2
            total = jnp.dot(row[0:part, :], mine, preferred_element_type=jnp.float32)
            total += jnp.dot(row[part:, :], other, preferred_element_type=jnp.float32)
            yield slice(top, top + part), slice(left, left + width), total * scale
            top += part
        left += width


def tile_kernel(k, parts, pieces, scale, place_ref, *refs):
    out_ref = refs[-1]
    keep = k < place_ref[2]
    for at, columns, block in blocks(refs[:parts], refs[parts : parts + pieces], scale):
        out_ref[0, at, columns] = jnp.where(keep, block, 0.0).astype(out_ref.dtype)


def tile(place, buffer, k, column, rows, rights, samples, after=()):
    count = sum(row.shape[0] for row in rows) // 2
    wide = sum(right.shape[1] for right in rights) // 2
    operands = [place, *rows, *rights, *after, buffer]
    return pl.pallas_call(
        functools.partial(tile_kernel, k, len(rows), len(rights), 1.0 / samples),
        grid=(1,),
        in_specs=[SMEM] + [VMEM] * (len(rows) + len(rights)) + [ANY] * (1 + len(after)),
        out_specs=pl.BlockSpec((1, count, wide), lambda i: (k, 0, column)),
        out_shape=jax.ShapeDtypeStruct(buffer.shape, buffer.dtype),
        input_output_aliases={len(operands) - 1: 0},
        compiler_params=PARAMS,
        cost_estimate=COST,
    )(*operands)


def far_kernel(scale, parts, pieces, place_ref, *refs):
    out_ref = refs[-2]
    for at, columns, block in blocks(refs[:parts], refs[parts : parts + pieces], scale):
        out_ref[at, columns] = block.astype(out_ref.dtype)


def far(place, buffer, rows, rights, samples):
    shape = (sum(row.shape[0] for row in rows) // 2, sum(right.shape[1] for right in rights) // 2)
    operands = [place, *rows, *rights, buffer]
    return pl.pallas_call(
        functools.partial(far_kernel, 1.0 / samples, len(rows), len(rights)),
        in_specs=[SMEM] + [VMEM] * (len(rows) + len(rights)) + [ANY],
        out_specs=[VMEM, ANY],
        out_shape=[
            jax.ShapeDtypeStruct(shape, jnp.bfloat16),
            jax.ShapeDtypeStruct(buffer.shape, buffer.dtype),
        ],
        input_output_aliases={len(operands) - 1: 1},
        compiler_params=PARAMS,
        cost_estimate=COST,
    )(*operands)


def choose_kernel(place_ref, odd_ref, even_ref, *refs):
    out_ref = refs[-1]

    @pl.when(place_ref[0] == 1)
    def _():
        out_ref[...] = odd_ref[...]

    @pl.when(place_ref[0] == 0)
    def _():
        out_ref[...] = even_ref[...]


def choose(place, if_odd, if_even, passed=(), after=()):
    operands = [if_even, *passed]
    return pl.pallas_call(
        choose_kernel,
        in_specs=[SMEM, VMEM, VMEM] + [ANY] * (len(passed) + len(after)),
        out_specs=[VMEM] + [ANY] * len(passed) + [VMEM],
        out_shape=[jax.ShapeDtypeStruct(x.shape, x.dtype) for x in (*operands, if_odd)],
        input_output_aliases={2 + n: n for n in range(len(operands))},
        compiler_params=PARAMS,
        cost_estimate=COST,
    )(place, if_odd, *operands, *after)


def hold(after, *passed):
    def kernel(*refs):
        pass

    return pl.pallas_call(
        kernel,
        in_specs=[ANY] * (len(after) + len(passed)),
        out_specs=[ANY] * len(passed),
        out_shape=[jax.ShapeDtypeStruct(x.shape, x.dtype) for x in passed],
        input_output_aliases={len(after) + n: n for n in range(len(passed))},
        compiler_params=PARAMS,
        cost_estimate=COST,
    )(*after, *passed)


def split_kernel(count, whole_ref, *refs):
    outs = refs[-count:]
    begin = 0
    for out in outs:
        out[...] = whole_ref[:, begin : begin + out.shape[1]]
        begin += out.shape[1]


def split(piece, after, count):
    samples, width = piece.shape
    return pl.pallas_call(
        functools.partial(split_kernel, count),
        in_specs=[VMEM] + [ANY] * len(after),
        out_specs=[VMEM] * count,
        out_shape=[jax.ShapeDtypeStruct((samples, width // count), piece.dtype)] * count,
        compiler_params=PARAMS,
        cost_estimate=COST,
    )(piece, *after)


def put_kernel(place_ref, top2, top3, bottom, out_ref, two, three, sems):
    part, wide = top2.shape
    first = wide * PIECES[0] // (PIECES[0] + PIECES[2])
    end = out_ref.shape[2]
    after = end - wide + first
    copies = []
    for k, scratch, upper, lower in (
        (2, two, top2, bottom[:, wide:]),
        (3, three, top3, bottom[:, 0:wide]),
    ):
        keep = k < place_ref[2]
        scratch[0:part, :] = jnp.where(keep, upper[...], 0.0).astype(scratch.dtype)
        scratch[part:, :] = jnp.where(keep, lower, 0.0).astype(scratch.dtype)
        for n, (here, there) in enumerate(
            ((pl.ds(0, first), pl.ds(0, first)), (pl.ds(first, wide - first), pl.ds(after, end - after)))
        ):
            copy = pltpu.make_async_copy(
                scratch.at[:, here], out_ref.at[k, :, there], sems.at[k - 2, n]
            )
            copy.start()
            copies.append(copy)
    for copy in copies:
        copy.wait()


def put(place, buffer, top2, top3, bottom, passed):
    operands = [place, top2, top3, bottom, passed, buffer]
    shape = (buffer.shape[1], top2.shape[1])

    def kernel(*refs):
        n = len(operands)
        put_kernel(*refs[: n - 2], *refs[n + 1 :])

    return pl.pallas_call(
        kernel,
        in_specs=[SMEM] + [VMEM] * (len(operands) - 3) + [ANY] * 2,
        out_specs=[ANY] * 2,
        out_shape=[jax.ShapeDtypeStruct(x.shape, x.dtype) for x in (passed, buffer)],
        scratch_shapes=[
            pltpu.VMEM(shape, buffer.dtype),
            pltpu.VMEM(shape, buffer.dtype),
            pltpu.SemaphoreType.DMA((2, 2)),
        ],
        input_output_aliases={len(operands) - 2: 0, len(operands) - 1: 1},
        compiler_params=PARAMS,
        cost_estimate=COST,
    )(*operands)


def last_kernel(place_ref, side, buffer_ref, out_ref):
    out_ref[0] = jnp.where(3 < place_ref[2], side[...], 0.0).astype(out_ref.dtype)


def last(place, buffer, side, column):
    count, width = side.shape
    return pl.pallas_call(
        last_kernel,
        grid=(1,),
        in_specs=[SMEM, VMEM, ANY],
        out_specs=pl.BlockSpec((1, count, width), lambda i: (3, 0, column)),
        out_shape=jax.ShapeDtypeStruct(buffer.shape, buffer.dtype),
        input_output_aliases={2: 0},
        compiler_params=PARAMS,
        cost_estimate=COST,
    )(place, side, buffer)


def per_device(dosage, observed, counts):
    places = lax.axis_size("var")
    samples = dosage.shape[0] * lax.axis_size("samp")
    width = dosage.shape[1]
    place = jnp.stack(
        [
            (lax.axis_index("var") % 2).astype(jnp.int32),
            lax.axis_index("samp").astype(jnp.int32),
            counts[0],
        ]
    )

    def send(shard, pairs):
        return lax.ppermute(shard, "var", pairs)

    before = [(i + 1, i) for i in range(places - 1)]
    up = [(i, i + 2) for i in range(places - 2)]
    down = [(i + 2, i) for i in range(places - 2)]
    down_odd = [pair for pair in down if pair[0] % 2 == 1]
    to_even = [(i + 1, i) for i in range(0, places - 1, 2)]
    swap = to_even + [(i, i + 1) for i in range(0, places - 1, 2)]

    def mate(shard):
        return lax.ppermute(shard, "samp", [(0, 1), (1, 0)])

    sums, masked = stats(dosage, observed)
    made = score(place, masked, sums, mate(sums))
    direct, relayed, detoured, sent = made[:4]
    here, away = made[4:-PARTS], made[-PARTS:]
    unset = jax.ShapeDtypeStruct((WIN, width // 2, width), jnp.bfloat16)

    upper, buffer = stack(here[0], mate(away[0]), (), (unset,))
    below0 = send(upper, up)
    above = send(relayed, down)
    across = send(detoured, swap)
    (sent,) = hold((across,), sent)
    next_direct = send(sent, before)
    (lower,) = stack(here[1], mate(away[1]))
    below1 = send(lower, up)
    rows = [upper, lower]
    own = [direct, mate(direct), detoured, mate(detoured)]
    (across,) = hold((above,), across)
    around = send(across, down_odd)

    buffer = tile(place, buffer, 0, 0, rows, own[:2], samples)
    buffer = tile(place, buffer, 0, 3, rows, own[2:], samples)
    above, buffer, swapped = choose(place, relayed, above, (buffer,))
    next_relayed = send(swapped, swap)
    (buffer,) = hold((below0,), buffer)
    made, buffer = far(place, buffer, [below0], own, samples)
    top2 = send(made, down)
    across, buffer, next_detoured = choose(place, around, across, (buffer,))
    high = []
    for piece in split(next_direct, (made, next_detoured, swapped), 3):
        high += [piece, mate(piece)]
    high += [next_detoured, mate(next_detoured)]
    made, buffer = far(place, buffer, [below0], high, samples)
    top3 = send(made, down)
    buffer = tile(place, buffer, 1, 0, rows, high[:-2], samples)
    buffer = tile(place, buffer, 0, 1, rows, [relayed, mate(relayed)], samples)

    (buffer,) = hold((below1, top2), buffer)
    made, buffer = far(place, buffer, [below1], high + own, samples)
    bottom = send(made, down)
    low = []
    for piece in split(next_relayed, (made, top3), 3):
        low += [piece, mate(piece)]
    made, buffer = far(place, buffer, [below0, below1], low, samples)
    side = send(made, down)
    buffer = tile(place, buffer, 1, 3, rows, high[-2:], samples)
    buffer = tile(place, buffer, 1, 1, rows, low, samples)
    pieces = list(split(above, (), 3))
    pieces[2], buffer = put(place, buffer, top2, top3, bottom, pieces[2])
    home = [array for piece in pieces for array in (piece, mate(piece))]
    buffer = tile(place, buffer, 2, 1, rows, home, samples)
    buffer = last(place, buffer, side, 1)
    return buffer[None]


def solution(mesh):
    in_specs = (P("samp", ("region", "var")), P("samp", ("region", "var")), P(("region", "var")))
    out_specs = P(("region", "var"), None, "samp", None)
    return jax.shard_map(
        per_device, mesh=mesh, in_specs=in_specs, out_specs=out_specs, check_vma=False
    )
```

```python
import functools

import jax
import jax.numpy as jnp
from jax import lax
from jax.experimental import pallas as pl
from jax.experimental.pallas import tpu as pltpu
from jax.sharding import PartitionSpec as P

WIN = 4
PIECES = (3, 3, 2)
ROWS = (17, 15)
PARTS = 2
BLOCKS = 8
STATS_VMEM = 50
epsilon = 1e-05

SMEM = pl.BlockSpec(memory_space=pltpu.SMEM)
VMEM = pl.BlockSpec(memory_space=pltpu.VMEM)
ANY = pl.BlockSpec(memory_space=pl.ANY)
PARAMS = pltpu.CompilerParams(vmem_limit_bytes=32 * 1024 * 1024)
COST = pl.CostEstimate(flops=1000, bytes_accessed=1000, transcendentals=0)


def stats_kernel(dosage_hbm, observed_hbm, sums_ref, masked_ref, dosage_ref, observed_ref, sems):
    samples, width = dosage_ref.shape
    block = samples // BLOCKS
    copies = []
    for n in range(BLOCKS):
        at = pl.ds(n * block, block)
        pair = [
            pltpu.make_async_copy(observed_hbm.at[at], observed_ref.at[at], sems.at[0, n]),
            pltpu.make_async_copy(dosage_hbm.at[at], dosage_ref.at[at], sems.at[1, n]),
        ]
        for copy in pair:
            copy.start()
        copies.append(pair)

    def fold(terms):
        return jnp.sum(terms.reshape(block // 8, 8, width), axis=0)

    totals = [jnp.zeros((8, width), jnp.float32)] * 3
    for n in range(BLOCKS):
        for copy in copies[n]:
            copy.wait()
        at = slice(n * block, (n + 1) * block)
        values = dosage_ref[at, :].astype(jnp.float32)
        present = observed_ref[at, :] > 0
        kept = jnp.where(present, values, 0.0)
        masked_ref[at, :] = jnp.where(present, values, -1.0).astype(masked_ref.dtype)
        terms = [jnp.where(present, 1.0, 0.0), kept, kept * kept]
        totals = [total + fold(term) for total, term in zip(totals, terms)]
    for n in range(3):
        sums_ref[n : n + 1, :] = jnp.sum(totals[n], axis=0, keepdims=True)
    sums_ref[3:, :] = jnp.zeros((5, width), jnp.float32)


def stats(dosage, observed):
    samples, width = dosage.shape
    return pl.pallas_call(
        stats_kernel,
        in_specs=[pl.BlockSpec(memory_space=pltpu.HBM)] * 2,
        out_specs=[VMEM, VMEM],
        out_shape=[
            jax.ShapeDtypeStruct((8, width), jnp.float32),
            jax.ShapeDtypeStruct((samples, width), jnp.bfloat16),
        ],
        scratch_shapes=[
            pltpu.VMEM(dosage.shape, dosage.dtype),
            pltpu.VMEM(observed.shape, observed.dtype),
            pltpu.SemaphoreType.DMA((2, BLOCKS)),
        ],
        compiler_params=pltpu.CompilerParams(vmem_limit_bytes=STATS_VMEM * 1024 * 1024),
        cost_estimate=COST,
    )(dosage, observed)


def score_kernel(place_ref, masked_ref, sums_ref, sums_other_ref, *outs):
    pieces, again_ref = outs[: len(PIECES)], outs[len(PIECES)]
    rows_here, rows_away = outs[len(PIECES) + 1 : -PARTS], outs[-PARTS:]
    core = place_ref[1]
    size = masked_ref.shape[1] // 4
    starts = [sum(piece.shape[1] for piece in pieces[:n]) for n in range(len(pieces))]
    for step in range(4):
        columns = slice(step * size, (step + 1) * size)
        totals = [
            sums_ref[n : n + 1, columns] + sums_other_ref[n : n + 1, columns]
            for n in range(3)
        ]
        count = jnp.maximum(totals[0], 1.0)
        center = totals[1] / count
        spread = totals[2] / count - center * center
        factor = lax.rsqrt(spread + epsilon)
        masked = masked_ref[:, columns].astype(jnp.float32)
        scored = jnp.where(masked >= 0.0, (masked - center) * factor, 0.0)
        scored = scored.astype(jnp.bfloat16)
        for at, piece in zip((*starts, 0), (*pieces, again_ref)):
            low, high = max(step * size, at), min(step * size + size, at + piece.shape[1])
            if low < high:
                piece[:, low - at : high - at] = scored[:, low - step * size : high - step * size]
        turned = scored.T

        def put(parts, turned=turned, begin=step % 2 * size):
            at = 0
            for part in parts:
                low, high = max(begin, at), min(begin + size, at + part.shape[0])
                if low < high:
                    part[low - at : high - at, :] = turned[low - begin : high - begin, :]
                at += part.shape[0]

        here = core == step // 2
        pl.when(here)(functools.partial(put, rows_here))
        pl.when(jnp.logical_not(here))(functools.partial(put, rows_away))


def score(place, masked, sums, sums_other):
    samples, width = masked.shape
    return pl.pallas_call(
        score_kernel,
        in_specs=[SMEM, VMEM, VMEM, VMEM],
        out_specs=[VMEM] * (len(PIECES) + 1 + 2 * PARTS),
        out_shape=[
            jax.ShapeDtypeStruct((samples, width * eighths // 8), jnp.bfloat16) for eighths in (*PIECES, PIECES[0])
        ]
        + [
            jax.ShapeDtypeStruct((width // 2 * share // sum(ROWS), samples), jnp.bfloat16)
            for share in ROWS + ROWS
        ],
        compiler_params=PARAMS,
        cost_estimate=COST,
    )(place, masked, sums, sums_other)


def stack(here, arrived, passed=(), unset=()):
    count, samples = here.shape

    def kernel(here_ref, arrived_ref, *refs):
        out_ref = refs[len(passed)]
        out_ref[0:count, :] = here_ref[...]
        out_ref[count:, :] = arrived_ref[...]

    return pl.pallas_call(
        kernel,
        in_specs=[VMEM, VMEM] + [ANY] * len(passed),
        out_specs=[VMEM] + [ANY] * (len(passed) + len(unset)),
        out_shape=[jax.ShapeDtypeStruct((2 * count, samples), here.dtype)]
        + [jax.ShapeDtypeStruct(x.shape, x.dtype) for x in (*passed, *unset)],
        input_output_aliases={2 + n: 1 + n for n in range(len(passed))},
        compiler_params=PARAMS,
        cost_estimate=COST,
    )(here, arrived, *passed)


def chunks(rights):
    pairs = list(zip(rights[::2], rights[1::2]))
    while pairs:
        group = [pairs.pop(0)]
        while pairs and sum(mine.shape[1] for mine, _ in group) + pairs[0][0].shape[1] <= 256:
            group.append(pairs.pop(0))
        if len(group) > 1:
            yield tuple(jnp.concatenate([ref[...] for ref in side], axis=1) for side in zip(*group))
            continue
        mine, other = group[0]
        for begin in range(0, mine.shape[1], 256):
            yield mine[:, begin : begin + 256], other[:, begin : begin + 256]


def blocks(rows, rights, scale):
    left = 0
    for mine, other in chunks(rights):
        width, top = mine.shape[1], 0
        for row in rows:
            part = row.shape[0] // 2
            total = jnp.dot(row[0:part, :], mine, preferred_element_type=jnp.float32)
            total += jnp.dot(row[part:, :], other, preferred_element_type=jnp.float32)
            yield slice(top, top + part), slice(left, left + width), total * scale
            top += part
        left += width


def tile_kernel(k, parts, pieces, scale, place_ref, *refs):
    out_ref = refs[-1]
    keep = k < place_ref[2]
    for at, columns, block in blocks(refs[:parts], refs[parts : parts + pieces], scale):
        out_ref[0, at, columns] = jnp.where(keep, block, 0.0).astype(out_ref.dtype)


def tile(place, buffer, k, column, rows, rights, samples, after=()):
    count = sum(row.shape[0] for row in rows) // 2
    wide = sum(right.shape[1] for right in rights) // 2
    operands = [place, *rows, *rights, *after, buffer]
    return pl.pallas_call(
        functools.partial(tile_kernel, k, len(rows), len(rights), 1.0 / samples),
        grid=(1,),
        in_specs=[SMEM] + [VMEM] * (len(rows) + len(rights)) + [ANY] * (1 + len(after)),
        out_specs=pl.BlockSpec((1, count, wide), lambda i: (k, 0, column)),
        out_shape=jax.ShapeDtypeStruct(buffer.shape, buffer.dtype),
        input_output_aliases={len(operands) - 1: 0},
        compiler_params=PARAMS,
        cost_estimate=COST,
    )(*operands)


def far_kernel(scale, parts, pieces, place_ref, *refs):
    out_ref = refs[-2]
    for at, columns, block in blocks(refs[:parts], refs[parts : parts + pieces], scale):
        out_ref[at, columns] = block.astype(out_ref.dtype)


def far(place, buffer, rows, rights, samples):
    shape = (sum(row.shape[0] for row in rows) // 2, sum(right.shape[1] for right in rights) // 2)
    operands = [place, *rows, *rights, buffer]
    return pl.pallas_call(
        functools.partial(far_kernel, 1.0 / samples, len(rows), len(rights)),
        in_specs=[SMEM] + [VMEM] * (len(rows) + len(rights)) + [ANY],
        out_specs=[VMEM, ANY],
        out_shape=[
            jax.ShapeDtypeStruct(shape, jnp.bfloat16),
            jax.ShapeDtypeStruct(buffer.shape, buffer.dtype),
        ],
        input_output_aliases={len(operands) - 1: 1},
        compiler_params=PARAMS,
        cost_estimate=COST,
    )(*operands)


def choose_kernel(place_ref, odd_ref, even_ref, *refs):
    out_ref = refs[-1]

    @pl.when(place_ref[0] == 1)
    def _():
        out_ref[...] = odd_ref[...]

    @pl.when(place_ref[0] == 0)
    def _():
        out_ref[...] = even_ref[...]


def choose(place, if_odd, if_even, passed=(), after=()):
    operands = [if_even, *passed]
    return pl.pallas_call(
        choose_kernel,
        in_specs=[SMEM, VMEM, VMEM] + [ANY] * (len(passed) + len(after)),
        out_specs=[VMEM] + [ANY] * len(passed) + [VMEM],
        out_shape=[jax.ShapeDtypeStruct(x.shape, x.dtype) for x in (*operands, if_odd)],
        input_output_aliases={2 + n: n for n in range(len(operands))},
        compiler_params=PARAMS,
        cost_estimate=COST,
    )(place, if_odd, *operands, *after)


def hold(after, *passed):
    def kernel(*refs):
        pass

    return pl.pallas_call(
        kernel,
        in_specs=[ANY] * (len(after) + len(passed)),
        out_specs=[ANY] * len(passed),
        out_shape=[jax.ShapeDtypeStruct(x.shape, x.dtype) for x in passed],
        input_output_aliases={len(after) + n: n for n in range(len(passed))},
        compiler_params=PARAMS,
        cost_estimate=COST,
    )(*after, *passed)


def split_kernel(count, whole_ref, *refs):
    outs = refs[-count:]
    begin = 0
    for out in outs:
        out[...] = whole_ref[:, begin : begin + out.shape[1]]
        begin += out.shape[1]


def split(piece, after, count):
    samples, width = piece.shape
    return pl.pallas_call(
        functools.partial(split_kernel, count),
        in_specs=[VMEM] + [ANY] * len(after),
        out_specs=[VMEM] * count,
        out_shape=[jax.ShapeDtypeStruct((samples, width // count), piece.dtype)] * count,
        compiler_params=PARAMS,
        cost_estimate=COST,
    )(piece, *after)


def put_kernel(place_ref, top2, top3, bottom, out_ref, two, three, sems):
    part, wide = top2.shape
    first = wide * PIECES[0] // (PIECES[0] + PIECES[2])
    end = out_ref.shape[2]
    after = end - wide + first
    copies = []
    for k, scratch, upper, lower in (
        (2, two, top2, bottom[:, wide:]),
        (3, three, top3, bottom[:, 0:wide]),
    ):
        keep = k < place_ref[2]
        scratch[0:part, :] = jnp.where(keep, upper[...], 0.0).astype(scratch.dtype)
        scratch[part:, :] = jnp.where(keep, lower, 0.0).astype(scratch.dtype)
        for n, (here, there) in enumerate(
            ((pl.ds(0, first), pl.ds(0, first)), (pl.ds(first, wide - first), pl.ds(after, end - after)))
        ):
            copy = pltpu.make_async_copy(
                scratch.at[:, here], out_ref.at[k, :, there], sems.at[k - 2, n]
            )
            copy.start()
            copies.append(copy)
    for copy in copies:
        copy.wait()


def put(place, buffer, top2, top3, bottom, passed):
    operands = [place, top2, top3, bottom, passed, buffer]
    shape = (buffer.shape[1], top2.shape[1])

    def kernel(*refs):
        n = len(operands)
        put_kernel(*refs[: n - 2], *refs[n + 1 :])

    return pl.pallas_call(
        kernel,
        in_specs=[SMEM] + [VMEM] * (len(operands) - 3) + [ANY] * 2,
        out_specs=[ANY] * 2,
        out_shape=[jax.ShapeDtypeStruct(x.shape, x.dtype) for x in (passed, buffer)],
        scratch_shapes=[
            pltpu.VMEM(shape, buffer.dtype),
            pltpu.VMEM(shape, buffer.dtype),
            pltpu.SemaphoreType.DMA((2, 2)),
        ],
        input_output_aliases={len(operands) - 2: 0, len(operands) - 1: 1},
        compiler_params=PARAMS,
        cost_estimate=COST,
    )(*operands)


def last_kernel(place_ref, side, buffer_ref, out_ref):
    out_ref[0] = jnp.where(3 < place_ref[2], side[...], 0.0).astype(out_ref.dtype)


def last(place, buffer, side, column):
    count, width = side.shape
    return pl.pallas_call(
        last_kernel,
        grid=(1,),
        in_specs=[SMEM, VMEM, ANY],
        out_specs=pl.BlockSpec((1, count, width), lambda i: (3, 0, column)),
        out_shape=jax.ShapeDtypeStruct(buffer.shape, buffer.dtype),
        input_output_aliases={2: 0},
        compiler_params=PARAMS,
        cost_estimate=COST,
    )(place, side, buffer)


def per_device(dosage, observed, counts):
    places = lax.axis_size("var")
    samples = dosage.shape[0] * lax.axis_size("samp")
    width = dosage.shape[1]
    place = jnp.stack(
        [
            (lax.axis_index("var") % 2).astype(jnp.int32),
            lax.axis_index("samp").astype(jnp.int32),
            counts[0],
        ]
    )

    def send(shard, pairs):
        return lax.ppermute(shard, "var", pairs)

    before = [(i + 1, i) for i in range(places - 1)]
    up = [(i, i + 2) for i in range(places - 2)]
    down = [(i + 2, i) for i in range(places - 2)]
    down_odd = [pair for pair in down if pair[0] % 2 == 1]
    to_even = [(i + 1, i) for i in range(0, places - 1, 2)]
    swap = to_even + [(i, i + 1) for i in range(0, places - 1, 2)]

    def mate(shard):
        return lax.ppermute(shard, "samp", [(0, 1), (1, 0)])

    sums, masked = stats(dosage, observed)
    made = score(place, masked, sums, mate(sums))
    direct, relayed, detoured, sent = made[:4]
    here, away = made[4:-PARTS], made[-PARTS:]
    unset = jax.ShapeDtypeStruct((WIN, width // 2, width), jnp.bfloat16)

    upper, buffer = stack(here[0], mate(away[0]), (), (unset,))
    below0 = send(upper, up)
    above = send(relayed, down)
    across = send(detoured, swap)
    (sent,) = hold((across,), sent)
    next_direct = send(sent, before)
    (lower,) = stack(here[1], mate(away[1]))
    below1 = send(lower, up)
    rows = [upper, lower]
    own = [direct, mate(direct), detoured, mate(detoured)]
    (across,) = hold((above,), across)
    around = send(across, down_odd)

    buffer = tile(place, buffer, 0, 0, rows, own[:2], samples)
    buffer = tile(place, buffer, 0, 3, rows, own[2:], samples)
    above, buffer, swapped = choose(place, relayed, above, (buffer,))
    next_relayed = send(swapped, swap)
    (buffer,) = hold((below0,), buffer)
    made, buffer = far(place, buffer, [below0], own, samples)
    top2 = send(made, down)
    across, buffer, next_detoured = choose(place, around, across, (buffer,))
    (next_direct,) = hold((made, next_detoured, swapped), next_direct)
    high = [next_direct, mate(next_direct)]
    high += [next_detoured, mate(next_detoured)]
    made, buffer = far(place, buffer, [below0], high, samples)
    top3 = send(made, down)
    buffer = tile(place, buffer, 1, 0, rows, high[:-2], samples)
    buffer = tile(place, buffer, 0, 1, rows, [relayed, mate(relayed)], samples)

    (buffer,) = hold((below1, top2), buffer)
    made, buffer = far(place, buffer, [below1], high + own, samples)
    bottom = send(made, down)
    low = []
    for piece in split(next_relayed, (made, top3), 3):
        low += [piece, mate(piece)]
    made, buffer = far(place, buffer, [below0, below1], low, samples)
    side = send(made, down)
    buffer = tile(place, buffer, 1, 3, rows, high[-2:], samples)
    buffer = tile(place, buffer, 1, 1, rows, low, samples)
    pieces = list(split(above, (), 3))
    pieces[2], buffer = put(place, buffer, top2, top3, bottom, pieces[2])
    home = [array for piece in pieces for array in (piece, mate(piece))]
    buffer = tile(place, buffer, 2, 1, rows, home, samples)
    buffer = last(place, buffer, side, 1)
    return buffer[None]


def solution(mesh):
    in_specs = (P("samp", ("region", "var")), P("samp", ("region", "var")), P(("region", "var")))
    out_specs = P(("region", "var"), None, "samp", None)
    return jax.shard_map(
        per_device, mesh=mesh, in_specs=in_specs, out_specs=out_specs, check_vma=False
    )
```

```python
import functools

import jax
import jax.numpy as jnp
from jax import lax
from jax.experimental import pallas as pl
from jax.experimental.pallas import tpu as pltpu
from jax.sharding import PartitionSpec as P

WIN = 4
PIECES = (3, 3, 2)
ROWS = (17, 15)
PARTS = 2
BLOCKS = 8
STATS_VMEM = 50
epsilon = 1e-05

SMEM = pl.BlockSpec(memory_space=pltpu.SMEM)
VMEM = pl.BlockSpec(memory_space=pltpu.VMEM)
ANY = pl.BlockSpec(memory_space=pl.ANY)
PARAMS = pltpu.CompilerParams(vmem_limit_bytes=32 * 1024 * 1024)
COST = pl.CostEstimate(flops=1000, bytes_accessed=1000, transcendentals=0)


def stats_kernel(dosage_hbm, observed_hbm, sums_ref, masked_ref, dosage_ref, observed_ref, sems):
    samples, width = dosage_ref.shape
    block = samples // BLOCKS
    copies = []
    for n in range(BLOCKS):
        at = pl.ds(n * block, block)
        pair = [
            pltpu.make_async_copy(observed_hbm.at[at], observed_ref.at[at], sems.at[0, n]),
            pltpu.make_async_copy(dosage_hbm.at[at], dosage_ref.at[at], sems.at[1, n]),
        ]
        for copy in pair:
            copy.start()
        copies.append(pair)

    def fold(terms):
        return jnp.sum(terms.reshape(block // 8, 8, width), axis=0)

    totals = [jnp.zeros((8, width), jnp.float32)] * 3
    for n in range(BLOCKS):
        for copy in copies[n]:
            copy.wait()
        at = slice(n * block, (n + 1) * block)
        values = dosage_ref[at, :].astype(jnp.float32)
        present = observed_ref[at, :] > 0
        kept = jnp.where(present, values, 0.0)
        masked_ref[at, :] = jnp.where(present, values, -1.0).astype(masked_ref.dtype)
        terms = [observed_ref[at, :].astype(jnp.float32), kept, kept * kept]
        totals = [total + fold(term) for total, term in zip(totals, terms)]
    for n in range(3):
        sums_ref[n : n + 1, :] = jnp.sum(totals[n], axis=0, keepdims=True)
    sums_ref[3:, :] = jnp.zeros((5, width), jnp.float32)


def stats(dosage, observed):
    samples, width = dosage.shape
    return pl.pallas_call(
        stats_kernel,
        in_specs=[pl.BlockSpec(memory_space=pltpu.HBM)] * 2,
        out_specs=[VMEM, VMEM],
        out_shape=[
            jax.ShapeDtypeStruct((8, width), jnp.float32),
            jax.ShapeDtypeStruct((samples, width), jnp.bfloat16),
        ],
        scratch_shapes=[
            pltpu.VMEM(dosage.shape, dosage.dtype),
            pltpu.VMEM(observed.shape, observed.dtype),
            pltpu.SemaphoreType.DMA((2, BLOCKS)),
        ],
        compiler_params=pltpu.CompilerParams(vmem_limit_bytes=STATS_VMEM * 1024 * 1024),
        cost_estimate=COST,
    )(dosage, observed)


def score_kernel(place_ref, masked_ref, sums_ref, sums_other_ref, *outs):
    pieces, again_ref = outs[: len(PIECES)], outs[len(PIECES)]
    rows_here, rows_away = outs[len(PIECES) + 1 : -PARTS], outs[-PARTS:]
    core = place_ref[1]
    size = masked_ref.shape[1] // 4
    starts = [sum(piece.shape[1] for piece in pieces[:n]) for n in range(len(pieces))]
    for step in range(4):
        columns = slice(step * size, (step + 1) * size)
        totals = [
            sums_ref[n : n + 1, columns] + sums_other_ref[n : n + 1, columns]
            for n in range(3)
        ]
        count = jnp.maximum(totals[0], 1.0)
        center = totals[1] / count
        spread = totals[2] / count - center * center
        factor = lax.rsqrt(spread + epsilon)
        masked = masked_ref[:, columns].astype(jnp.float32)
        scored = jnp.where(masked >= 0.0, (masked - center) * factor, 0.0)
        scored = scored.astype(jnp.bfloat16)
        for at, piece in zip((*starts, 0), (*pieces, again_ref)):
            low, high = max(step * size, at), min(step * size + size, at + piece.shape[1])
            if low < high:
                piece[:, low - at : high - at] = scored[:, low - step * size : high - step * size]
        turned = scored.T

        def put(parts, turned=turned, begin=step % 2 * size):
            at = 0
            for part in parts:
                low, high = max(begin, at), min(begin + size, at + part.shape[0])
                if low < high:
                    part[low - at : high - at, :] = turned[low - begin : high - begin, :]
                at += part.shape[0]

        here = core == step // 2
        pl.when(here)(functools.partial(put, rows_here))
        pl.when(jnp.logical_not(here))(functools.partial(put, rows_away))


def score(place, masked, sums, sums_other):
    samples, width = masked.shape
    return pl.pallas_call(
        score_kernel,
        in_specs=[SMEM, VMEM, VMEM, VMEM],
        out_specs=[VMEM] * (len(PIECES) + 1 + 2 * PARTS),
        out_shape=[
            jax.ShapeDtypeStruct((samples, width * eighths // 8), jnp.bfloat16) for eighths in (*PIECES, PIECES[0])
        ]
        + [
            jax.ShapeDtypeStruct((width // 2 * share // sum(ROWS), samples), jnp.bfloat16)
            for share in ROWS + ROWS
        ],
        compiler_params=PARAMS,
        cost_estimate=COST,
    )(place, masked, sums, sums_other)


def stack(here, arrived, passed=(), unset=()):
    count, samples = here.shape

    def kernel(here_ref, arrived_ref, *refs):
        out_ref = refs[len(passed)]
        out_ref[0:count, :] = here_ref[...]
        out_ref[count:, :] = arrived_ref[...]

    return pl.pallas_call(
        kernel,
        in_specs=[VMEM, VMEM] + [ANY] * len(passed),
        out_specs=[VMEM] + [ANY] * (len(passed) + len(unset)),
        out_shape=[jax.ShapeDtypeStruct((2 * count, samples), here.dtype)]
        + [jax.ShapeDtypeStruct(x.shape, x.dtype) for x in (*passed, *unset)],
        input_output_aliases={2 + n: 1 + n for n in range(len(passed))},
        compiler_params=PARAMS,
        cost_estimate=COST,
    )(here, arrived, *passed)


def chunks(rights):
    pairs = list(zip(rights[::2], rights[1::2]))
    while pairs:
        group = [pairs.pop(0)]
        while pairs and sum(mine.shape[1] for mine, _ in group) + pairs[0][0].shape[1] <= 256:
            group.append(pairs.pop(0))
        if len(group) > 1:
            yield tuple(jnp.concatenate([ref[...] for ref in side], axis=1) for side in zip(*group))
            continue
        mine, other = group[0]
        for begin in range(0, mine.shape[1], 256):
            yield mine[:, begin : begin + 256], other[:, begin : begin + 256]


def blocks(rows, rights, scale):
    left = 0
    for mine, other in chunks(rights):
        width, top = mine.shape[1], 0
        for row in rows:
            part = row.shape[0] // 2
            total = jnp.dot(row[0:part, :], mine, preferred_element_type=jnp.float32)
            total += jnp.dot(row[part:, :], other, preferred_element_type=jnp.float32)
            yield slice(top, top + part), slice(left, left + width), total * scale
            top += part
        left += width


def tile_kernel(k, parts, pieces, scale, place_ref, *refs):
    out_ref = refs[-1]
    keep = k < place_ref[2]
    for at, columns, block in blocks(refs[:parts], refs[parts : parts + pieces], scale):
        out_ref[0, at, columns] = jnp.where(keep, block, 0.0).astype(out_ref.dtype)


def tile(place, buffer, k, column, rows, rights, samples, after=()):
    count = sum(row.shape[0] for row in rows) // 2
    wide = sum(right.shape[1] for right in rights) // 2
    operands = [place, *rows, *rights, *after, buffer]
    return pl.pallas_call(
        functools.partial(tile_kernel, k, len(rows), len(rights), 1.0 / samples),
        grid=(1,),
        in_specs=[SMEM] + [VMEM] * (len(rows) + len(rights)) + [ANY] * (1 + len(after)),
        out_specs=pl.BlockSpec((1, count, wide), lambda i: (k, 0, column)),
        out_shape=jax.ShapeDtypeStruct(buffer.shape, buffer.dtype),
        input_output_aliases={len(operands) - 1: 0},
        compiler_params=PARAMS,
        cost_estimate=COST,
    )(*operands)


def far_kernel(scale, parts, pieces, place_ref, *refs):
    out_ref = refs[-2]
    for at, columns, block in blocks(refs[:parts], refs[parts : parts + pieces], scale):
        out_ref[at, columns] = block.astype(out_ref.dtype)


def far(place, buffer, rows, rights, samples):
    shape = (sum(row.shape[0] for row in rows) // 2, sum(right.shape[1] for right in rights) // 2)
    operands = [place, *rows, *rights, buffer]
    return pl.pallas_call(
        functools.partial(far_kernel, 1.0 / samples, len(rows), len(rights)),
        in_specs=[SMEM] + [VMEM] * (len(rows) + len(rights)) + [ANY],
        out_specs=[VMEM, ANY],
        out_shape=[
            jax.ShapeDtypeStruct(shape, jnp.bfloat16),
            jax.ShapeDtypeStruct(buffer.shape, buffer.dtype),
        ],
        input_output_aliases={len(operands) - 1: 1},
        compiler_params=PARAMS,
        cost_estimate=COST,
    )(*operands)


def choose_kernel(place_ref, odd_ref, even_ref, *refs):
    out_ref = refs[-1]

    @pl.when(place_ref[0] == 1)
    def _():
        out_ref[...] = odd_ref[...]

    @pl.when(place_ref[0] == 0)
    def _():
        out_ref[...] = even_ref[...]


def choose(place, if_odd, if_even, passed=(), after=()):
    operands = [if_even, *passed]
    return pl.pallas_call(
        choose_kernel,
        in_specs=[SMEM, VMEM, VMEM] + [ANY] * (len(passed) + len(after)),
        out_specs=[VMEM] + [ANY] * len(passed) + [VMEM],
        out_shape=[jax.ShapeDtypeStruct(x.shape, x.dtype) for x in (*operands, if_odd)],
        input_output_aliases={2 + n: n for n in range(len(operands))},
        compiler_params=PARAMS,
        cost_estimate=COST,
    )(place, if_odd, *operands, *after)


def hold(after, *passed):
    def kernel(*refs):
        pass

    return pl.pallas_call(
        kernel,
        in_specs=[ANY] * (len(after) + len(passed)),
        out_specs=[ANY] * len(passed),
        out_shape=[jax.ShapeDtypeStruct(x.shape, x.dtype) for x in passed],
        input_output_aliases={len(after) + n: n for n in range(len(passed))},
        compiler_params=PARAMS,
        cost_estimate=COST,
    )(*after, *passed)


def split_kernel(count, whole_ref, *refs):
    outs = refs[-count:]
    begin = 0
    for out in outs:
        out[...] = whole_ref[:, begin : begin + out.shape[1]]
        begin += out.shape[1]


def split(piece, after, count):
    samples, width = piece.shape
    return pl.pallas_call(
        functools.partial(split_kernel, count),
        in_specs=[VMEM] + [ANY] * len(after),
        out_specs=[VMEM] * count,
        out_shape=[jax.ShapeDtypeStruct((samples, width // count), piece.dtype)] * count,
        compiler_params=PARAMS,
        cost_estimate=COST,
    )(piece, *after)


def put_kernel(place_ref, top2, top3, bottom, out_ref, two, three, sems):
    part, wide = top2.shape
    first = wide * PIECES[0] // (PIECES[0] + PIECES[2])
    end = out_ref.shape[2]
    after = end - wide + first
    copies = []
    for k, scratch, upper, lower in (
        (2, two, top2, bottom[:, wide:]),
        (3, three, top3, bottom[:, 0:wide]),
    ):
        keep = k < place_ref[2]
        scratch[0:part, :] = jnp.where(keep, upper[...], 0.0).astype(scratch.dtype)
        scratch[part:, :] = jnp.where(keep, lower, 0.0).astype(scratch.dtype)
        for n, (here, there) in enumerate(
            ((pl.ds(0, first), pl.ds(0, first)), (pl.ds(first, wide - first), pl.ds(after, end - after)))
        ):
            copy = pltpu.make_async_copy(
                scratch.at[:, here], out_ref.at[k, :, there], sems.at[k - 2, n]
            )
            copy.start()
            copies.append(copy)
    for copy in copies:
        copy.wait()


def put(place, buffer, top2, top3, bottom, passed):
    operands = [place, top2, top3, bottom, passed, buffer]
    shape = (buffer.shape[1], top2.shape[1])

    def kernel(*refs):
        n = len(operands)
        put_kernel(*refs[: n - 2], *refs[n + 1 :])

    return pl.pallas_call(
        kernel,
        in_specs=[SMEM] + [VMEM] * (len(operands) - 3) + [ANY] * 2,
        out_specs=[ANY] * 2,
        out_shape=[jax.ShapeDtypeStruct(x.shape, x.dtype) for x in (passed, buffer)],
        scratch_shapes=[
            pltpu.VMEM(shape, buffer.dtype),
            pltpu.VMEM(shape, buffer.dtype),
            pltpu.SemaphoreType.DMA((2, 2)),
        ],
        input_output_aliases={len(operands) - 2: 0, len(operands) - 1: 1},
        compiler_params=PARAMS,
        cost_estimate=COST,
    )(*operands)


def last_kernel(place_ref, side, buffer_ref, out_ref):
    out_ref[0] = jnp.where(3 < place_ref[2], side[...], 0.0).astype(out_ref.dtype)


def last(place, buffer, side, column):
    count, width = side.shape
    return pl.pallas_call(
        last_kernel,
        grid=(1,),
        in_specs=[SMEM, VMEM, ANY],
        out_specs=pl.BlockSpec((1, count, width), lambda i: (3, 0, column)),
        out_shape=jax.ShapeDtypeStruct(buffer.shape, buffer.dtype),
        input_output_aliases={2: 0},
        compiler_params=PARAMS,
        cost_estimate=COST,
    )(place, side, buffer)


def per_device(dosage, observed, counts):
    places = lax.axis_size("var")
    samples = dosage.shape[0] * lax.axis_size("samp")
    width = dosage.shape[1]
    place = jnp.stack(
        [
            (lax.axis_index("var") % 2).astype(jnp.int32),
            lax.axis_index("samp").astype(jnp.int32),
            counts[0],
        ]
    )

    def send(shard, pairs):
        return lax.ppermute(shard, "var", pairs)

    before = [(i + 1, i) for i in range(places - 1)]
    up = [(i, i + 2) for i in range(places - 2)]
    down = [(i + 2, i) for i in range(places - 2)]
    down_odd = [pair for pair in down if pair[0] % 2 == 1]
    to_even = [(i + 1, i) for i in range(0, places - 1, 2)]
    swap = to_even + [(i, i + 1) for i in range(0, places - 1, 2)]

    def mate(shard):
        return lax.ppermute(shard, "samp", [(0, 1), (1, 0)])

    sums, masked = stats(dosage, observed)
    made = score(place, masked, sums, mate(sums))
    direct, relayed, detoured, sent = made[:4]
    here, away = made[4:-PARTS], made[-PARTS:]
    unset = jax.ShapeDtypeStruct((WIN, width // 2, width), jnp.bfloat16)

    upper, buffer = stack(here[0], mate(away[0]), (), (unset,))
    below0 = send(upper, up)
    above = send(relayed, down)
    across = send(detoured, swap)
    (sent,) = hold((across,), sent)
    next_direct = send(sent, before)
    (lower,) = stack(here[1], mate(away[1]))
    below1 = send(lower, up)
    rows = [upper, lower]
    own = [direct, mate(direct), detoured, mate(detoured)]
    (across,) = hold((above,), across)
    around = send(across, down_odd)

    buffer = tile(place, buffer, 0, 0, rows, own[:2], samples)
    buffer = tile(place, buffer, 0, 3, rows, own[2:], samples)
    above, buffer, swapped = choose(place, relayed, above, (buffer,))
    next_relayed = send(swapped, swap)
    (buffer,) = hold((below0,), buffer)
    made, buffer = far(place, buffer, [below0], own, samples)
    top2 = send(made, down)
    across, buffer, next_detoured = choose(place, around, across, (buffer,))
    (next_direct,) = hold((made, next_detoured, swapped), next_direct)
    high = [next_direct, mate(next_direct)]
    high += [next_detoured, mate(next_detoured)]
    made, buffer = far(place, buffer, [below0], high, samples)
    top3 = send(made, down)
    buffer = tile(place, buffer, 1, 0, rows, high[:-2], samples)
    buffer = tile(place, buffer, 0, 1, rows, [relayed, mate(relayed)], samples)

    (buffer,) = hold((below1, top2), buffer)
    made, buffer = far(place, buffer, [below1], high + own, samples)
    bottom = send(made, down)
    low = []
    for piece in split(next_relayed, (made, top3), 3):
        low += [piece, mate(piece)]
    made, buffer = far(place, buffer, [below0, below1], low, samples)
    side = send(made, down)
    buffer = tile(place, buffer, 1, 3, rows, high[-2:], samples)
    buffer = tile(place, buffer, 1, 1, rows, low, samples)
    pieces = list(split(above, (), 3))
    pieces[2], buffer = put(place, buffer, top2, top3, bottom, pieces[2])
    home = [array for piece in pieces for array in (piece, mate(piece))]
    buffer = tile(place, buffer, 2, 1, rows, home, samples)
    buffer = last(place, buffer, side, 1)
    return buffer[None]


def solution(mesh):
    in_specs = (P("samp", ("region", "var")), P("samp", ("region", "var")), P(("region", "var")))
    out_specs = P(("region", "var"), None, "samp", None)
    return jax.shard_map(
        per_device, mesh=mesh, in_specs=in_specs, out_specs=out_specs, check_vma=False
    )
```
